32 devices in a mesh: fsdp: 16 (over z, y, x), seq: 2 (over core).
Axes of the slice: x: 2, y: 2, z: 4, core: 2. Of those that a mesh axis runs over, the one named last changes fastest.
Arguments:
- hidden_in: bfloat16 [16, 1024, 768], P('fsdp', 'seq'), may hold values from -6 to 6
- memory: bfloat16 [16, 1024, 768], P('fsdp', 'seq'), may hold values from -6 to 6
- target_ids: int32 [16, 1024], P('fsdp', 'seq'), may hold values from 0 to 4, never falling along the last dimension, each value on 1 to 512 neighbouring positions
- memory_ids: int32 [16, 1024], P('fsdp', 'seq'), may hold values from 0 to 4, never falling along the last dimension, each value on 1 to 512 neighbouring positions
- out_grad: bfloat16 [16, 1024, 768], P('fsdp', 'seq'), may hold values from -6 to 6
- self_query: bfloat16 [768, 768], P('fsdp'), may hold values from -0.21875 to 0.21875
- self_query_bias: bfloat16 [768], P('fsdp'), may hold values from -3 to 3
- self_key: bfloat16 [768, 768], P('fsdp'), may hold values from -0.21875 to 0.21875
- self_value: bfloat16 [768, 768], P('fsdp'), may hold values from -0.21875 to 0.21875
- self_value_bias: bfloat16 [768], P('fsdp'), may hold values from -3 to 3
- self_output: bfloat16 [768, 768], P('fsdp'), may hold values from -1.75 to 1.75
- self_output_bias: bfloat16 [768], P('fsdp'), may hold values from -3 to 3
- first_gain: bfloat16 [768], P('fsdp'), may hold values from 0.5 to 1.5
- first_shift: bfloat16 [768], P('fsdp'), may hold values from -3 to 3
- cross_query: bfloat16 [768, 768], P('fsdp'), may hold values from -0.21875 to 0.21875
- cross_query_bias: bfloat16 [768], P('fsdp'), may hold values from -3 to 3
- cross_key: bfloat16 [768, 768], P('fsdp'), may hold values from -0.21875 to 0.21875
- cross_value: bfloat16 [768, 768], P('fsdp'), may hold values from -0.21875 to 0.21875
- cross_value_bias: bfloat16 [768], P('fsdp'), may hold values from -3 to 3
- cross_output: bfloat16 [768, 768], P('fsdp'), may hold values from -1.75 to 1.75
- cross_output_bias: bfloat16 [768], P('fsdp'), may hold values from -3 to 3
- second_gain: bfloat16 [768], P('fsdp'), may hold values from 0.5 to 1.5
- second_shift: bfloat16 [768], P('fsdp'), may hold values from -3 to 3
- inner_weight: bfloat16 [768, 3072], P('fsdp'), may hold values from -0.21875 to 0.21875
- inner_bias: bfloat16 [3072], P('fsdp'), may hold values from -3 to 3
- outer_weight: bfloat16 [3072, 768], P('fsdp'), may hold values from -0.109375 to 0.109375
- outer_bias: bfloat16 [768], P('fsdp'), may hold values from -3 to 3
- third_gain: bfloat16 [768], P('fsdp'), may hold values from 0.5 to 1.5
- third_shift: bfloat16 [768], P('fsdp'), may hold values from -3 to 3
Outputs:
- layer_out: bfloat16 [16, 1024, 768], P('fsdp', 'seq')
- input_grad: bfloat16 [16, 1024, 768], P('fsdp', 'seq')
- memory_grad: bfloat16 [16, 1024, 768], P('fsdp', 'seq')
- self_query_grad: float32 [768, 768], P('fsdp')
- self_query_bias_grad: float32 [768], P('fsdp')
- self_key_grad: float32 [768, 768], P('fsdp')
- self_value_grad: float32 [768, 768], P('fsdp')
- self_value_bias_grad: float32 [768], P('fsdp')
- self_output_grad: float32 [768, 768], P('fsdp')
- self_output_bias_grad: float32 [768], P('fsdp')
- first_gain_grad: float32 [768], P('fsdp')
- first_shift_grad: float32 [768], P('fsdp')
- cross_query_grad: float32 [768, 768], P('fsdp')
- cross_query_bias_grad: float32 [768], P('fsdp')
- cross_key_grad: float32 [768, 768], P('fsdp')
- cross_value_grad: float32 [768, 768], P('fsdp')
- cross_value_bias_grad: float32 [768], P('fsdp')
- cross_output_grad: float32 [768, 768], P('fsdp')
- cross_output_bias_grad: float32 [768], P('fsdp')
- second_gain_grad: float32 [768], P('fsdp')
- second_shift_grad: float32 [768], P('fsdp')
- inner_weight_grad: float32 [768, 3072], P('fsdp')
- inner_bias_grad: float32 [3072], P('fsdp')
- outer_weight_grad: float32 [3072, 768], P('fsdp')
- outer_bias_grad: float32 [768], P('fsdp')
- third_gain_grad: float32 [768], P('fsdp')
- third_shift_grad: float32 [768], P('fsdp')
The draws below stay inside these ranges and needn't reach their ends.
Inputs may be any that keep to these rules, and one draw needn't show every extreme that they name: `target_ids`: in each row the ids never fall and every id from 0 to 4 occurs; 0 is padding at the row's start; no id holds more than 512 positions of a row, and one of each row holds exactly that many. `memory_ids`: in each row the ids never fall and every id from 0 to 4 occurs; no id holds more than 512 positions of a row, and one of each row holds exactly that many.
All inputs are finite; a program needn't handle non-finite values.
Results may differ from the reference program's by a relative error of at most 0.025.
Values may be sent and summed in bfloat16 or wider, within the bound.
A program may use at most 192 MiB of HBM per device.

```python
import math
import jax
import jax.numpy as jnp
import numpy as np
from jax import lax

D = 768
HEADS = 12
HEAD_DIM = 64
FF = 3072
SEQ_LEN = 1024
SEGS = 5
ROWS = 16


def levels(stream_key, dims, cuts, least, high):
    level = 1.0
    for position, blocks in cuts:
        heights = jax.random.uniform(jax.random.fold_in(jax.random.fold_in(stream_key, 6), position), (blocks,), jnp.float32, least / len(cuts), high / len(cuts))
        level = level * jnp.repeat(jnp.exp(heights), dims[position] // blocks).reshape((-1,) + (1,) * (len(dims) - 1 - position))
    return level


def split_up(number_of, total, reach, slope):
    weights = [(1 << 20) // math.isqrt(standing ** slope) + 1 for standing in range(2, number_of + 1)]
    rest, given = total - reach - (number_of - 1), [1] * (number_of - 1)
    while rest > 0:
        free = [i for i in range(number_of - 1) if given[i] < reach]
        mass, left = sum([weights[i] for i in free]), rest
        for i in free:
            addition = min(reach - given[i], max(1, left * weights[i] // mass), rest)
            given[i] = given[i] + addition
            rest = rest - addition
    return np.array([reach] + given)


def ragged_sizes(own_key, amount, total, bound, skew):
    if amount == 2:
        one = jax.random.randint(own_key, (), max(1, total - bound), min(bound, total - 1) + 1)
        return jnp.stack([one, total - one])
    lengths = jnp.asarray(split_up(amount, total, bound, skew), jnp.int32)
    couples = (amount - 1) // 2
    giver, receiver = lengths[1:1 + 2 * couples:2], lengths[2:2 + 2 * couples:2]
    room = jnp.minimum(giver - 1, bound - receiver)
    moved = jax.random.randint(jax.random.fold_in(own_key, 1), (couples,), 0, 1 << 20) % (room + 1)
    lengths = lengths.at[1:1 + 2 * couples:2].set(giver - moved).at[2:2 + 2 * couples:2].set(receiver + moved)
    return lengths[jax.random.permutation(jax.random.fold_in(own_key, 2), amount)]


def normal_values(key, dims, scale, reach, shards=(), dtype=jnp.bfloat16):
    values = scale * jax.random.normal(key, dims, jnp.float32)
    if shards:
        values = values * levels(key, dims, shards, -0.22, 0.18)
    return jnp.clip(values, -reach, reach).astype(dtype)


def setup_inputs(seed: int = 0) -> dict:
    key_of = jax.random.split(jax.random.key(seed), 30)
    return {
        "hidden_in": normal_values(key_of[0], (ROWS, SEQ_LEN, D), 1.0, 6.0, ((0, 16), (1, 2))),
        "memory": normal_values(key_of[1], (ROWS, SEQ_LEN, D), 1.0, 6.0, ((0, 16), (1, 2))),
        "target_ids": jax.vmap(lambda own: jnp.searchsorted(jnp.cumsum(ragged_sizes(own, SEGS, SEQ_LEN, SEQ_LEN // 2, 2)), jnp.arange(SEQ_LEN), side="right"))(jax.random.split(key_of[2], ROWS)).reshape((ROWS, SEQ_LEN)).astype(jnp.int32),
        "memory_ids": jax.vmap(lambda own: jnp.searchsorted(jnp.cumsum(ragged_sizes(own, SEGS, SEQ_LEN, SEQ_LEN // 2, 2)), jnp.arange(SEQ_LEN), side="right"))(jax.random.split(key_of[3], ROWS)).reshape((ROWS, SEQ_LEN)).astype(jnp.int32),
        "out_grad": normal_values(key_of[4], (ROWS, SEQ_LEN, D), 1.0, 6.0, ((0, 16), (1, 2))),
        "self_query": normal_values(key_of[5], (D, D), D ** -0.5, 0.21875, ((0, 16),)),
        "self_query_bias": normal_values(key_of[6], (D,), 0.5, 3.0, ((0, 16),)),
        "self_key": normal_values(key_of[7], (D, D), D ** -0.5, 0.21875, ((0, 16),)),
        "self_value": normal_values(key_of[8], (D, D), D ** -0.5, 0.21875, ((0, 16),)),
        "self_value_bias": normal_values(key_of[9], (D,), 0.5, 3.0, ((0, 16),)),
        "self_output": normal_values(key_of[10], (D, D), (D // 64) ** -0.5, 1.75, ((0, 16),)),
        "self_output_bias": normal_values(key_of[11], (D,), 0.5, 3.0, ((0, 16),)),
        "first_gain": jnp.clip(1.0 + 0.1 * jax.random.normal(key_of[12], (D,), jnp.float32), 0.5, 1.5).astype(jnp.bfloat16),
        "first_shift": normal_values(key_of[13], (D,), 0.5, 3.0, ((0, 16),)),
        "cross_query": normal_values(key_of[14], (D, D), D ** -0.5, 0.21875, ((0, 16),)),
        "cross_query_bias": normal_values(key_of[15], (D,), 0.5, 3.0, ((0, 16),)),
        "cross_key": normal_values(key_of[16], (D, D), D ** -0.5, 0.21875, ((0, 16),)),
        "cross_value": normal_values(key_of[17], (D, D), D ** -0.5, 0.21875, ((0, 16),)),
        "cross_value_bias": normal_values(key_of[18], (D,), 0.5, 3.0, ((0, 16),)),
        "cross_output": normal_values(key_of[19], (D, D), (D // 64) ** -0.5, 1.75, ((0, 16),)),
        "cross_output_bias": normal_values(key_of[20], (D,), 0.5, 3.0, ((0, 16),)),
        "second_gain": jnp.clip(1.0 + 0.1 * jax.random.normal(key_of[21], (D,), jnp.float32), 0.5, 1.5).astype(jnp.bfloat16),
        "second_shift": normal_values(key_of[22], (D,), 0.5, 3.0, ((0, 16),)),
        "inner_weight": normal_values(key_of[23], (D, FF), D ** -0.5, 0.21875, ((0, 16),)),
        "inner_bias": normal_values(key_of[24], (FF,), 0.5, 3.0, ((0, 16),)),
        "outer_weight": normal_values(key_of[25], (FF, D), FF ** -0.5, 0.109375, ((0, 16),)),
        "outer_bias": normal_values(key_of[26], (D,), 0.5, 3.0, ((0, 16),)),
        "third_gain": jnp.clip(1.0 + 0.1 * jax.random.normal(key_of[27], (D,), jnp.float32), 0.5, 1.5).astype(jnp.bfloat16),
        "third_shift": normal_values(key_of[28], (D,), 0.5, 3.0, ((0, 16),)),
    }


@jax.custom_vjp
def low(v):
    return lax.optimization_barrier(v.astype(jnp.bfloat16)).astype(jnp.float32)

@jax.custom_vjp
def low_back(v):
    return v

def low_keep(v):
    return (low(v), None)

def low_pass(kept, grad):
    return (grad,)

def back_keep(v):
    return (v, None)

def back_low(kept, grad):
    return (low(grad),)
low.defvjp(low_keep, low_pass)
low_back.defvjp(back_keep, back_low)
eps_norm = 1e-05
masked_score = -1e+30

def product(left, right):
    return jnp.dot(left, right, precision=lax.Precision.HIGHEST)

def layer_norm(resid, gain, shift):
    center = resid - lax.optimization_barrier(jnp.mean(resid, axis=-1, keepdims=True))
    spread = lax.optimization_barrier(jnp.mean(center * center, axis=-1, keepdims=True))
    return center * lax.rsqrt(spread + eps_norm) * gain + shift

def attend(query, keys, values, allowed):
    rows, length, width = query.shape
    query = query.reshape(rows, length, HEADS, HEAD_DIM)
    keys = keys.reshape(rows, keys.shape[1], HEADS, HEAD_DIM)
    values = values.reshape(rows, values.shape[1], HEADS, HEAD_DIM)
    scores = jnp.einsum('gqhe,gkhe->ghqk', query, keys, precision=lax.Precision.HIGHEST)
    scores = low_back(jnp.where(allowed[:, None], scores, masked_score))
    probs = low(jax.nn.softmax(scores, axis=-1))
    mixed = jnp.einsum('ghqk,gkhe->gqhe', probs, values, precision=lax.Precision.HIGHEST)
    return mixed.reshape(rows, length, width)

def forward(params, hidden, source, target_rows, source_rows):
    self_query, self_query_bias, self_key, self_value, self_value_bias, self_output, self_output_bias, first_gain, first_shift, cross_query, cross_query_bias, cross_key, cross_value, cross_value_bias, cross_output, cross_output_bias, second_gain, second_shift, inner_weight, inner_bias, outer_weight, outer_bias, third_gain, third_shift = params
    scale = HEAD_DIM ** (-0.5)
    places = jnp.arange(SEQ_LEN)
    allowed_self = (target_rows[:, :, None] == target_rows[:, None, :]) & (places[None, :, None] >= places[None, None, :])
    allowed_cross = target_rows[:, :, None] == source_rows[:, None, :]
    query_one = low(low_back((product(hidden, self_query) + self_query_bias) * scale))
    key_one = low(low_back(product(hidden, self_key)))
    value_one = low(low_back(product(hidden, self_value) + self_value_bias))
    mixed_one = low(low_back(attend(query_one, key_one, value_one, allowed_self)))
    branch_one = low_back(product(mixed_one, self_output) + self_output_bias)
    first = low(layer_norm(hidden + branch_one, first_gain, first_shift))
    query_two = low(low_back((product(first, cross_query) + cross_query_bias) * scale))
    key_two = low(low_back(product(source, cross_key)))
    value_two = low(low_back(product(source, cross_value) + cross_value_bias))
    mixed_two = low(low_back(attend(query_two, key_two, value_two, allowed_cross)))
    branch_two = low_back(product(mixed_two, cross_output) + cross_output_bias)
    second = low(layer_norm(first + branch_two, second_gain, second_shift))
    inner = low_back(product(second, inner_weight) + inner_bias)
    active = low(jax.nn.gelu(inner, approximate=False))
    branch_three = low_back(product(active, outer_weight) + outer_bias)
    return layer_norm(second + branch_three, third_gain, third_shift)

def reference(hidden_in, memory, target_ids, memory_ids, out_grad, self_query, self_query_bias, self_key, self_value, self_value_bias, self_output, self_output_bias, first_gain, first_shift, cross_query, cross_query_bias, cross_key, cross_value, cross_value_bias, cross_output, cross_output_bias, second_gain, second_shift, inner_weight, inner_bias, outer_weight, outer_bias, third_gain, third_shift):
    params = tuple((weight.astype(jnp.float32) for weight in (self_query, self_query_bias, self_key, self_value, self_value_bias, self_output, self_output_bias, first_gain, first_shift, cross_query, cross_query_bias, cross_key, cross_value, cross_value_bias, cross_output, cross_output_bias, second_gain, second_shift, inner_weight, inner_bias, outer_weight, outer_bias, third_gain, third_shift)))
    group = math.gcd(ROWS, max(1, 4096 // SEQ_LEN))
    count = ROWS // group

    def split(array):
        return array.reshape((count, group) + array.shape[1:])

    def one_group(totals, pieces):
        hidden, source, target_rows, source_rows, cotangent = pieces

        def closed(weights, hidden_rows, source_states):
            return forward(weights, hidden_rows, source_states, target_rows, source_rows)
        result, pull = jax.vjp(closed, params, hidden.astype(jnp.float32), source.astype(jnp.float32))
        keep = (target_rows > 0).astype(jnp.float32)[:, :, None]
        grads, hidden_grad, source_grad = pull(cotangent.astype(jnp.float32) * keep)
        totals = jax.tree.map(jnp.add, totals, grads)
        return (totals, (result.astype(jnp.bfloat16), hidden_grad.astype(jnp.bfloat16), source_grad.astype(jnp.bfloat16)))
    zeros = tuple((jnp.zeros(weight.shape, jnp.float32) for weight in params))
    totals, stacked = lax.scan(one_group, zeros, (split(hidden_in), split(memory), split(target_ids), split(memory_ids), split(out_grad)))
    layer_out = stacked[0].reshape(ROWS, SEQ_LEN, D)
    input_grad = stacked[1].reshape(ROWS, SEQ_LEN, D)
    memory_grad = stacked[2].reshape(ROWS, SEQ_LEN, D)
    return (layer_out, input_grad, memory_grad, totals[0], totals[1], totals[2], totals[3], totals[4], totals[5], totals[6], totals[7], totals[8], totals[9], totals[10], totals[11], totals[12], totals[13], totals[14], totals[15], totals[16], totals[17], totals[18], totals[19], totals[20], totals[21], totals[22], totals[23])
```

```python
import functools
import math
from types import SimpleNamespace
from typing import NamedTuple

import jax
import jax.numpy as jnp
from jax import lax
from jax.experimental import pallas as pl
from jax.experimental.pallas import tpu as pltpu
from jax.sharding import PartitionSpec as P

HEAD_DIM = 64
PAIR = 2 * HEAD_DIM
SEGMENTS = 5
TILE = 256
eps_norm = 1e-05
masked_score = -1e30


class Weights(NamedTuple):
    self_query: jax.Array
    self_query_bias: jax.Array
    self_key: jax.Array
    self_value: jax.Array
    self_value_bias: jax.Array
    self_output: jax.Array
    self_output_bias: jax.Array
    first_gain: jax.Array
    first_shift: jax.Array
    cross_query: jax.Array
    cross_query_bias: jax.Array
    cross_key: jax.Array
    cross_value: jax.Array
    cross_value_bias: jax.Array
    cross_output: jax.Array
    cross_output_bias: jax.Array
    second_gain: jax.Array
    second_shift: jax.Array
    inner_weight: jax.Array
    inner_bias: jax.Array
    outer_weight: jax.Array
    outer_bias: jax.Array
    third_gain: jax.Array
    third_shift: jax.Array


def split_vectors(w):
    return [array for array in w if array.ndim == 1]


def dense(left, right):
    return jnp.dot(left, right, preferred_element_type=jnp.float32)


def dense_back(left, right):
    return lax.dot_general(
        left, right, (((1,), (1,)), ((), ())), preferred_element_type=jnp.float32
    )


def dense_grad(left, right):
    return lax.dot_general(
        left, right, (((0,), (0,)), ((), ())), preferred_element_type=jnp.float32
    )


def column_sum(values):
    return jnp.sum(values, axis=0, dtype=jnp.float32)


def layer_norm(resid, gain, shift):
    center = resid - jnp.mean(resid, axis=-1, keepdims=True)
    spread = jnp.mean(center * center, axis=-1, keepdims=True)
    inverse = lax.rsqrt(spread + eps_norm)
    normed = center * inverse
    return (normed * gain + shift, normed, inverse)


def norm_back(upstream, normed, inverse, gain):
    scaled = upstream * gain
    plain_mean = jnp.mean(scaled, axis=-1, keepdims=True)
    cross_mean = jnp.mean(scaled * normed, axis=-1, keepdims=True)
    result = inverse * (scaled - plain_mean - normed * cross_mean)
    return (result, jnp.sum(upstream * normed, axis=0), jnp.sum(upstream, axis=0))


class Staged:
    staged = True

    def __init__(self):
        self.f = lax.axis_index("fsdp")
        self.c = lax.axis_index("seq")
        self.z, self.y, self.x = self.f // 4, (self.f // 2) % 2, self.f % 2

    def _send(self, array, move):
        pairs = []
        for f in range(16):
            for c in range(2):
                g, d = move(f, c)
                pairs.append((f * 2 + c, g * 2 + d))
        return lax.ppermute(array, ("fsdp", "seq"), pairs)

    def along_z(self, array, k):
        return self._send(array, lambda f, c: ((f + 4 * k) % 16, c))

    def along_x(self, array):
        return self._send(array, lambda f, c: (f ^ 1, c))

    def along_y(self, array):
        return self._send(array, lambda f, c: (f ^ 2, c))

    def along_own(self, array):
        return self._send(array, lambda f, c: (f ^ (1 if c == 0 else 2), c))

    def along_other(self, array):
        return self._send(array, lambda f, c: (f ^ (2 if c == 0 else 1), c))

    def swap(self, array):
        return self._send(array, lambda f, c: (f, 1 - c))


    def _pieces(self, half):
        column = jnp.stack([half] + [self.along_z(half, k) for k in (1, 2, 3)])
        by_x, by_y = self.along_x(column), self.along_y(column)
        by_both = self.along_other(jnp.where(self.c == 0, by_x, by_y))
        return [column, by_x, by_y, by_both]

    def _half(self, array, part):
        width = array.shape[1] // 2
        return lax.dynamic_slice_in_dim(array, part * width, width, 1)

    def gather(self, shards, vectors=None):
        parts = [self._half(s, self.c) for s in shards]
        rows = [p.shape[0] for p in parts]
        width = parts[0].shape[1]
        if vectors is not None:
            flat = jnp.concatenate(vectors)
            parts.append(jnp.pad(flat, (0, 16 * width - flat.shape[0])).reshape(16, width))
        packed = jnp.concatenate(parts) if len(parts) > 1 else parts[0]
        mine = self._pieces(packed)
        theirs = [self.swap(p) for p in mine]
        place = jnp.stack([self.z, self.y * 2 + self.x, self.c]).astype(jnp.int32)
        shapes = [jax.ShapeDtypeStruct((16 * r, 2 * width), packed.dtype) for r in rows]
        out_specs = [
            pl.BlockSpec((4 * r, 2 * width), lambda k, p: (lax.rem(p[0] - k + 4, 4), 0))
            for r in rows
        ]
        if vectors is not None:
            shapes.append(jax.ShapeDtypeStruct((16, 16, width), packed.dtype))
            out_specs.append(
                pl.BlockSpec((4, 16, width), lambda k, p: (lax.rem(p[0] - k + 4, 4), 0, 0))
            )

        def assemble(place_ref, *refs):
            pieces, outs = refs[:8], refs[8:]
            for core in range(2):

                @pl.when(place_ref[2] == core)
                def _():
                    for r in range(4):
                        source = place_ref[1] ^ r
                        for h in range(2):
                            offset = 0
                            columns = slice((core ^ h) * width, (core ^ h) * width + width)
                            for count, out in zip(rows, outs):
                                start = pl.multiple_of(source * count, 16)
                                out[pl.ds(start, count), columns] = pieces[h * 4 + r][
                                    0, offset : offset + count, :
                                ]
                                offset += count
                        if vectors is not None:
                            outs[-1][source] = pieces[r][0, offset : offset + 16, :]

        total = packed.shape[0]
        results = pl.pallas_call(
            assemble,
            out_shape=shapes,
            grid_spec=pltpu.PrefetchScalarGridSpec(
                num_scalar_prefetch=1,
                grid=(4,),
                in_specs=[pl.BlockSpec((1, total, width), lambda k, p: (k, 0, 0))] * 8,
                out_specs=out_specs,
            ),
            compiler_params=pltpu.CompilerParams(vmem_limit_bytes=48 * 2**20),
        )(place, *mine, *theirs)
        if vectors is None:
            return results
        table = results[-1].reshape(16, 16 * width)
        wholes, offset = [], 0
        for v in vectors:
            size = v.shape[0]
            wholes.append(table[:, offset : offset + size].reshape(-1).astype(jnp.float32))
            offset += size
        return results[:-1], wholes


    def _reduce(self, total):
        rows = total.shape[0] // 16
        blocks = total.reshape(4, 2, 2, rows, total.shape[1])
        kind = total.dtype

        def block(y, x):
            return lax.dynamic_slice(
                blocks, (0, y, x, 0, 0), (4, 1, 1, rows, total.shape[1])
            ).reshape(4, rows, total.shape[1])

        y, x = self.y, self.x
        passed = self.along_own(block(1 - y, 1 - x)).astype(jnp.float32)
        first = self.c == 0
        for_x = block(y, 1 - x).astype(jnp.float32) + jnp.where(first, 0.0, passed)
        for_y = block(1 - y, x).astype(jnp.float32) + jnp.where(first, passed, 0.0)
        own = (
            block(y, x).astype(jnp.float32)
            + self.along_x(for_x.astype(kind)).astype(jnp.float32)
            + self.along_y(for_y.astype(kind)).astype(jnp.float32)
        ).astype(kind)

        def at(z):
            return lax.dynamic_index_in_dim(own, z % 4, 0, keepdims=False)

        result = at(self.z).astype(jnp.float32)
        for k in (1, 2, 3):
            result = result + self.along_z(at(self.z + k), k).astype(jnp.float32)
        return result

    def reduce_product(self, left, rights):
        other = jnp.concatenate([self._half(r, 1 - self.c) for r in rights], axis=1)
        own = jnp.concatenate([self._half(r, self.c) for r in rights], axis=1)
        there = self.swap(dense_grad(left, other).astype(jnp.bfloat16))
        total = (dense_grad(left, own) + there.astype(jnp.float32)).astype(jnp.bfloat16)
        mine = self._reduce(total).astype(jnp.bfloat16)
        theirs = self.swap(mine)
        first = self.c == 0
        low = jnp.where(first, mine, theirs).astype(jnp.float32)
        high = jnp.where(first, theirs, mine).astype(jnp.float32)
        results, offset = [], 0
        for r in rights:
            width = r.shape[1] // 2
            results.append(
                jnp.concatenate(
                    [low[:, offset : offset + width], high[:, offset : offset + width]], axis=1
                )
            )
            offset += width
        return results

    def reduce_vectors(self, vectors):
        sizes = [v.shape[0] // 16 for v in vectors]
        table = jnp.concatenate([v.reshape(16, -1) for v in vectors], axis=1)
        used = table.shape[1]
        table = jnp.pad(table, ((0, 0), (0, 1024 - used))).reshape(16 * 8, 128)
        table = table + self.swap(table)
        summed = self._reduce(table).reshape(1024)
        results, offset = [], 0
        for size in sizes:
            results.append(summed[offset : offset + size])
            offset += size
        return results


    def gather_row(self, array):
        return jnp.concatenate([array, self.swap(array)], axis=1)

    def places(self, length):
        steps = jnp.arange(length)
        return jnp.concatenate([self.c * length + steps, (1 - self.c) * length + steps])

    def scatter_row(self, array):
        length = array.shape[1] // 2
        there = self.swap(array[:, length:].astype(jnp.bfloat16))
        return array[:, :length] + there.astype(jnp.float32)


class Plain:
    staged = False

    def gather(self, shards, vectors=None):
        results = [lax.all_gather(s, "fsdp", axis=0, tiled=True) for s in shards]
        if vectors is None:
            return results
        return results, [
            lax.all_gather(v, "fsdp", axis=0, tiled=True).astype(jnp.float32) for v in vectors
        ]

    def _reduce(self, total):
        part = lax.psum_scatter(
            total.astype(jnp.bfloat16), "fsdp", scatter_dimension=0, tiled=True
        )
        return lax.psum(part, "seq").astype(jnp.float32)

    def reduce_product(self, left, rights):
        return [self._reduce(dense_grad(left, r)) for r in rights]

    def reduce_vectors(self, vectors):
        return [self._reduce(v) for v in vectors]

    def gather_row(self, array):
        return lax.all_gather(array, "seq", axis=1, tiled=True)

    def places(self, length):
        return jnp.arange(length * lax.axis_size("seq"))

    def scatter_row(self, array):
        return lax.psum_scatter(
            array.astype(jnp.bfloat16), "seq", scatter_dimension=1, tiled=True
        ).astype(jnp.float32)


def query_marks(ids):
    lanes = jnp.arange(PAIR)[None, :] % HEAD_DIM
    return jnp.where((lanes < SEGMENTS) & (ids[:, None] != lanes), masked_score, 0.0).astype(
        jnp.bfloat16
    )


def key_marks_of(ids):
    lanes = jnp.arange(PAIR)[None, :] % HEAD_DIM
    ones = (lanes >= SEGMENTS) & (lanes < SEGMENTS + 3)
    return (ones | (ids[:, None] == lanes)).astype(jnp.bfloat16)


def against(left, right):
    return lax.dot_general(
        left, right, (((1,), (1,)), ((), ())), preferred_element_type=jnp.float32
    )


def three(value):
    high = value.astype(jnp.bfloat16).astype(jnp.float32)
    rest = value - high
    middle = rest.astype(jnp.bfloat16).astype(jnp.float32)
    return high, middle, rest - middle


def place_three(lanes, base, value, other):
    high, middle, small = three(value)
    first = base + SEGMENTS
    return jnp.where(
        lanes == first,
        high,
        jnp.where(lanes == first + 1, middle, jnp.where(lanes == first + 2, small, other)),
    )


def plan(length, causal, later):
    half = length // 2
    result = []
    for tile in range(2):
        if not causal:
            result.append([(0, 2 * length, False)])
            continue
        ranges = [(0, half, False)] if tile else []
        ranges.append((tile * half, half, True))
        if later:
            ranges.append((length + tile * half, length - tile * half, False))
        result.append(ranges)
    return result


def each_plan(core, length, causal, run):
    if not causal:
        run(plan(length, False, False))
        return
    for later in range(2):
        @pl.when(core == later)
        def _():
            run(plan(length, True, bool(later)))


def forward_kernel(causal, core_ref, q_ref, k_ref, v_ref, qm_ref, km_ref, mixed_ref, qx_ref):
    length = q_ref.shape[0]

    def run(tiles):
        for head in range(2):
            base = HEAD_DIM * (1 - head)

            def own(lanes):
                return (lanes < HEAD_DIM) if head == 0 else (lanes >= HEAD_DIM)

            for tile, ranges in enumerate(tiles):
                rows = slice(tile * TILE, tile * TILE + TILE)
                lanes = lax.broadcasted_iota(jnp.int32, (TILE, PAIR), 1)
                q = jnp.where(own(lanes), q_ref[rows, :], qm_ref[rows, :])
                scores = []
                for start, size, diagonal in ranges:
                    keys = slice(start, start + size)
                    key_lanes = lax.broadcasted_iota(jnp.int32, (size, PAIR), 1)
                    k = jnp.where(own(key_lanes), k_ref[keys, :], km_ref[keys, :])
                    s = against(q, k)
                    if diagonal:
                        i = lax.broadcasted_iota(jnp.int32, s.shape, 0)
                        j = lax.broadcasted_iota(jnp.int32, s.shape, 1)
                        s = jnp.where(j <= i, s, masked_score)
                    scores.append(s)
                highest = functools.reduce(
                    jnp.maximum, [jnp.max(s, axis=1, keepdims=True) for s in scores]
                )
                out = jnp.zeros((TILE, PAIR), jnp.float32)
                for s, (start, size, _) in zip(scores, ranges):
                    keys = slice(start, start + size)
                    key_lanes = lax.broadcasted_iota(jnp.int32, (size, PAIR), 1)
                    v = jnp.where(own(key_lanes), v_ref[keys, :], jnp.ones((), jnp.bfloat16))
                    e = jnp.exp(s - highest).astype(jnp.bfloat16)
                    out = out + jnp.dot(e, v, preferred_element_type=jnp.float32)
                total = pltpu.roll(out, HEAD_DIM, 1)
                mixed = (out / total).astype(jnp.bfloat16)
                if head:
                    mixed = jnp.where(own(lanes), mixed, mixed_ref[rows, :])
                mixed_ref[rows, :] = mixed
                logsum = highest + jnp.log(out)
                qx = place_three(lanes, base, -logsum, q.astype(jnp.float32))
                qx_ref[head, rows, :] = qx.astype(jnp.bfloat16)

    each_plan(core_ref[0], length, causal, run)


def attend(core, query, keys, values, q_marks, k_marks, causal):
    length, width = query.shape
    extent = keys.shape[0]
    pairs = width // PAIR
    column = lambda rows: pl.BlockSpec((rows, PAIR), lambda i, p: (0, i))
    fixed = lambda rows: pl.BlockSpec((rows, PAIR), lambda i, p: (0, 0))
    return pl.pallas_call(
        functools.partial(forward_kernel, causal),
        out_shape=[
            jax.ShapeDtypeStruct((length, width), jnp.bfloat16),
            jax.ShapeDtypeStruct((2 * pairs, length, PAIR), jnp.bfloat16),
        ],
        grid_spec=pltpu.PrefetchScalarGridSpec(
            num_scalar_prefetch=1,
            grid=(pairs,),
            in_specs=[column(length), column(extent), column(extent), fixed(length), fixed(extent)],
            out_specs=[column(length), pl.BlockSpec((2, length, PAIR), lambda i, p: (i, 0, 0))],
        ),
        compiler_params=pltpu.CompilerParams(vmem_limit_bytes=48 * 2**20),
        cost_estimate=pl.CostEstimate(
            flops=16 * length * extent * width, bytes_accessed=8 * extent * width, transcendentals=0
        ),
    )(core, query, keys, values, q_marks, k_marks)


def backward_kernel(
    causal, core_ref, qx_ref, k_ref, v_ref, e_ref, o_ref, km_ref, dq_ref, dk_ref, dv_ref, dk_acc, dv_acc, dq_acc
):
    length = e_ref.shape[0]
    scale = HEAD_DIM ** (-0.5)

    def run(tiles):
        dk_acc[...] = jnp.zeros_like(dk_acc)
        dv_acc[...] = jnp.zeros_like(dv_acc)
        for head in range(2):
            base = HEAD_DIM * (1 - head)

            def own(lanes):
                return (lanes < HEAD_DIM) if head == 0 else (lanes >= HEAD_DIM)

            for tile, ranges in enumerate(tiles):
                rows = slice(tile * TILE, tile * TILE + TILE)
                lanes = lax.broadcasted_iota(jnp.int32, (TILE, PAIR), 1)
                nothing = jnp.zeros((), jnp.bfloat16)
                qx = qx_ref[head, rows, :]
                q = jnp.where(own(lanes), qx, nothing)
                e = jnp.where(own(lanes), e_ref[rows, :], nothing)
                wide = e.astype(jnp.float32)
                delta = jnp.sum(wide * o_ref[rows, :].astype(jnp.float32), axis=1, keepdims=True)
                ex = place_three(lanes, base, -delta, wide).astype(jnp.bfloat16)
                dq = jnp.zeros((HEAD_DIM, TILE), jnp.float32)
                for start, size, diagonal in ranges:
                    keys = slice(start, start + size)
                    key_lanes = lax.broadcasted_iota(jnp.int32, (size, PAIR), 1)
                    k = jnp.where(own(key_lanes), k_ref[keys, :], km_ref[keys, :])
                    v = jnp.where(own(key_lanes), v_ref[keys, :], km_ref[keys, :])
                    p = jnp.exp(against(k, qx))
                    if diagonal:
                        j = lax.broadcasted_iota(jnp.int32, p.shape, 0)
                        i = lax.broadcasted_iota(jnp.int32, p.shape, 1)
                        p = jnp.where(j <= i, p, 0.0)
                    ds = (p * against(v, ex)).astype(jnp.bfloat16)
                    p = p.astype(jnp.bfloat16)
                    dv_acc[keys, :] += jnp.dot(p, e, preferred_element_type=jnp.float32)
                    dk_acc[keys, :] += jnp.dot(ds, q, preferred_element_type=jnp.float32)
                    kt = k_ref[keys, :].T[head * HEAD_DIM : (head + 1) * HEAD_DIM, :]
                    dq = dq + jnp.dot(kt, ds, preferred_element_type=jnp.float32)
                dq_acc[head * HEAD_DIM : (head + 1) * HEAD_DIM, rows] = dq
        dq_ref[...] = (dq_acc[...].T.astype(jnp.bfloat16) * jnp.bfloat16(scale)).astype(jnp.bfloat16)
        dk_ref[...] = dk_acc[...].astype(jnp.bfloat16)
        dv_ref[...] = dv_acc[...].astype(jnp.bfloat16)

    each_plan(core_ref[0], length, causal, run)


def attend_back(core, qx, keys, values, grad, mixed, k_marks, causal):
    length, width = grad.shape
    extent = keys.shape[0]
    pairs = width // PAIR
    column = lambda rows: pl.BlockSpec((rows, PAIR), lambda i, p: (0, i))
    fixed = lambda rows: pl.BlockSpec((rows, PAIR), lambda i, p: (0, 0))
    return pl.pallas_call(
        functools.partial(backward_kernel, causal),
        out_shape=[
            jax.ShapeDtypeStruct((length, width), jnp.bfloat16),
            jax.ShapeDtypeStruct((extent, width), jnp.bfloat16),
            jax.ShapeDtypeStruct((extent, width), jnp.bfloat16),
        ],
        grid_spec=pltpu.PrefetchScalarGridSpec(
            num_scalar_prefetch=1,
            grid=(pairs,),
            in_specs=[
                pl.BlockSpec((2, length, PAIR), lambda i, p: (i, 0, 0)),
                column(extent), column(extent), column(length), column(length), fixed(extent),
            ],
            out_specs=[column(length), column(extent), column(extent)],
            scratch_shapes=[
                pltpu.VMEM((extent, PAIR), jnp.float32),
                pltpu.VMEM((extent, PAIR), jnp.float32),
                pltpu.VMEM((PAIR, length), jnp.float32),
            ],
        ),
        compiler_params=pltpu.CompilerParams(vmem_limit_bytes=48 * 2**20),
        cost_estimate=pl.CostEstimate(
            flops=40 * length * extent * width, bytes_accessed=16 * extent * width, transcendentals=0
        ),
    )(core, qx, keys, values, grad, mixed, k_marks)


def head_slice(array, start, span):
    piece = lax.dynamic_slice_in_dim(array, start, span, 2)
    return piece.reshape(array.shape[0], array.shape[1], 2, span // 2)


def plain_attend(query, keys, values, allowed):
    rows, length, width = query.shape
    span = 2 * HEAD_DIM
    pairs = width // span

    def one_pair(index, carry):
        mixed, logsum = carry
        start = index * span
        query_part = head_slice(query, start, span)
        key_part = head_slice(keys, start, span)
        value_part = head_slice(values, start, span)
        scores = jnp.einsum(
            "rqhe,rkhe->rhqk", query_part, key_part, preferred_element_type=jnp.float32
        )
        scores = jnp.where(allowed[:, None], scores, masked_score)
        highest = jnp.max(scores, axis=-1, keepdims=True)
        exponent = jnp.exp(scores - highest)
        total = jnp.sum(exponent, axis=-1, keepdims=True)
        probs = (exponent / total).astype(jnp.bfloat16)
        part = jnp.einsum("rhqk,rkhe->rqhe", probs, value_part, preferred_element_type=jnp.float32)
        mixed = lax.dynamic_update_slice_in_dim(mixed, part.reshape(rows, length, span), start, 2)
        logsum = lax.dynamic_update_slice_in_dim(
            logsum, (highest + jnp.log(total))[None, :, :, :, 0], index, 0
        )
        return (mixed, logsum)

    mixed = jnp.zeros((rows, length, width), jnp.float32)
    logsum = jnp.zeros((pairs, rows, 2, length), jnp.float32)
    return lax.fori_loop(0, pairs, one_pair, (mixed, logsum))


def plain_attend_back(query, keys, values, allowed, logsum, grad_mixed):
    rows, length, width = query.shape
    extent = keys.shape[1]
    span = 2 * HEAD_DIM
    pairs = width // span

    def one_pair(index, carry):
        start = index * span
        query_part = head_slice(query, start, span)
        key_part = head_slice(keys, start, span)
        value_part = head_slice(values, start, span)
        grad_part = head_slice(grad_mixed, start, span)
        scores = jnp.einsum(
            "rqhe,rkhe->rhqk", query_part, key_part, preferred_element_type=jnp.float32
        )
        scores = jnp.where(allowed[:, None], scores, masked_score)
        pair_logsum = lax.dynamic_index_in_dim(logsum, index, 0, keepdims=False)
        probs = jnp.exp(scores - pair_logsum[..., None])
        prob_grad = jnp.einsum(
            "rqhe,rkhe->rhqk", grad_part, value_part, preferred_element_type=jnp.float32
        )
        row_total = jnp.sum(probs * prob_grad, axis=-1, keepdims=True)
        score_grad = (probs * (prob_grad - row_total)).astype(jnp.bfloat16)
        query_grad = jnp.einsum(
            "rhqk,rkhe->rqhe", score_grad, key_part, preferred_element_type=jnp.float32
        )
        grad_query = lax.dynamic_update_slice_in_dim(
            carry[0], query_grad.reshape(rows, length, span), start, 2
        )
        probs_low = probs.astype(jnp.bfloat16)
        value_grad = jnp.einsum(
            "rhqk,rqhe->rkhe", probs_low, grad_part, preferred_element_type=jnp.float32
        )
        key_grad = jnp.einsum(
            "rhqk,rqhe->rkhe", score_grad, query_part, preferred_element_type=jnp.float32
        )
        grad_keys = lax.dynamic_update_slice_in_dim(
            carry[1], key_grad.reshape(rows, extent, span), start, 2
        )
        grad_values = lax.dynamic_update_slice_in_dim(
            carry[2], value_grad.reshape(rows, extent, span), start, 2
        )
        return (grad_query, grad_keys, grad_values)

    start_query = jnp.zeros((rows, length, width), jnp.float32)
    start_keys = jnp.zeros((rows, extent, width), jnp.float32)
    return lax.fori_loop(0, pairs, one_pair, (start_query, start_keys, start_keys))


def attention(net, query, keys, values, target_ids, key_ids, causal):
    rows, length, width = query.shape
    if net.staged and rows == 1 and length == 2 * TILE:
        core = net.c.reshape(1)
        k_marks = key_marks_of(key_ids[0])
        q_marks = query_marks(target_ids[0])
        mixed, qx = attend(core, query[0], keys[0], values[0], q_marks, k_marks, causal)

        def back(grad):
            results = attend_back(core, qx, keys[0], values[0], grad, mixed, k_marks, causal)
            return [array[None] for array in results]

        return mixed, back
    allowed = target_ids[:, :, None] == key_ids[:, None, :]
    if causal:
        query_places = lax.axis_index("seq") * length + jnp.arange(length)
        allowed &= net.places(length)[None, None, :] <= query_places[None, :, None]
    mixed, logsum = plain_attend(query, keys, values, allowed)

    def plain_back(grad):
        query_sum, key_sum, value_sum = plain_attend_back(
            query, keys, values, allowed, logsum, grad.reshape(rows, length, width)
        )
        return [query_sum.astype(jnp.bfloat16) * HEAD_DIM ** (-0.5), key_sum, value_sum]

    return mixed.astype(jnp.bfloat16).reshape(rows * length, width), plain_back


def body(staged, hidden_in, memory, target_ids, memory_ids, out_grad, *weights):
    w = Weights(*weights)
    net = Staged() if staged else Plain()
    all_ = SimpleNamespace()
    (all_.self_query, all_.self_key, all_.self_value), vectors = net.gather(
        [w.self_query, w.self_key, w.self_value], split_vectors(w)
    )
    (
        self_query_bias, self_value_bias, self_output_bias, first_gain, first_shift,
        cross_query_bias, cross_value_bias, cross_output_bias, second_gain, second_shift,
        inner_bias, outer_bias, third_gain, third_shift,
    ) = vectors
    all_.cross_key, all_.cross_value, all_.self_output = net.gather(
        [w.cross_key, w.cross_value, w.self_output]
    )
    all_.cross_query, all_.cross_output = net.gather([w.cross_query, w.cross_output])
    (all_.inner_weight,) = net.gather([w.inner_weight])
    (all_.outer_weight,) = net.gather([w.outer_weight])

    rows, length, width = hidden_in.shape
    tokens = rows * length
    scale = HEAD_DIM ** (-0.5)
    flat_in = hidden_in.reshape(tokens, width)
    flat_memory = memory.reshape(tokens, width)

    def flat(array):
        return array.astype(jnp.bfloat16).reshape(tokens, width)

    def low(array):
        return array.astype(jnp.bfloat16).reshape(rows, length, width)

    row_ids, source_ids = net.gather_row(target_ids), net.gather_row(memory_ids)
    key_one = low(dense(flat_in, all_.self_key))
    value_one = low(dense(flat_in, all_.self_value) + self_value_bias)
    query_one = low((dense(flat_in, all_.self_query) + self_query_bias) * scale)
    keys_one, values_one = net.gather_row(key_one), net.gather_row(value_one)
    mixed_one, back_one = attention(
        net, query_one, keys_one, values_one, target_ids, row_ids, True
    )

    key_two = low(dense(flat_memory, all_.cross_key))
    value_two = low(dense(flat_memory, all_.cross_value) + cross_value_bias)
    keys_two, values_two = net.gather_row(key_two), net.gather_row(value_two)

    resid_one = (
        flat_in.astype(jnp.float32) + dense(mixed_one, all_.self_output) + self_output_bias
    )
    first, normed_one, inverse_one = layer_norm(resid_one, first_gain, first_shift)
    first = first.astype(jnp.bfloat16)
    query_two = low((dense(first, all_.cross_query) + cross_query_bias) * scale)
    mixed_two, back_two = attention(
        net, query_two, keys_two, values_two, target_ids, source_ids, False
    )
    resid_two = (
        first.astype(jnp.float32) + dense(mixed_two, all_.cross_output) + cross_output_bias
    )
    second, normed_two, inverse_two = layer_norm(resid_two, second_gain, second_shift)
    second = second.astype(jnp.bfloat16)
    inner = dense(second, all_.inner_weight) + inner_bias
    cumulative = 0.5 * (1.0 + lax.erf(inner * math.sqrt(0.5)))
    active = (inner * cumulative).astype(jnp.bfloat16)
    density = jnp.exp(-0.5 * inner * inner) * (1.0 / math.sqrt(2.0 * math.pi))
    slope = cumulative + inner * density
    resid_three = second.astype(jnp.float32) + dense(active, all_.outer_weight) + outer_bias
    final, normed_three, inverse_three = layer_norm(resid_three, third_gain, third_shift)
    layer_out = final.astype(jnp.bfloat16).reshape(rows, length, width)

    g, sums = SimpleNamespace(), SimpleNamespace()
    keep = (target_ids > 0).astype(jnp.float32).reshape(tokens, 1)
    upstream = out_grad.reshape(tokens, width).astype(jnp.float32) * keep
    grad_three, sums.third_gain, sums.third_shift = norm_back(
        upstream, normed_three, inverse_three, third_gain
    )
    grad_outer = grad_three.astype(jnp.bfloat16)
    sums.outer_bias = column_sum(grad_outer)
    (g.outer_weight,) = net.reduce_product(active, [grad_outer])
    grad_active = dense_back(grad_outer, all_.outer_weight)
    grad_inner = (grad_active * slope).astype(jnp.bfloat16)
    sums.inner_bias = column_sum(grad_inner)
    (g.inner_weight,) = net.reduce_product(second, [grad_inner])
    grad_second = grad_three + dense_back(grad_inner, all_.inner_weight)
    grad_two, sums.second_gain, sums.second_shift = norm_back(
        grad_second, normed_two, inverse_two, second_gain
    )
    branch_two = grad_two.astype(jnp.bfloat16)
    sums.cross_output_bias = column_sum(branch_two)
    (g.cross_output,) = net.reduce_product(mixed_two, [branch_two])
    query_grad_two, key_sum_two, value_sum_two = back_two(
        flat(dense_back(branch_two, all_.cross_output))
    )
    key_grad_two = flat(net.scatter_row(key_sum_two))
    value_grad_two = flat(net.scatter_row(value_sum_two))
    query_grad_two = flat(query_grad_two)
    sums.cross_query_bias = column_sum(query_grad_two)
    sums.cross_value_bias = column_sum(value_grad_two)
    (g.cross_query,) = net.reduce_product(first, [query_grad_two])
    g.cross_key, g.cross_value = net.reduce_product(flat_memory, [key_grad_two, value_grad_two])
    memory_grad = low(
        dense_back(key_grad_two, all_.cross_key) + dense_back(value_grad_two, all_.cross_value)
    )
    grad_first = grad_two + dense_back(query_grad_two, all_.cross_query)
    grad_one, sums.first_gain, sums.first_shift = norm_back(
        grad_first, normed_one, inverse_one, first_gain
    )
    branch_one = grad_one.astype(jnp.bfloat16)
    sums.self_output_bias = column_sum(branch_one)
    (g.self_output,) = net.reduce_product(mixed_one, [branch_one])
    query_grad_one, key_sum_one, value_sum_one = back_one(
        flat(dense_back(branch_one, all_.self_output))
    )
    key_grad_one = flat(net.scatter_row(key_sum_one))
    value_grad_one = flat(net.scatter_row(value_sum_one))
    query_grad_one = flat(query_grad_one)
    sums.self_query_bias = column_sum(query_grad_one)
    sums.self_value_bias = column_sum(value_grad_one)
    g.self_query, g.self_key, g.self_value = net.reduce_product(
        flat_in, [query_grad_one, key_grad_one, value_grad_one]
    )
    input_grad = low(
        grad_one
        + dense_back(query_grad_one, all_.self_query)
        + dense_back(key_grad_one, all_.self_key)
        + dense_back(value_grad_one, all_.self_value)
    )
    (
        g.self_query_bias, g.self_value_bias, g.self_output_bias, g.first_gain, g.first_shift,
        g.cross_query_bias, g.cross_value_bias, g.cross_output_bias, g.second_gain,
        g.second_shift, g.inner_bias, g.outer_bias, g.third_gain, g.third_shift,
    ) = net.reduce_vectors(
        [
            sums.self_query_bias, sums.self_value_bias, sums.self_output_bias, sums.first_gain,
            sums.first_shift, sums.cross_query_bias, sums.cross_value_bias,
            sums.cross_output_bias, sums.second_gain, sums.second_shift, sums.inner_bias,
            sums.outer_bias, sums.third_gain, sums.third_shift,
        ]
    )
    return (layer_out, input_grad, memory_grad, *Weights(**vars(g)))


def solution(mesh):
    staged = mesh.shape["fsdp"] == 16 and mesh.shape["seq"] == 2
    row, ids = P("fsdp", "seq", None), P("fsdp", "seq")
    matrix, vector = P("fsdp", None), P("fsdp")
    weights = Weights(
        matrix, vector, matrix, matrix, vector, matrix, vector, vector, vector, matrix, vector,
        matrix, matrix, vector, matrix, vector, vector, vector, matrix, vector, matrix, vector,
        vector, vector,
    )
    return jax.shard_map(
        functools.partial(body, staged),
        mesh=mesh,
        in_specs=(row, row, ids, ids, row, *weights),
        out_specs=(row, row, row, *weights),
        check_vma=False,
    )
```

```python
import functools
import math
from types import SimpleNamespace
from typing import NamedTuple

import jax
import jax.numpy as jnp
from jax import lax
from jax.experimental import pallas as pl
from jax.experimental.pallas import tpu as pltpu
from jax.sharding import PartitionSpec as P

HEAD_DIM = 64
PAIR = 2 * HEAD_DIM
SEGMENTS = 5
TILE = 256
eps_norm = 1e-05
masked_score = -1e30


class Weights(NamedTuple):
    self_query: jax.Array
    self_query_bias: jax.Array
    self_key: jax.Array
    self_value: jax.Array
    self_value_bias: jax.Array
    self_output: jax.Array
    self_output_bias: jax.Array
    first_gain: jax.Array
    first_shift: jax.Array
    cross_query: jax.Array
    cross_query_bias: jax.Array
    cross_key: jax.Array
    cross_value: jax.Array
    cross_value_bias: jax.Array
    cross_output: jax.Array
    cross_output_bias: jax.Array
    second_gain: jax.Array
    second_shift: jax.Array
    inner_weight: jax.Array
    inner_bias: jax.Array
    outer_weight: jax.Array
    outer_bias: jax.Array
    third_gain: jax.Array
    third_shift: jax.Array


def split_vectors(w):
    return [array for array in w if array.ndim == 1]


def dense(left, right):
    return jnp.dot(left, right, preferred_element_type=jnp.float32)


def dense_back(left, right):
    return lax.dot_general(
        left, right, (((1,), (1,)), ((), ())), preferred_element_type=jnp.float32
    )


def dense_grad(left, right):
    return lax.dot_general(
        left, right, (((0,), (0,)), ((), ())), preferred_element_type=jnp.float32
    )


def column_sum(values):
    return jnp.sum(values, axis=0, dtype=jnp.float32)


def layer_norm(resid, gain, shift):
    center = resid - jnp.mean(resid, axis=-1, keepdims=True)
    spread = jnp.mean(center * center, axis=-1, keepdims=True)
    inverse = lax.rsqrt(spread + eps_norm)
    normed = center * inverse
    return (normed * gain + shift, normed, inverse)


def norm_back(upstream, normed, inverse, gain):
    scaled = upstream * gain
    plain_mean = jnp.mean(scaled, axis=-1, keepdims=True)
    cross_mean = jnp.mean(scaled * normed, axis=-1, keepdims=True)
    result = inverse * (scaled - plain_mean - normed * cross_mean)
    return (result, jnp.sum(upstream * normed, axis=0), jnp.sum(upstream, axis=0))


MESH = pl.DeviceIdType.MESH


class Spot:
    def __init__(self):
        f, c = lax.axis_index("fsdp"), lax.axis_index("seq")
        self.c, self.z, self.plane = c, f // 4, f % 4
        self.other = (f, 1 - c)
        self.by_x = ((f // 2) * 2 + (1 - f % 2), c)
        self.by_y = (self.z * 4 + (self.plane + 2) % 4, c)
        self.first = (jnp.where(c == 0, self.by_x[0], self.by_y[0]), c)
        self.second = (jnp.where(c == 0, self.by_y[0], self.by_x[0]), c)
        self.plane_x = self.by_x[0] % 4
        self.plane_y = self.by_y[0] % 4
        self.plane_first = jnp.where(c == 0, self.plane_x, self.plane_y)
        self.plane_second = jnp.where(c == 0, self.plane_y, self.plane_x)
        self.plane_both = 3 - self.plane

    def at_z(self, k):
        z = (self.z + k) % 4
        return z, (z * 4 + self.plane, self.c)

    def meet(self):
        barrier = pltpu.get_barrier_semaphore()
        partners = [self.other, self.by_x, self.by_y] + [self.at_z(k)[1] for k in (1, 2, 3)]
        for partner in partners:
            pl.semaphore_signal(barrier, inc=1, device_id=partner, device_id_type=MESH)
        pl.semaphore_wait(barrier, len(partners))


class Gather:
    sems = 31
    order = (0, 1, 3, 2)

    def __init__(self, spot, shards, wholes, send, recv, local):
        self.spot, self.shards, self.wholes = spot, shards, wholes
        self.send, self.recv, self.local = send, recv, local
        self.all = range(len(shards))

    def _columns(self, j):
        half = self.wholes[j].shape[3] // 2
        return pl.ds(pl.multiple_of(self.spot.c * half, 128), half)

    def _view(self, j, p, plane):
        return self.wholes[j].at[(self.spot.z + 4 - p) % 4, plane, :, self._columns(j)]

    def _copy(self, j, n, source, target, partner):
        return pltpu.make_async_remote_copy(
            source, target, self.send.at[j, n], self.recv.at[j, n], device_id=partner,
            device_id_type=MESH,
        )

    def _z(self, j, k):
        spot = self.spot
        source = self.shards[j].at[:, self._columns(j)]
        return self._copy(j, k - 1, source, self._view(j, 0, spot.plane), spot.at_z(k)[1])

    def _near(self, j, p, way):
        spot = self.spot
        view = self._view(j, p, spot.plane)
        source = view if p else self.shards[j].at[:, self._columns(j)]
        return self._copy(j, 3 + 2 * p + way, source, view, spot.by_y if way else spot.by_x)

    def _far(self, j, p):
        view = self._view(j, p, self.spot.plane_first)
        return self._copy(j, 11 + p, view, view, self.spot.second)

    def _swap(self, j, p, n):
        spot = self.spot
        plane = (spot.plane, spot.plane_x, spot.plane_y, spot.plane_both)[n]
        view = self._view(j, p, plane)
        return self._copy(j, 15 + 4 * p + n, view, view, spot.other)

    def _locals(self):
        return [
            pltpu.make_async_copy(
                self.shards[j], self.wholes[j].at[self.spot.z, self.spot.plane], self.local.at[j]
            )
            for j in self.all
        ]

    def start(self):
        for k in self.order[1:2]:
            for j in self.all:
                self._z(j, k).start()
        for j in self.all:
            for way in range(2):
                self._near(j, 0, way).start()
        for k in self.order[2:]:
            for j in self.all:
                self._z(j, k).start()
        for copy in self._locals():
            copy.start()

    def advance(self, i):
        if i < 4:
            p = self.order[i]
            for j in self.all:
                self._z(j, p).wait_recv()
                self._near(j, p, 0).start()
                self._near(j, p, 1).start()
                self._swap(j, p, 0).start()
        if 1 <= i < 5:
            p = self.order[i - 1]
            for j in self.all:
                self._near(j, p, 0).wait_recv()
                self._near(j, p, 1).wait_recv()
                self._far(j, p).start()
                self._swap(j, p, 1).start()
                self._swap(j, p, 2).start()
        if 2 <= i < 6:
            p = self.order[i - 2]
            for j in self.all:
                self._far(j, p).wait_recv()
                self._swap(j, p, 3).start()

    def finish(self):
        for copy in self._locals():
            copy.wait()
        for j in self.all:
            for p in self.order:
                if p:
                    self._z(j, p).wait_send()
                self._near(j, p, 0).wait_send()
                self._near(j, p, 1).wait_send()
                self._far(j, p).wait_send()
                for n in range(0 if p else 1, 4):
                    self._swap(j, p, n).wait()
class Reduce:
    sems = 21
    order = (2, 3, 1, 0)

    def __init__(self, spot, parts, outs, mine, there, far, near, line, send, recv, local):
        self.spot, self.parts, self.outs = spot, parts, outs
        self.mine, self.there, self.far, self.near, self.line = mine, there, far, near, line
        self.send, self.recv, self.local = send, recv, local
        self.all = range(len(parts))

    @staticmethod
    def scratch(shapes, dtypes):
        def buffers(*lead):
            return [pltpu.VMEM((*lead, r, w // 2), d) for (r, w), d in zip(shapes, dtypes)]
        n = len(shapes)
        return (
            buffers(4, 4) + buffers(4, 4) + buffers(4) + buffers(4, 2) + buffers(4)
            + [
                pltpu.SemaphoreType.DMA((n, Reduce.sems)),
                pltpu.SemaphoreType.DMA((n, Reduce.sems)),
                pltpu.SemaphoreType.DMA((n, 4)),
            ]
        )

    @staticmethod
    def unpack(spot, parts, outs, refs):
        n = len(parts)
        groups = [refs[i * n : (i + 1) * n] for i in range(5)]
        return Reduce(spot, parts, outs, *groups, *refs[5 * n : 5 * n + 3])

    def _columns(self, j, core):
        half = self.parts[j].shape[3] // 2
        return pl.ds(pl.multiple_of(core * half, 128), half)

    def _part(self, j, p, core):
        return self.parts[j].at[(self.spot.z + p) % 4, :, :, self._columns(j, core)]

    def _copy(self, j, n, source, target, partner):
        return pltpu.make_async_remote_copy(
            source, target, self.send.at[j, n], self.recv.at[j, n], device_id=partner,
            device_id_type=MESH,
        )

    def _own(self, j, p):
        return pltpu.make_async_copy(
            self._part(j, p, self.spot.c), self.mine[j].at[p], self.local.at[j, p]
        )

    def _cross(self, j, p):
        spot = self.spot
        return self._copy(j, p, self._part(j, p, 1 - spot.c), self.there[j].at[p], spot.other)

    def _far(self, j, p):
        spot = self.spot
        return self._copy(
            j, 4 + p, self.mine[j].at[p, spot.plane_both], self.far[j].at[p], spot.first
        )

    def _near(self, j, p, way):
        spot = self.spot
        plane, partner = (spot.plane_y, spot.by_y) if way else (spot.plane_x, spot.by_x)
        return self._copy(
            j, 8 + 2 * p + way, self.mine[j].at[p, plane], self.near[j].at[p, way], partner
        )

    def _line(self, j, p):
        spot = self.spot
        return self._copy(
            j, 16 + p, self.mine[j].at[p, spot.plane], self.line[j].at[p], spot.at_z(p)[1]
        )

    def _last(self, j):
        view = self.outs[j].at[:, self._columns(j, self.spot.c)]
        return self._copy(j, 20, view, view, self.spot.other)

    def start(self):
        for p in self.order:
            for j in self.all:
                self._own(j, p).start()
                self._cross(j, p).start()

    def _sum(self, j, p, plane, *others):
        total = self.mine[j][p, plane].astype(jnp.float32)
        total = total + self.there[j][p, plane].astype(jnp.float32)
        for other in others:
            total = total + other.astype(jnp.float32)
        return total

    def _store(self, j, p, plane, total):
        self.mine[j][p, plane] = total.astype(self.mine[j].dtype)

    def advance(self, i):
        spot = self.spot
        if i < 4:
            p = self.order[i]
            for j in self.all:
                self._own(j, p).wait()
                self._cross(j, p).wait_recv()
                self._store(j, p, spot.plane_both, self._sum(j, p, spot.plane_both))
                self._far(j, p).start()
        if 0 <= i - 1 < 4:
            p = self.order[i - 1]
            for j in self.all:
                self._store(j, p, spot.plane_first, self._sum(j, p, spot.plane_first))
                self._far(j, p).wait_recv()
                self._store(
                    j, p, spot.plane_second, self._sum(j, p, spot.plane_second, self.far[j][p])
                )
                self._near(j, p, 0).start()
                self._near(j, p, 1).start()
        if 0 <= i - 2 < 4:
            p = self.order[i - 2]
            for j in self.all:
                self._near(j, p, 0).wait_recv()
                self._near(j, p, 1).wait_recv()
                total = self._sum(j, p, spot.plane, self.near[j][p, 0], self.near[j][p, 1])
                if p:
                    self._store(j, p, spot.plane, total)
                    self._line(j, p).start()
                else:
                    for k in (1, 2, 3):
                        self._line(j, k).wait_recv()
                        total = total + self.line[j][k].astype(jnp.float32)
                    self.outs[j][:, self._columns(j, spot.c)] = total
                    self._last(j).start()

    def finish(self):
        for j in self.all:
            for p in self.order:
                self._cross(j, p).wait_send()
                self._far(j, p).wait_send()
                self._near(j, p, 0).wait_send()
                self._near(j, p, 1).wait_send()
                if p:
                    self._line(j, p).wait_send()
            self._last(j).wait()


def gather_kernel(count, *refs):
    shards, wholes, sems = refs[:count], refs[count : 2 * count], refs[2 * count :]
    spot = Spot()
    spot.meet()
    gather = Gather(spot, shards, wholes, *sems)
    gather.start()
    for i in range(1, 6):
        gather.advance(i)
    gather.finish()


def reduce_kernel(count, *refs):
    spot = Spot()
    spot.meet()
    reduce = Reduce.unpack(spot, refs[:count], refs[count : 2 * count], refs[2 * count :])
    reduce.start()
    for i in range(6):
        reduce.advance(i)
    reduce.finish()


class Staged:
    staged = True

    def __init__(self):
        self.c = lax.axis_index("seq")
        self.parts = []

    def swap(self, array):
        pairs = [(f * 2 + c, f * 2 + 1 - c) for f in range(16) for c in range(2)]
        return lax.ppermute(array, ("fsdp", "seq"), pairs)

    def gather(self, shards, vectors):
        narrow = [v for v in vectors if v.shape[0] == 48]
        (wide,) = [v for v in vectors if v.shape[0] != 48]
        table = jnp.concatenate([jnp.stack(narrow), wide.reshape(-1, 48)]).astype(jnp.float32)
        table = jnp.pad(table, ((0, 24 - table.shape[0]), (0, 256 - 48)))
        shards = [*shards, table]
        count = len(shards)
        anywhere = pl.BlockSpec(memory_space=pl.ANY)
        *wholes, table = pl.pallas_call(
            functools.partial(gather_kernel, count),
            out_shape=[jax.ShapeDtypeStruct((4, 4) + s.shape, s.dtype) for s in shards],
            in_specs=[anywhere] * count,
            out_specs=[anywhere] * count,
            scratch_shapes=[
                pltpu.SemaphoreType.DMA((count, Gather.sems)),
                pltpu.SemaphoreType.DMA((count, Gather.sems)),
                pltpu.SemaphoreType.DMA((count,)),
            ],
            compiler_params=pltpu.CompilerParams(collective_id=0, has_side_effects=True),
        )(*shards)
        rows = len(narrow)
        table = table[:, :, :, :48].reshape(16, 24, 48)
        lines = table[:, :rows].transpose(1, 0, 2).reshape(rows, 768)
        wholes_1d, row = [], 0
        for v in vectors:
            if v.shape[0] == 48:
                wholes_1d.append(lines[row])
                row += 1
            else:
                wholes_1d.append(table[:, rows : rows + v.shape[0] // 48].reshape(-1))
        return [w.reshape(-1, w.shape[3]) for w in wholes], wholes_1d

    def reduce(self, products, vectors):
        parts = [
            dense_grad(left, right).astype(jnp.bfloat16).reshape(4, 4, -1, right.shape[1])
            for left, right in products
        ]
        narrow = [v for v in vectors if v.shape[0] == 768]
        (wide,) = [v for v in vectors if v.shape[0] != 768]
        rows = len(narrow)
        table = jnp.concatenate(
            [
                jnp.stack(narrow).reshape(rows, 16, 48).transpose(1, 0, 2),
                wide.reshape(16, -1, 48),
            ],
            axis=1,
        )
        table = jnp.pad(table, ((0, 0), (0, 24 - table.shape[1]), (0, 256 - 48)))
        parts.append(table.reshape(4, 4, 24, 256))
        count = len(parts)
        shapes = [p.shape[2:] for p in parts]
        *results, table = pl.pallas_call(
            functools.partial(reduce_kernel, count),
            out_shape=[jax.ShapeDtypeStruct(s, jnp.float32) for s in shapes],
            in_specs=[pl.BlockSpec(memory_space=pl.ANY)] * count,
            out_specs=[pl.BlockSpec(memory_space=pltpu.VMEM)] * count,
            scratch_shapes=Reduce.scratch(shapes, [p.dtype for p in parts]),
            compiler_params=pltpu.CompilerParams(
                collective_id=1, has_side_effects=True, vmem_limit_bytes=56 * 2**20
            ),
        )(*parts)
        sums, row = [], 0
        for v in vectors:
            if v.shape[0] == 768:
                sums.append(table[row, :48])
                row += 1
            else:
                sums.append(table[rows : rows + v.shape[0] // 768, :48].reshape(-1))
        return results, sums


    def gather_row(self, array):
        return jnp.concatenate([array, self.swap(array)], axis=1)

    def scatter_row(self, array):
        length = array.shape[1] // 2
        there = self.swap(array[:, length:].astype(jnp.bfloat16))
        return array[:, :length].astype(jnp.float32) + there.astype(jnp.float32)


class Plain:
    staged = False

    def gather(self, shards, vectors):
        results = [lax.all_gather(s, "fsdp", axis=0, tiled=True) for s in shards]
        return results, [
            lax.all_gather(v, "fsdp", axis=0, tiled=True).astype(jnp.float32) for v in vectors
        ]

    def _reduce(self, total):
        part = lax.psum_scatter(
            total.astype(jnp.bfloat16), "fsdp", scatter_dimension=0, tiled=True
        )
        return lax.psum(part, "seq").astype(jnp.float32)

    def reduce(self, products, vectors):
        return (
            [self._reduce(dense_grad(left, right)) for left, right in products],
            [self._reduce(v) for v in vectors],
        )

    def gather_row(self, array):
        return lax.all_gather(array, "seq", axis=1, tiled=True)

    def places(self, length):
        return jnp.arange(length * lax.axis_size("seq"))

    def scatter_row(self, array):
        return lax.psum_scatter(
            array.astype(jnp.bfloat16), "seq", scatter_dimension=1, tiled=True
        ).astype(jnp.float32)


def query_marks(ids):
    lanes = jnp.arange(PAIR)[None, :] % HEAD_DIM
    return jnp.where((lanes < SEGMENTS) & (ids[:, None] != lanes), masked_score, 0.0).astype(
        jnp.bfloat16
    )


def key_marks_of(ids):
    lanes = jnp.arange(PAIR)[None, :] % HEAD_DIM
    ones = (lanes >= SEGMENTS) & (lanes < SEGMENTS + 3)
    return (ones | (ids[:, None] == lanes)).astype(jnp.bfloat16)


def against(left, right):
    return lax.dot_general(
        left, right, (((1,), (1,)), ((), ())), preferred_element_type=jnp.float32
    )


def three(value):
    high = value.astype(jnp.bfloat16).astype(jnp.float32)
    rest = value - high
    middle = rest.astype(jnp.bfloat16).astype(jnp.float32)
    return high, middle, rest - middle


def place_three(lanes, base, value, other):
    high, middle, small = three(value)
    first = base + SEGMENTS
    return jnp.where(
        lanes == first,
        high,
        jnp.where(lanes == first + 1, middle, jnp.where(lanes == first + 2, small, other)),
    )


def plan(length, causal, later):
    half = length // 2
    result = []
    for tile in range(2):
        if not causal:
            result.append([(0, 2 * length, False)])
            continue
        ranges = [(0, half, False)] if tile else []
        ranges.append((tile * half, half, True))
        if later:
            ranges.append((length + tile * half, length - tile * half, False))
        result.append(ranges)
    return result


def each_plan(core, length, causal, run):
    if not causal:
        run(plan(length, False, False))
        return
    for later in range(2):
        @pl.when(core == later)
        def _():
            run(plan(length, True, bool(later)))


def forward_kernel(causal, core_ref, q_ref, k_ref, v_ref, qm_ref, km_ref, mixed_ref, qx_ref):
    length = q_ref.shape[0]

    def run(tiles):
        for head in range(2):
            base = HEAD_DIM * (1 - head)

            def own(lanes):
                return (lanes < HEAD_DIM) if head == 0 else (lanes >= HEAD_DIM)

            for tile, ranges in enumerate(tiles):
                rows = slice(tile * TILE, tile * TILE + TILE)
                lanes = lax.broadcasted_iota(jnp.int32, (TILE, PAIR), 1)
                q = jnp.where(own(lanes), q_ref[rows, :], qm_ref[rows, :])
                scores = []
                for start, size, diagonal in ranges:
                    keys = slice(start, start + size)
                    key_lanes = lax.broadcasted_iota(jnp.int32, (size, PAIR), 1)
                    k = jnp.where(own(key_lanes), k_ref[keys, :], km_ref[keys, :])
                    s = against(q, k)
                    if diagonal:
                        i = lax.broadcasted_iota(jnp.int32, s.shape, 0)
                        j = lax.broadcasted_iota(jnp.int32, s.shape, 1)
                        s = jnp.where(j <= i, s, masked_score)
                    scores.append(s)
                highest = functools.reduce(
                    jnp.maximum, [jnp.max(s, axis=1, keepdims=True) for s in scores]
                )
                out = jnp.zeros((TILE, PAIR), jnp.float32)
                for s, (start, size, _) in zip(scores, ranges):
                    keys = slice(start, start + size)
                    key_lanes = lax.broadcasted_iota(jnp.int32, (size, PAIR), 1)
                    v = jnp.where(own(key_lanes), v_ref[keys, :], jnp.ones((), jnp.bfloat16))
                    e = jnp.exp(s - highest).astype(jnp.bfloat16)
                    out = out + jnp.dot(e, v, preferred_element_type=jnp.float32)
                total = pltpu.roll(out, HEAD_DIM, 1)
                mixed = (out / total).astype(jnp.bfloat16)
                if head:
                    mixed = jnp.where(own(lanes), mixed, mixed_ref[rows, :])
                mixed_ref[rows, :] = mixed
                logsum = highest + jnp.log(out)
                qx = place_three(lanes, base, -logsum, q.astype(jnp.float32))
                qx_ref[head, rows, :] = qx.astype(jnp.bfloat16)

    each_plan(core_ref[0], length, causal, run)


def attend(core, query, keys, values, q_marks, k_marks, causal):
    length, width = query.shape
    extent = keys.shape[0]
    pairs = width // PAIR
    column = lambda rows: pl.BlockSpec((rows, PAIR), lambda i, p: (0, i))
    fixed = lambda rows: pl.BlockSpec((rows, PAIR), lambda i, p: (0, 0))
    return pl.pallas_call(
        functools.partial(forward_kernel, causal),
        out_shape=[
            jax.ShapeDtypeStruct((length, width), jnp.bfloat16),
            jax.ShapeDtypeStruct((2 * pairs, length, PAIR), jnp.bfloat16),
        ],
        grid_spec=pltpu.PrefetchScalarGridSpec(
            num_scalar_prefetch=1,
            grid=(pairs,),
            in_specs=[column(length), column(extent), column(extent), fixed(length), fixed(extent)],
            out_specs=[column(length), pl.BlockSpec((2, length, PAIR), lambda i, p: (i, 0, 0))],
        ),
        compiler_params=pltpu.CompilerParams(vmem_limit_bytes=48 * 2**20),
        cost_estimate=pl.CostEstimate(
            flops=16 * length * extent * width, bytes_accessed=8 * extent * width, transcendentals=0
        ),
    )(core, query, keys, values, q_marks, k_marks)


def backward_kernel(
    causal, core_ref, qx_ref, k_ref, v_ref, e_ref, o_ref, km_ref, dq_ref, dk_ref, dv_ref, dk_acc, dv_acc, dq_acc
):
    length = e_ref.shape[0]
    scale = HEAD_DIM ** (-0.5)

    def run(tiles):
        dk_acc[...] = jnp.zeros_like(dk_acc)
        dv_acc[...] = jnp.zeros_like(dv_acc)
        for head in range(2):
            base = HEAD_DIM * (1 - head)

            def own(lanes):
                return (lanes < HEAD_DIM) if head == 0 else (lanes >= HEAD_DIM)

            for tile, ranges in enumerate(tiles):
                rows = slice(tile * TILE, tile * TILE + TILE)
                lanes = lax.broadcasted_iota(jnp.int32, (TILE, PAIR), 1)
                nothing = jnp.zeros((), jnp.bfloat16)
                qx = qx_ref[head, rows, :]
                q = jnp.where(own(lanes), qx, nothing)
                e = jnp.where(own(lanes), e_ref[rows, :], nothing)
                wide = e.astype(jnp.float32)
                delta = jnp.sum(wide * o_ref[rows, :].astype(jnp.float32), axis=1, keepdims=True)
                ex = place_three(lanes, base, -delta, wide).astype(jnp.bfloat16)
                dq = jnp.zeros((HEAD_DIM, TILE), jnp.float32)
                for start, size, diagonal in ranges:
                    keys = slice(start, start + size)
                    key_lanes = lax.broadcasted_iota(jnp.int32, (size, PAIR), 1)
                    k = jnp.where(own(key_lanes), k_ref[keys, :], km_ref[keys, :])
                    v = jnp.where(own(key_lanes), v_ref[keys, :], km_ref[keys, :])
                    p = jnp.exp(against(k, qx))
                    if diagonal:
                        j = lax.broadcasted_iota(jnp.int32, p.shape, 0)
                        i = lax.broadcasted_iota(jnp.int32, p.shape, 1)
                        p = jnp.where(j <= i, p, 0.0)
                    ds = (p * against(v, ex)).astype(jnp.bfloat16)
                    p = p.astype(jnp.bfloat16)
                    dv_acc[keys, :] += jnp.dot(p, e, preferred_element_type=jnp.float32)
                    dk_acc[keys, :] += jnp.dot(ds, q, preferred_element_type=jnp.float32)
                    kt = k_ref[keys, :].T[head * HEAD_DIM : (head + 1) * HEAD_DIM, :]
                    dq = dq + jnp.dot(kt, ds, preferred_element_type=jnp.float32)
                dq_acc[head * HEAD_DIM : (head + 1) * HEAD_DIM, rows] = dq
        dq_ref[...] = (dq_acc[...].T.astype(jnp.bfloat16) * jnp.bfloat16(scale)).astype(jnp.bfloat16)
        dk_ref[...] = dk_acc[...].astype(jnp.bfloat16)
        dv_ref[...] = dv_acc[...].astype(jnp.bfloat16)

    each_plan(core_ref[0], length, causal, run)


def attend_back(core, qx, keys, values, grad, mixed, k_marks, causal):
    length, width = grad.shape
    extent = keys.shape[0]
    pairs = width // PAIR
    column = lambda rows: pl.BlockSpec((rows, PAIR), lambda i, p: (0, i))
    fixed = lambda rows: pl.BlockSpec((rows, PAIR), lambda i, p: (0, 0))
    return pl.pallas_call(
        functools.partial(backward_kernel, causal),
        out_shape=[
            jax.ShapeDtypeStruct((length, width), jnp.bfloat16),
            jax.ShapeDtypeStruct((extent, width), jnp.bfloat16),
            jax.ShapeDtypeStruct((extent, width), jnp.bfloat16),
        ],
        grid_spec=pltpu.PrefetchScalarGridSpec(
            num_scalar_prefetch=1,
            grid=(pairs,),
            in_specs=[
                pl.BlockSpec((2, length, PAIR), lambda i, p: (i, 0, 0)),
                column(extent), column(extent), column(length), column(length), fixed(extent),
            ],
            out_specs=[column(length), column(extent), column(extent)],
            scratch_shapes=[
                pltpu.VMEM((extent, PAIR), jnp.float32),
                pltpu.VMEM((extent, PAIR), jnp.float32),
                pltpu.VMEM((PAIR, length), jnp.float32),
            ],
        ),
        compiler_params=pltpu.CompilerParams(vmem_limit_bytes=48 * 2**20),
        cost_estimate=pl.CostEstimate(
            flops=40 * length * extent * width, bytes_accessed=16 * extent * width, transcendentals=0
        ),
    )(core, qx, keys, values, grad, mixed, k_marks)


def head_slice(array, start, span):
    piece = lax.dynamic_slice_in_dim(array, start, span, 2)
    return piece.reshape(array.shape[0], array.shape[1], 2, span // 2)


def plain_attend(query, keys, values, allowed):
    rows, length, width = query.shape
    span = 2 * HEAD_DIM
    pairs = width // span

    def one_pair(index, carry):
        mixed, logsum = carry
        start = index * span
        query_part = head_slice(query, start, span)
        key_part = head_slice(keys, start, span)
        value_part = head_slice(values, start, span)
        scores = jnp.einsum(
            "rqhe,rkhe->rhqk", query_part, key_part, preferred_element_type=jnp.float32
        )
        scores = jnp.where(allowed[:, None], scores, masked_score)
        highest = jnp.max(scores, axis=-1, keepdims=True)
        exponent = jnp.exp(scores - highest)
        total = jnp.sum(exponent, axis=-1, keepdims=True)
        probs = (exponent / total).astype(jnp.bfloat16)
        part = jnp.einsum("rhqk,rkhe->rqhe", probs, value_part, preferred_element_type=jnp.float32)
        mixed = lax.dynamic_update_slice_in_dim(mixed, part.reshape(rows, length, span), start, 2)
        logsum = lax.dynamic_update_slice_in_dim(
            logsum, (highest + jnp.log(total))[None, :, :, :, 0], index, 0
        )
        return (mixed, logsum)

    mixed = jnp.zeros((rows, length, width), jnp.float32)
    logsum = jnp.zeros((pairs, rows, 2, length), jnp.float32)
    return lax.fori_loop(0, pairs, one_pair, (mixed, logsum))


def plain_attend_back(query, keys, values, allowed, logsum, grad_mixed):
    rows, length, width = query.shape
    extent = keys.shape[1]
    span = 2 * HEAD_DIM
    pairs = width // span

    def one_pair(index, carry):
        start = index * span
        query_part = head_slice(query, start, span)
        key_part = head_slice(keys, start, span)
        value_part = head_slice(values, start, span)
        grad_part = head_slice(grad_mixed, start, span)
        scores = jnp.einsum(
            "rqhe,rkhe->rhqk", query_part, key_part, preferred_element_type=jnp.float32
        )
        scores = jnp.where(allowed[:, None], scores, masked_score)
        pair_logsum = lax.dynamic_index_in_dim(logsum, index, 0, keepdims=False)
        probs = jnp.exp(scores - pair_logsum[..., None])
        prob_grad = jnp.einsum(
            "rqhe,rkhe->rhqk", grad_part, value_part, preferred_element_type=jnp.float32
        )
        row_total = jnp.sum(probs * prob_grad, axis=-1, keepdims=True)
        score_grad = (probs * (prob_grad - row_total)).astype(jnp.bfloat16)
        query_grad = jnp.einsum(
            "rhqk,rkhe->rqhe", score_grad, key_part, preferred_element_type=jnp.float32
        )
        grad_query = lax.dynamic_update_slice_in_dim(
            carry[0], query_grad.reshape(rows, length, span), start, 2
        )
        probs_low = probs.astype(jnp.bfloat16)
        value_grad = jnp.einsum(
            "rhqk,rqhe->rkhe", probs_low, grad_part, preferred_element_type=jnp.float32
        )
        key_grad = jnp.einsum(
            "rhqk,rqhe->rkhe", score_grad, query_part, preferred_element_type=jnp.float32
        )
        grad_keys = lax.dynamic_update_slice_in_dim(
            carry[1], key_grad.reshape(rows, extent, span), start, 2
        )
        grad_values = lax.dynamic_update_slice_in_dim(
            carry[2], value_grad.reshape(rows, extent, span), start, 2
        )
        return (grad_query, grad_keys, grad_values)

    start_query = jnp.zeros((rows, length, width), jnp.float32)
    start_keys = jnp.zeros((rows, extent, width), jnp.float32)
    return lax.fori_loop(0, pairs, one_pair, (start_query, start_keys, start_keys))


def attention(net, query, keys, values, target_ids, key_ids, causal):
    rows, length, width = query.shape
    if net.staged and rows == 1 and length == 2 * TILE:
        core = net.c.reshape(1)
        k_marks = key_marks_of(key_ids[0])
        q_marks = query_marks(target_ids[0])
        mixed, qx = attend(core, query[0], keys[0], values[0], q_marks, k_marks, causal)

        def back(grad):
            results = attend_back(core, qx, keys[0], values[0], grad, mixed, k_marks, causal)
            return [array[None] for array in results]

        return mixed, back
    allowed = target_ids[:, :, None] == key_ids[:, None, :]
    if causal:
        query_places = lax.axis_index("seq") * length + jnp.arange(length)
        allowed &= net.places(length)[None, None, :] <= query_places[None, :, None]
    mixed, logsum = plain_attend(query, keys, values, allowed)

    def plain_back(grad):
        query_sum, key_sum, value_sum = plain_attend_back(
            query, keys, values, allowed, logsum, grad.reshape(rows, length, width)
        )
        return [query_sum.astype(jnp.bfloat16) * HEAD_DIM ** (-0.5), key_sum, value_sum]

    return mixed.astype(jnp.bfloat16).reshape(rows * length, width), plain_back


def body(staged, hidden_in, memory, target_ids, memory_ids, out_grad, *weights):
    w = Weights(*weights)
    net = Staged() if staged else Plain()
    all_ = SimpleNamespace()
    (
        all_.self_query, all_.self_key, all_.self_value, all_.self_output, all_.cross_query,
        all_.cross_key, all_.cross_value, all_.cross_output, all_.inner_weight, all_.outer_weight,
    ), vectors = net.gather(
        [
            w.self_query, w.self_key, w.self_value, w.self_output, w.cross_query, w.cross_key,
            w.cross_value, w.cross_output, w.inner_weight, w.outer_weight,
        ],
        split_vectors(w),
    )
    (
        self_query_bias, self_value_bias, self_output_bias, first_gain, first_shift,
        cross_query_bias, cross_value_bias, cross_output_bias, second_gain, second_shift,
        inner_bias, outer_bias, third_gain, third_shift,
    ) = vectors

    rows, length, width = hidden_in.shape
    tokens = rows * length
    scale = HEAD_DIM ** (-0.5)
    flat_in = hidden_in.reshape(tokens, width)
    flat_memory = memory.reshape(tokens, width)

    def flat(array):
        return array.astype(jnp.bfloat16).reshape(tokens, width)

    def low(array):
        return array.astype(jnp.bfloat16).reshape(rows, length, width)

    row_ids, source_ids = net.gather_row(target_ids), net.gather_row(memory_ids)
    key_one = low(dense(flat_in, all_.self_key))
    value_one = low(dense(flat_in, all_.self_value) + self_value_bias)
    query_one = low((dense(flat_in, all_.self_query) + self_query_bias) * scale)
    keys_one, values_one = net.gather_row(key_one), net.gather_row(value_one)
    mixed_one, back_one = attention(
        net, query_one, keys_one, values_one, target_ids, row_ids, True
    )

    key_two = low(dense(flat_memory, all_.cross_key))
    value_two = low(dense(flat_memory, all_.cross_value) + cross_value_bias)
    keys_two, values_two = net.gather_row(key_two), net.gather_row(value_two)

    resid_one = (
        flat_in.astype(jnp.float32) + dense(mixed_one, all_.self_output) + self_output_bias
    )
    first, normed_one, inverse_one = layer_norm(resid_one, first_gain, first_shift)
    first = first.astype(jnp.bfloat16)
    query_two = low((dense(first, all_.cross_query) + cross_query_bias) * scale)
    mixed_two, back_two = attention(
        net, query_two, keys_two, values_two, target_ids, source_ids, False
    )
    resid_two = (
        first.astype(jnp.float32) + dense(mixed_two, all_.cross_output) + cross_output_bias
    )
    second, normed_two, inverse_two = layer_norm(resid_two, second_gain, second_shift)
    second = second.astype(jnp.bfloat16)
    inner = dense(second, all_.inner_weight) + inner_bias
    cumulative = 0.5 * (1.0 + lax.erf(inner * math.sqrt(0.5)))
    active = (inner * cumulative).astype(jnp.bfloat16)
    density = jnp.exp(-0.5 * inner * inner) * (1.0 / math.sqrt(2.0 * math.pi))
    slope = cumulative + inner * density
    resid_three = second.astype(jnp.float32) + dense(active, all_.outer_weight) + outer_bias
    final, normed_three, inverse_three = layer_norm(resid_three, third_gain, third_shift)
    layer_out = final.astype(jnp.bfloat16).reshape(rows, length, width)

    g, sums = SimpleNamespace(), SimpleNamespace()
    keep = (target_ids > 0).astype(jnp.float32).reshape(tokens, 1)
    upstream = out_grad.reshape(tokens, width).astype(jnp.float32) * keep
    grad_three, sums.third_gain, sums.third_shift = norm_back(
        upstream, normed_three, inverse_three, third_gain
    )
    grad_outer = grad_three.astype(jnp.bfloat16)
    sums.outer_bias = column_sum(grad_outer)
    grad_active = dense_back(grad_outer, all_.outer_weight)
    grad_inner = (grad_active * slope).astype(jnp.bfloat16)
    sums.inner_bias = column_sum(grad_inner)
    grad_second = grad_three + dense_back(grad_inner, all_.inner_weight)
    grad_two, sums.second_gain, sums.second_shift = norm_back(
        grad_second, normed_two, inverse_two, second_gain
    )
    branch_two = grad_two.astype(jnp.bfloat16)
    sums.cross_output_bias = column_sum(branch_two)
    query_grad_two, key_sum_two, value_sum_two = back_two(
        flat(dense_back(branch_two, all_.cross_output))
    )
    key_grad_two = flat(net.scatter_row(key_sum_two))
    value_grad_two = flat(net.scatter_row(value_sum_two))
    query_grad_two = flat(query_grad_two)
    sums.cross_query_bias = column_sum(query_grad_two)
    sums.cross_value_bias = column_sum(value_grad_two)
    memory_grad = low(
        dense_back(key_grad_two, all_.cross_key) + dense_back(value_grad_two, all_.cross_value)
    )
    grad_first = grad_two + dense_back(query_grad_two, all_.cross_query)
    grad_one, sums.first_gain, sums.first_shift = norm_back(
        grad_first, normed_one, inverse_one, first_gain
    )
    branch_one = grad_one.astype(jnp.bfloat16)
    sums.self_output_bias = column_sum(branch_one)
    query_grad_one, key_sum_one, value_sum_one = back_one(
        flat(dense_back(branch_one, all_.self_output))
    )
    key_grad_one = flat(net.scatter_row(key_sum_one))
    value_grad_one = flat(net.scatter_row(value_sum_one))
    query_grad_one = flat(query_grad_one)
    sums.self_query_bias = column_sum(query_grad_one)
    sums.self_value_bias = column_sum(value_grad_one)
    input_grad = low(
        grad_one
        + dense_back(query_grad_one, all_.self_query)
        + dense_back(key_grad_one, all_.self_key)
        + dense_back(value_grad_one, all_.self_value)
    )
    (
        g.self_query, g.self_key, g.self_value, g.self_output, g.cross_query, g.cross_key,
        g.cross_value, g.cross_output, g.inner_weight, g.outer_weight,
    ), (
        g.self_query_bias, g.self_value_bias, g.self_output_bias, g.first_gain, g.first_shift,
        g.cross_query_bias, g.cross_value_bias, g.cross_output_bias, g.second_gain,
        g.second_shift, g.inner_bias, g.outer_bias, g.third_gain, g.third_shift,
    ) = net.reduce(
        [
            (flat_in, query_grad_one), (flat_in, key_grad_one), (flat_in, value_grad_one),
            (mixed_one, branch_one), (first, query_grad_two), (flat_memory, key_grad_two),
            (flat_memory, value_grad_two), (mixed_two, branch_two), (second, grad_inner),
            (active, grad_outer),
        ],
        [
            sums.self_query_bias, sums.self_value_bias, sums.self_output_bias, sums.first_gain,
            sums.first_shift, sums.cross_query_bias, sums.cross_value_bias,
            sums.cross_output_bias, sums.second_gain, sums.second_shift, sums.inner_bias,
            sums.outer_bias, sums.third_gain, sums.third_shift,
        ],
    )
    return (layer_out, input_grad, memory_grad, *Weights(**vars(g)))


def solution(mesh):
    staged = mesh.shape["fsdp"] == 16 and mesh.shape["seq"] == 2
    row, ids = P("fsdp", "seq", None), P("fsdp", "seq")
    matrix, vector = P("fsdp", None), P("fsdp")
    weights = Weights(
        matrix, vector, matrix, matrix, vector, matrix, vector, vector, vector, matrix, vector,
        matrix, matrix, vector, matrix, vector, vector, vector, matrix, vector, matrix, vector,
        vector, vector,
    )
    return jax.shard_map(
        functools.partial(body, staged),
        mesh=mesh,
        in_specs=(row, row, ids, ids, row, *weights),
        out_specs=(row, row, row, *weights),
        check_vma=False,
    )
```

```python
import functools
import math
from types import SimpleNamespace
from typing import NamedTuple

import jax
import jax.numpy as jnp
from jax import lax
from jax.experimental import pallas as pl
from jax.experimental.pallas import tpu as pltpu
from jax.sharding import PartitionSpec as P

HEAD_DIM = 64
PAIR = 2 * HEAD_DIM
SEGMENTS = 5
TILE = 256
eps_norm = 1e-05
masked_score = -1e30


class Weights(NamedTuple):
    self_query: jax.Array
    self_query_bias: jax.Array
    self_key: jax.Array
    self_value: jax.Array
    self_value_bias: jax.Array
    self_output: jax.Array
    self_output_bias: jax.Array
    first_gain: jax.Array
    first_shift: jax.Array
    cross_query: jax.Array
    cross_query_bias: jax.Array
    cross_key: jax.Array
    cross_value: jax.Array
    cross_value_bias: jax.Array
    cross_output: jax.Array
    cross_output_bias: jax.Array
    second_gain: jax.Array
    second_shift: jax.Array
    inner_weight: jax.Array
    inner_bias: jax.Array
    outer_weight: jax.Array
    outer_bias: jax.Array
    third_gain: jax.Array
    third_shift: jax.Array


def split_vectors(w):
    return [array for array in w if array.ndim == 1]


def dense(left, right):
    return jnp.dot(left, right, preferred_element_type=jnp.float32)


def dense_back(left, right):
    return lax.dot_general(
        left, right, (((1,), (1,)), ((), ())), preferred_element_type=jnp.float32
    )


def dense_grad(left, right):
    return lax.dot_general(
        left, right, (((0,), (0,)), ((), ())), preferred_element_type=jnp.float32
    )


def column_sum(values):
    return jnp.sum(values, axis=0, dtype=jnp.float32)


def layer_norm(resid, gain, shift):
    center = resid - jnp.mean(resid, axis=-1, keepdims=True)
    spread = jnp.mean(center * center, axis=-1, keepdims=True)
    inverse = lax.rsqrt(spread + eps_norm)
    normed = center * inverse
    return (normed * gain + shift, normed, inverse)


def norm_back(upstream, normed, inverse, gain):
    scaled = upstream * gain
    plain_mean = jnp.mean(scaled, axis=-1, keepdims=True)
    cross_mean = jnp.mean(scaled * normed, axis=-1, keepdims=True)
    result = inverse * (scaled - plain_mean - normed * cross_mean)
    return (result, jnp.sum(upstream * normed, axis=0), jnp.sum(upstream, axis=0))


MESH = pl.DeviceIdType.MESH


class Spot:
    def __init__(self):
        f, c = lax.axis_index("fsdp"), lax.axis_index("seq")
        self.c, self.z, self.plane = c, f // 4, f % 4
        self.other = (f, 1 - c)
        self.by_x = ((f // 2) * 2 + (1 - f % 2), c)
        self.by_y = (self.z * 4 + (self.plane + 2) % 4, c)
        self.first = (jnp.where(c == 0, self.by_x[0], self.by_y[0]), c)
        self.second = (jnp.where(c == 0, self.by_y[0], self.by_x[0]), c)
        self.plane_x = self.by_x[0] % 4
        self.plane_y = self.by_y[0] % 4
        self.plane_first = jnp.where(c == 0, self.plane_x, self.plane_y)
        self.plane_second = jnp.where(c == 0, self.plane_y, self.plane_x)
        self.plane_both = 3 - self.plane

    def at_z(self, k):
        z = (self.z + k) % 4
        return z, (z * 4 + self.plane, self.c)

    def meet(self):
        barrier = pltpu.get_barrier_semaphore()
        partners = [self.other, self.by_x, self.by_y] + [self.at_z(k)[1] for k in (1, 2, 3)]
        for partner in partners:
            pl.semaphore_signal(barrier, inc=1, device_id=partner, device_id_type=MESH)
        pl.semaphore_wait(barrier, len(partners))


class Gather:
    sems = 31
    order = (0, 1, 3, 2)

    def __init__(self, spot, shards, wholes, send, recv, local):
        self.spot, self.shards, self.wholes = spot, shards, wholes
        self.send, self.recv, self.local = send, recv, local
        self.all = range(len(shards))

    def _columns(self, j):
        half = self.wholes[j].shape[3] // 2
        return pl.ds(pl.multiple_of(self.spot.c * half, 128), half)

    def _view(self, j, p, plane):
        return self.wholes[j].at[(self.spot.z + 4 - p) % 4, plane, :, self._columns(j)]

    def _copy(self, j, n, source, target, partner):
        return pltpu.make_async_remote_copy(
            source, target, self.send.at[j, n], self.recv.at[j, n], device_id=partner,
            device_id_type=MESH,
        )

    def _z(self, j, k):
        spot = self.spot
        source = self.shards[j].at[:, self._columns(j)]
        return self._copy(j, k - 1, source, self._view(j, 0, spot.plane), spot.at_z(k)[1])

    def _near(self, j, p, way):
        spot = self.spot
        view = self._view(j, p, spot.plane)
        source = view if p else self.shards[j].at[:, self._columns(j)]
        return self._copy(j, 3 + 2 * p + way, source, view, spot.by_y if way else spot.by_x)

    def _far(self, j, p):
        view = self._view(j, p, self.spot.plane_first)
        return self._copy(j, 11 + p, view, view, self.spot.second)

    def _swap(self, j, p, n):
        spot = self.spot
        plane = (spot.plane, spot.plane_x, spot.plane_y, spot.plane_both)[n]
        view = self._view(j, p, plane)
        return self._copy(j, 15 + 4 * p + n, view, view, spot.other)

    def _locals(self):
        return [
            pltpu.make_async_copy(
                self.shards[j], self.wholes[j].at[self.spot.z, self.spot.plane], self.local.at[j]
            )
            for j in self.all
        ]

    def start(self):
        for k in self.order[1:2]:
            for j in self.all:
                self._z(j, k).start()
        for j in self.all:
            for way in range(2):
                self._near(j, 0, way).start()
        for k in self.order[2:]:
            for j in self.all:
                self._z(j, k).start()
        for copy in self._locals():
            copy.start()

    def advance(self, i):
        if i < 4:
            p = self.order[i]
            for j in self.all:
                self._z(j, p).wait_recv()
                self._near(j, p, 0).start()
                self._near(j, p, 1).start()
                self._swap(j, p, 0).start()
        if 1 <= i < 5:
            p = self.order[i - 1]
            for j in self.all:
                self._near(j, p, 0).wait_recv()
                self._near(j, p, 1).wait_recv()
                self._far(j, p).start()
                self._swap(j, p, 1).start()
                self._swap(j, p, 2).start()
        if 2 <= i < 6:
            p = self.order[i - 2]
            for j in self.all:
                self._far(j, p).wait_recv()
                self._swap(j, p, 3).start()

    def finish(self):
        for copy in self._locals():
            copy.wait()
        for j in self.all:
            for p in self.order:
                if p:
                    self._z(j, p).wait_send()
                self._near(j, p, 0).wait_send()
                self._near(j, p, 1).wait_send()
                self._far(j, p).wait_send()
                for n in range(0 if p else 1, 4):
                    self._swap(j, p, n).wait()
class Reduce:
    sems = 21
    order = (2, 3, 1, 0)

    def __init__(self, spot, outs, give, mine, there, far, near, line, send, recv):
        self.spot, self.outs, self.give = spot, outs, give
        self.mine, self.there, self.far, self.near, self.line = mine, there, far, near, line
        self.send, self.recv = send, recv
        self.all = range(len(outs))

    @staticmethod
    def scratch(shapes, dtypes):
        def buffers(*lead):
            return [pltpu.VMEM((*lead, r, w // 2), d) for (r, w), d in zip(shapes, dtypes)]

        n = len(shapes)
        return (
            buffers(4, 4) + buffers(4, 4) + buffers(4, 4) + buffers(4) + buffers(4, 2) + buffers(4)
            + [pltpu.SemaphoreType.DMA((n, Reduce.sems))] * 2
        )

    @staticmethod
    def unpack(spot, outs, refs):
        n = len(outs)
        groups = [refs[i * n : (i + 1) * n] for i in range(6)]
        return Reduce(spot, outs, *groups, *refs[6 * n : 6 * n + 2])

    def part(self, js):
        def some(items):
            return [items[j] for j in js]

        lists = (self.outs, self.give, self.mine, self.there, self.far, self.near, self.line)
        chosen = Reduce(self.spot, *[some(items) for items in lists], self.send, self.recv)
        chosen.base = js[0]
        return chosen

    base = 0

    def put(self, j, core_of, value, columns=None, z_first=0):
        target = self.give[j] if core_of else self.mine[j]
        rows = target.shape[2]
        block = 4 * rows
        columns = slice(None) if columns is None else columns
        for i in range(value.shape[0] // block):
            p = (z_first + i + 4 - self.spot.z) % 4
            piece = value[i * block : (i + 1) * block]
            target[p, :, :, columns] = piece.reshape(4, rows, -1).astype(target.dtype)

    def _columns(self, j, core):
        half = self.outs[j].shape[1] // 2
        return pl.ds(pl.multiple_of(core * half, 128), half)

    def _copy(self, j, n, source, target, partner):
        return pltpu.make_async_remote_copy(
            source, target, self.send.at[self.base + j, n], self.recv.at[self.base + j, n],
            device_id=partner, device_id_type=MESH,
        )

    def _cross(self, j, p):
        return self._copy(j, p, self.give[j].at[p], self.there[j].at[p], self.spot.other)

    def _far(self, j, p):
        spot = self.spot
        return self._copy(
            j, 4 + p, self.mine[j].at[p, spot.plane_both], self.far[j].at[p], spot.first
        )

    def _near(self, j, p, way):
        spot = self.spot
        plane, partner = (spot.plane_y, spot.by_y) if way else (spot.plane_x, spot.by_x)
        return self._copy(
            j, 8 + 2 * p + way, self.mine[j].at[p, plane], self.near[j].at[p, way], partner
        )

    def _line(self, j, p):
        spot = self.spot
        return self._copy(
            j, 16 + p, self.mine[j].at[p, spot.plane], self.line[j].at[p], spot.at_z(p)[1]
        )

    def _last(self, j):
        view = self.outs[j].at[:, self._columns(j, self.spot.c)]
        return self._copy(j, 20, view, view, self.spot.other)

    def start(self, j):
        for p in self.order:
            self._cross(j, p).start()

    def _sum(self, j, p, plane, *others):
        total = self.mine[j][p, plane].astype(jnp.float32)
        total = total + self.there[j][p, plane].astype(jnp.float32)
        for other in others:
            total = total + other.astype(jnp.float32)
        return total

    def _store(self, j, p, plane, total):
        self.mine[j][p, plane] = total.astype(self.mine[j].dtype)

    def advance(self, i):
        spot = self.spot
        if i < 4:
            p = self.order[i]
            for j in self.all:
                self._cross(j, p).wait_recv()
                self._store(j, p, spot.plane_both, self._sum(j, p, spot.plane_both))
                self._far(j, p).start()
        if 0 <= i - 1 < 4:
            p = self.order[i - 1]
            for j in self.all:
                self._store(j, p, spot.plane_first, self._sum(j, p, spot.plane_first))
                self._far(j, p).wait_recv()
                self._store(
                    j, p, spot.plane_second, self._sum(j, p, spot.plane_second, self.far[j][p])
                )
                self._near(j, p, 0).start()
                self._near(j, p, 1).start()
        if 0 <= i - 2 < 4:
            p = self.order[i - 2]
            for j in self.all:
                self._near(j, p, 0).wait_recv()
                self._near(j, p, 1).wait_recv()
                total = self._sum(j, p, spot.plane, self.near[j][p, 0], self.near[j][p, 1])
                if p:
                    self._store(j, p, spot.plane, total)
                    self._line(j, p).start()
                else:
                    for k in (1, 2, 3):
                        self._line(j, k).wait_recv()
                        total = total + self.line[j][k].astype(jnp.float32)
                    self.outs[j][:, self._columns(j, spot.c)] = total
                    self._last(j).start()

    def finish(self):
        for j in self.all:
            for p in self.order:
                self._cross(j, p).wait_send()
                self._far(j, p).wait_send()
                self._near(j, p, 0).wait_send()
                self._near(j, p, 1).wait_send()
                if p:
                    self._line(j, p).wait_send()
            self._last(j).wait()


def gather_kernel(count, *refs):
    shards, wholes, sems = refs[:count], refs[count : 2 * count], refs[2 * count :]
    spot = Spot()
    spot.meet()
    gather = Gather(spot, shards, wholes, *sems)
    gather.start()
    for i in range(1, 6):
        gather.advance(i)
    gather.finish()


def reduce_kernel(count, *refs):
    factors, refs = refs[: 2 * count], refs[2 * count :]
    table, grad_one, wholes, refs = refs[0], refs[1], refs[2:7], refs[7:]
    outs, input_ref, memory_ref, refs = refs[: count + 1], refs[count + 1], refs[count + 2], refs[count + 3 :]
    wide, narrow, weight, total, sem, wide_sem, weight_sem = refs[-7:]
    spot = Spot()
    reduce = Reduce.unpack(spot, outs, refs[:-7])
    c = spot.c
    active, grad_outer, second, grad_inner = factors[:4]

    def load_pair(i):
        slot = 2 * (i % 3)
        return [
            pltpu.make_async_copy(factors[2 * i + n], narrow.at[slot + n], sem.at[slot + n])
            for n in range(2)
        ]

    def load_weight(i):
        return pltpu.make_async_copy(wholes[i], weight.at[i % 2], weight_sem.at[i % 2])

    early = [
        pltpu.make_async_copy(active, wide.at[0], wide_sem.at[0]),
        pltpu.make_async_copy(grad_outer, narrow.at[0], sem.at[0]),
        pltpu.make_async_copy(second, narrow.at[1], sem.at[1]),
        pltpu.make_async_copy(grad_inner, wide.at[1], wide_sem.at[1]),
    ]
    for copy in early:
        copy.start()
    for copy in load_pair(2):
        copy.start()
    spot.meet()
    for copy in early[:2]:
        copy.wait()
    width = grad_outer.shape[1]
    half = width // 2
    for core_of in (1, 0):
        start = pl.multiple_of((spot.c if core_of == 0 else 1 - spot.c) * half, 128)
        right = narrow[0, :, pl.ds(start, half)]
        for chunk in range(4):
            left = wide[0, :, chunk * width : (chunk + 1) * width]
            reduce.put(0, core_of, dense_grad(left, right), None, chunk)
        if core_of:
            reduce.start(0)
    for copy in early[2:]:
        copy.wait()
    for core_of in (1, 0):
        for chunk in range(4):
            base = (spot.c if core_of == 0 else 1 - spot.c) * 2 * width + chunk * half
            right = wide[1, :, pl.ds(pl.multiple_of(base, 128), half)]
            columns = slice(chunk * half, (chunk + 1) * half)
            reduce.put(1, core_of, dense_grad(narrow[1], right), columns)
        if core_of:
            reduce.start(1)
    first = reduce.part((0, 1))
    others = reduce.part(tuple(range(2, count + 1)))
    for copy in load_pair(3):
        copy.start()
    first.advance(0)

    for core_of in (1, 0):
        start = pl.multiple_of((spot.c if core_of == 0 else 1 - spot.c) * 128, 128)
        for z in range(4):
            p = (z + 4 - spot.z) % 4
            target = reduce.give[count] if core_of else reduce.mine[count]
            target[p] = table[z, :, :, pl.ds(start, 128)]
    reduce.start(count)
    for i in range(2, count):
        if i + 2 < count:
            for copy in load_pair(i + 2):
                copy.start()
        if i == 5:
            first.advance(1)
        for copy in load_pair(i):
            copy.wait()
        slot = 2 * (i % 3)
        left = narrow[slot].T
        for core_of in (1, 0):
            start = pl.multiple_of((spot.c if core_of == 0 else 1 - spot.c) * half, 128)
            right = narrow[slot + 1, :, pl.ds(start, half)]
            reduce.put(i, core_of, dense(left, right))
            if core_of:
                reduce.start(i)
    first.advance(2)
    others.advance(0)
    load_weight(0).start()
    load_weight(1).start()
    pairs = (count - 3, count - 2, count - 1, 4, 5)
    gone = pltpu.make_async_copy(grad_one, total, sem.at[6])
    gone.start()

    def load_right(i):
        return pltpu.make_async_copy(
            factors[2 * pairs[i] + 1], narrow.at[i % 2], sem.at[i % 2]
        )

    load_right(0).start()
    load_right(1).start()
    gone.wait()
    for i in range(5):
        load_weight(i).wait()
        load_right(i).wait()
        whole = weight[i % 2].reshape(width, width)
        product = dense_back(narrow[i % 2], whole)
        if i == 3:
            total[...] = product
        else:
            total[...] += product
        if i == 2:
            input_ref[...] = total[...].astype(jnp.bfloat16)
        if i == 4:
            memory_ref[...] = total[...].astype(jnp.bfloat16)
        if i + 2 < 5:
            load_weight(i + 2).start()
            load_right(i + 2).start()
        if i == 0:
            first.advance(3)
            others.advance(1)
        if i == 2:
            first.advance(4)
            others.advance(2)
    first.advance(5)
    others.advance(3)
    others.advance(4)
    others.advance(5)
    reduce.finish()


class Staged:
    staged = True

    def __init__(self):
        self.c = lax.axis_index("seq")
        self.parts = []

    def swap(self, array):
        pairs = [(f * 2 + c, f * 2 + 1 - c) for f in range(16) for c in range(2)]
        return lax.ppermute(array, ("fsdp", "seq"), pairs)

    def gather(self, shards, vectors):
        narrow = [v for v in vectors if v.shape[0] == 48]
        (wide,) = [v for v in vectors if v.shape[0] != 48]
        table = jnp.concatenate([jnp.stack(narrow), wide.reshape(-1, 48)]).astype(jnp.float32)
        table = jnp.pad(table, ((0, 24 - table.shape[0]), (0, 256 - 48)))
        shards = [*shards, table]
        count = len(shards)
        anywhere = pl.BlockSpec(memory_space=pl.ANY)
        *wholes, table = pl.pallas_call(
            functools.partial(gather_kernel, count),
            out_shape=[jax.ShapeDtypeStruct((4, 4) + s.shape, s.dtype) for s in shards],
            in_specs=[anywhere] * count,
            out_specs=[anywhere] * count,
            scratch_shapes=[
                pltpu.SemaphoreType.DMA((count, Gather.sems)),
                pltpu.SemaphoreType.DMA((count, Gather.sems)),
                pltpu.SemaphoreType.DMA((count,)),
            ],
            compiler_params=pltpu.CompilerParams(collective_id=0, has_side_effects=True),
        )(*shards)
        rows = len(narrow)
        table = table[:, :, :, :48].reshape(16, 24, 48)
        lines = table[:, :rows].transpose(1, 0, 2).reshape(rows, 768)
        wholes_1d, row = [], 0
        for v in vectors:
            if v.shape[0] == 48:
                wholes_1d.append(lines[row])
                row += 1
            else:
                wholes_1d.append(table[:, rows : rows + v.shape[0] // 48].reshape(-1))
        return [w.reshape(-1, w.shape[3]) for w in wholes], wholes_1d

    def reduce(self, products, vectors, grad_one, wholes):
        narrow = [v for v in vectors if v.shape[0] == 768]
        (wide,) = [v for v in vectors if v.shape[0] != 768]
        rows = len(narrow)
        table = jnp.concatenate(
            [
                jnp.stack(narrow).reshape(rows, 16, 48).transpose(1, 0, 2),
                wide.reshape(16, -1, 48),
            ],
            axis=1,
        )
        table = jnp.pad(table, ((0, 0), (0, 24 - table.shape[1]), (0, 256 - 48)))
        table = table.reshape(4, 4, 24, 256)
        count = len(products)
        shapes = [(left.shape[1] // 16, right.shape[1]) for left, right in products] + [(24, 256)]
        kinds = [jnp.bfloat16] * count + [jnp.float32]
        tokens, width = grad_one.shape
        anywhere, near = pl.BlockSpec(memory_space=pl.ANY), pl.BlockSpec(memory_space=pltpu.VMEM)
        *results, table, input_grad, memory_grad = pl.pallas_call(
            functools.partial(reduce_kernel, count),
            out_shape=[jax.ShapeDtypeStruct(s, jnp.float32) for s in shapes]
            + [jax.ShapeDtypeStruct((tokens, width), jnp.bfloat16)] * 2,
            in_specs=[anywhere] * (2 * count) + [near] + [anywhere] * 6,
            out_specs=[near] * (count + 3),
            scratch_shapes=Reduce.scratch(shapes, kinds)
            + [
                pltpu.VMEM((2, tokens, 4 * width), jnp.bfloat16),
                pltpu.VMEM((6, tokens, width), jnp.bfloat16),
                pltpu.VMEM((2, 4, 4, width // 16, width), jnp.bfloat16),
                pltpu.VMEM((tokens, width), jnp.float32),
                pltpu.SemaphoreType.DMA((7,)),
                pltpu.SemaphoreType.DMA((2,)),
                pltpu.SemaphoreType.DMA((2,)),
            ],
            compiler_params=pltpu.CompilerParams(
                collective_id=1, has_side_effects=True, vmem_limit_bytes=60 * 2**20
            ),
        )(
            *[factor for pair in products for factor in pair],
            table,
            grad_one,
            *[w.reshape(4, 4, -1, width) for w in wholes],
        )
        sums, row = [], 0
        for v in vectors:
            if v.shape[0] == 768:
                sums.append(table[row, :48])
                row += 1
            else:
                sums.append(table[rows : rows + v.shape[0] // 768, :48].reshape(-1))
        return results, sums, input_grad, memory_grad


    def gather_row(self, array):
        return jnp.concatenate([array, self.swap(array)], axis=1)

    def scatter_row(self, array):
        length = array.shape[1] // 2
        there = self.swap(array[:, length:].astype(jnp.bfloat16))
        return array[:, :length].astype(jnp.float32) + there.astype(jnp.float32)


class Plain:
    staged = False

    def gather(self, shards, vectors):
        results = [lax.all_gather(s, "fsdp", axis=0, tiled=True) for s in shards]
        return results, [
            lax.all_gather(v, "fsdp", axis=0, tiled=True).astype(jnp.float32) for v in vectors
        ]

    def _reduce(self, total):
        part = lax.psum_scatter(
            total.astype(jnp.bfloat16), "fsdp", scatter_dimension=0, tiled=True
        )
        return lax.psum(part, "seq").astype(jnp.float32)

    def reduce(self, products, vectors, grad_one, wholes):
        backs = [right for _, right in (*products[-3:], *products[4:6])]
        backs = [dense_back(right, whole) for right, whole in zip(backs, wholes)]
        return (
            [self._reduce(dense_grad(left, right)) for left, right in products],
            [self._reduce(v) for v in vectors],
            grad_one + backs[0] + backs[1] + backs[2],
            backs[3] + backs[4],
        )

    def gather_row(self, array):
        return lax.all_gather(array, "seq", axis=1, tiled=True)

    def places(self, length):
        return jnp.arange(length * lax.axis_size("seq"))

    def scatter_row(self, array):
        return lax.psum_scatter(
            array.astype(jnp.bfloat16), "seq", scatter_dimension=1, tiled=True
        ).astype(jnp.float32)


def query_marks(ids):
    lanes = jnp.arange(PAIR)[None, :] % HEAD_DIM
    return jnp.where((lanes < SEGMENTS) & (ids[:, None] != lanes), masked_score, 0.0).astype(
        jnp.bfloat16
    )


def key_marks_of(ids):
    lanes = jnp.arange(PAIR)[None, :] % HEAD_DIM
    ones = (lanes >= SEGMENTS) & (lanes < SEGMENTS + 3)
    return (ones | (ids[:, None] == lanes)).astype(jnp.bfloat16)


def against(left, right):
    return lax.dot_general(
        left, right, (((1,), (1,)), ((), ())), preferred_element_type=jnp.float32
    )


def three(value):
    high = value.astype(jnp.bfloat16).astype(jnp.float32)
    rest = value - high
    middle = rest.astype(jnp.bfloat16).astype(jnp.float32)
    return high, middle, rest - middle


def place_three(lanes, base, value, other):
    high, middle, small = three(value)
    first = base + SEGMENTS
    return jnp.where(
        lanes == first,
        high,
        jnp.where(lanes == first + 1, middle, jnp.where(lanes == first + 2, small, other)),
    )


def plan(length, causal, later):
    half = length // 2
    result = []
    for tile in range(2):
        if not causal:
            result.append([(0, 2 * length, False)])
            continue
        ranges = [(0, half, False)] if tile else []
        ranges.append((tile * half, half, True))
        if later:
            ranges.append((length + tile * half, length - tile * half, False))
        result.append(ranges)
    return result


def each_plan(core, length, causal, run):
    if not causal:
        run(plan(length, False, False))
        return
    for later in range(2):
        @pl.when(core == later)
        def _():
            run(plan(length, True, bool(later)))


def forward_kernel(causal, core_ref, q_ref, k_ref, v_ref, qm_ref, km_ref, mixed_ref, qx_ref):
    length = q_ref.shape[0]

    def run(tiles):
        for head in range(2):
            base = HEAD_DIM * (1 - head)

            def own(lanes):
                return (lanes < HEAD_DIM) if head == 0 else (lanes >= HEAD_DIM)

            for tile, ranges in enumerate(tiles):
                rows = slice(tile * TILE, tile * TILE + TILE)
                lanes = lax.broadcasted_iota(jnp.int32, (TILE, PAIR), 1)
                q = jnp.where(own(lanes), q_ref[rows, :], qm_ref[rows, :])
                scores = []
                for start, size, diagonal in ranges:
                    keys = slice(start, start + size)
                    key_lanes = lax.broadcasted_iota(jnp.int32, (size, PAIR), 1)
                    k = jnp.where(own(key_lanes), k_ref[keys, :], km_ref[keys, :])
                    s = against(q, k)
                    if diagonal:
                        i = lax.broadcasted_iota(jnp.int32, s.shape, 0)
                        j = lax.broadcasted_iota(jnp.int32, s.shape, 1)
                        s = jnp.where(j <= i, s, masked_score)
                    scores.append(s)
                highest = functools.reduce(
                    jnp.maximum, [jnp.max(s, axis=1, keepdims=True) for s in scores]
                )
                out = jnp.zeros((TILE, PAIR), jnp.float32)
                for s, (start, size, _) in zip(scores, ranges):
                    keys = slice(start, start + size)
                    key_lanes = lax.broadcasted_iota(jnp.int32, (size, PAIR), 1)
                    v = jnp.where(own(key_lanes), v_ref[keys, :], jnp.ones((), jnp.bfloat16))
                    e = jnp.exp(s - highest).astype(jnp.bfloat16)
                    out = out + jnp.dot(e, v, preferred_element_type=jnp.float32)
                total = pltpu.roll(out, HEAD_DIM, 1)
                mixed = (out / total).astype(jnp.bfloat16)
                if head:
                    mixed = jnp.where(own(lanes), mixed, mixed_ref[rows, :])
                mixed_ref[rows, :] = mixed
                logsum = highest + jnp.log(out)
                qx = place_three(lanes, base, -logsum, q.astype(jnp.float32))
                qx_ref[head, rows, :] = qx.astype(jnp.bfloat16)

    each_plan(core_ref[0], length, causal, run)


def attend(core, query, keys, values, q_marks, k_marks, causal):
    length, width = query.shape
    extent = keys.shape[0]
    pairs = width // PAIR
    column = lambda rows: pl.BlockSpec((rows, PAIR), lambda i, p: (0, i))
    fixed = lambda rows: pl.BlockSpec((rows, PAIR), lambda i, p: (0, 0))
    return pl.pallas_call(
        functools.partial(forward_kernel, causal),
        out_shape=[
            jax.ShapeDtypeStruct((length, width), jnp.bfloat16),
            jax.ShapeDtypeStruct((2 * pairs, length, PAIR), jnp.bfloat16),
        ],
        grid_spec=pltpu.PrefetchScalarGridSpec(
            num_scalar_prefetch=1,
            grid=(pairs,),
            in_specs=[column(length), column(extent), column(extent), fixed(length), fixed(extent)],
            out_specs=[column(length), pl.BlockSpec((2, length, PAIR), lambda i, p: (i, 0, 0))],
        ),
        compiler_params=pltpu.CompilerParams(vmem_limit_bytes=48 * 2**20),
        cost_estimate=pl.CostEstimate(
            flops=16 * length * extent * width, bytes_accessed=8 * extent * width, transcendentals=0
        ),
    )(core, query, keys, values, q_marks, k_marks)


def backward_kernel(
    causal, core_ref, qx_ref, k_ref, v_ref, e_ref, o_ref, km_ref, dq_ref, dk_ref, dv_ref, dk_acc, dv_acc, dq_acc
):
    length = e_ref.shape[0]
    scale = HEAD_DIM ** (-0.5)

    def run(tiles):
        dk_acc[...] = jnp.zeros_like(dk_acc)
        dv_acc[...] = jnp.zeros_like(dv_acc)
        for head in range(2):
            base = HEAD_DIM * (1 - head)

            def own(lanes):
                return (lanes < HEAD_DIM) if head == 0 else (lanes >= HEAD_DIM)

            for tile, ranges in enumerate(tiles):
                rows = slice(tile * TILE, tile * TILE + TILE)
                lanes = lax.broadcasted_iota(jnp.int32, (TILE, PAIR), 1)
                nothing = jnp.zeros((), jnp.bfloat16)
                qx = qx_ref[head, rows, :]
                q = jnp.where(own(lanes), qx, nothing)
                e = jnp.where(own(lanes), e_ref[rows, :], nothing)
                wide = e.astype(jnp.float32)
                delta = jnp.sum(wide * o_ref[rows, :].astype(jnp.float32), axis=1, keepdims=True)
                ex = place_three(lanes, base, -delta, wide).astype(jnp.bfloat16)
                dq = jnp.zeros((HEAD_DIM, TILE), jnp.float32)
                for start, size, diagonal in ranges:
                    keys = slice(start, start + size)
                    key_lanes = lax.broadcasted_iota(jnp.int32, (size, PAIR), 1)
                    k = jnp.where(own(key_lanes), k_ref[keys, :], km_ref[keys, :])
                    v = jnp.where(own(key_lanes), v_ref[keys, :], km_ref[keys, :])
                    p = jnp.exp(against(k, qx))
                    if diagonal:
                        j = lax.broadcasted_iota(jnp.int32, p.shape, 0)
                        i = lax.broadcasted_iota(jnp.int32, p.shape, 1)
                        p = jnp.where(j <= i, p, 0.0)
                    ds = (p * against(v, ex)).astype(jnp.bfloat16)
                    p = p.astype(jnp.bfloat16)
                    dv_acc[keys, :] += jnp.dot(p, e, preferred_element_type=jnp.float32)
                    dk_acc[keys, :] += jnp.dot(ds, q, preferred_element_type=jnp.float32)
                    kt = k_ref[keys, :].T[head * HEAD_DIM : (head + 1) * HEAD_DIM, :]
                    dq = dq + jnp.dot(kt, ds, preferred_element_type=jnp.float32)
                dq_acc[head * HEAD_DIM : (head + 1) * HEAD_DIM, rows] = dq
        dq_ref[...] = (dq_acc[...].T.astype(jnp.bfloat16) * jnp.bfloat16(scale)).astype(jnp.bfloat16)
        dk_ref[...] = dk_acc[...].astype(jnp.bfloat16)
        dv_ref[...] = dv_acc[...].astype(jnp.bfloat16)

    each_plan(core_ref[0], length, causal, run)


def attend_back(core, qx, keys, values, grad, mixed, k_marks, causal):
    length, width = grad.shape
    extent = keys.shape[0]
    pairs = width // PAIR
    column = lambda rows: pl.BlockSpec((rows, PAIR), lambda i, p: (0, i))
    fixed = lambda rows: pl.BlockSpec((rows, PAIR), lambda i, p: (0, 0))
    return pl.pallas_call(
        functools.partial(backward_kernel, causal),
        out_shape=[
            jax.ShapeDtypeStruct((length, width), jnp.bfloat16),
            jax.ShapeDtypeStruct((extent, width), jnp.bfloat16),
            jax.ShapeDtypeStruct((extent, width), jnp.bfloat16),
        ],
        grid_spec=pltpu.PrefetchScalarGridSpec(
            num_scalar_prefetch=1,
            grid=(pairs,),
            in_specs=[
                pl.BlockSpec((2, length, PAIR), lambda i, p: (i, 0, 0)),
                column(extent), column(extent), column(length), column(length), fixed(extent),
            ],
            out_specs=[column(length), column(extent), column(extent)],
            scratch_shapes=[
                pltpu.VMEM((extent, PAIR), jnp.float32),
                pltpu.VMEM((extent, PAIR), jnp.float32),
                pltpu.VMEM((PAIR, length), jnp.float32),
            ],
        ),
        compiler_params=pltpu.CompilerParams(vmem_limit_bytes=48 * 2**20),
        cost_estimate=pl.CostEstimate(
            flops=40 * length * extent * width, bytes_accessed=16 * extent * width, transcendentals=0
        ),
    )(core, qx, keys, values, grad, mixed, k_marks)


def head_slice(array, start, span):
    piece = lax.dynamic_slice_in_dim(array, start, span, 2)
    return piece.reshape(array.shape[0], array.shape[1], 2, span // 2)


def plain_attend(query, keys, values, allowed):
    rows, length, width = query.shape
    span = 2 * HEAD_DIM
    pairs = width // span

    def one_pair(index, carry):
        mixed, logsum = carry
        start = index * span
        query_part = head_slice(query, start, span)
        key_part = head_slice(keys, start, span)
        value_part = head_slice(values, start, span)
        scores = jnp.einsum(
            "rqhe,rkhe->rhqk", query_part, key_part, preferred_element_type=jnp.float32
        )
        scores = jnp.where(allowed[:, None], scores, masked_score)
        highest = jnp.max(scores, axis=-1, keepdims=True)
        exponent = jnp.exp(scores - highest)
        total = jnp.sum(exponent, axis=-1, keepdims=True)
        probs = (exponent / total).astype(jnp.bfloat16)
        part = jnp.einsum("rhqk,rkhe->rqhe", probs, value_part, preferred_element_type=jnp.float32)
        mixed = lax.dynamic_update_slice_in_dim(mixed, part.reshape(rows, length, span), start, 2)
        logsum = lax.dynamic_update_slice_in_dim(
            logsum, (highest + jnp.log(total))[None, :, :, :, 0], index, 0
        )
        return (mixed, logsum)

    mixed = jnp.zeros((rows, length, width), jnp.float32)
    logsum = jnp.zeros((pairs, rows, 2, length), jnp.float32)
    return lax.fori_loop(0, pairs, one_pair, (mixed, logsum))


def plain_attend_back(query, keys, values, allowed, logsum, grad_mixed):
    rows, length, width = query.shape
    extent = keys.shape[1]
    span = 2 * HEAD_DIM
    pairs = width // span

    def one_pair(index, carry):
        start = index * span
        query_part = head_slice(query, start, span)
        key_part = head_slice(keys, start, span)
        value_part = head_slice(values, start, span)
        grad_part = head_slice(grad_mixed, start, span)
        scores = jnp.einsum(
            "rqhe,rkhe->rhqk", query_part, key_part, preferred_element_type=jnp.float32
        )
        scores = jnp.where(allowed[:, None], scores, masked_score)
        pair_logsum = lax.dynamic_index_in_dim(logsum, index, 0, keepdims=False)
        probs = jnp.exp(scores - pair_logsum[..., None])
        prob_grad = jnp.einsum(
            "rqhe,rkhe->rhqk", grad_part, value_part, preferred_element_type=jnp.float32
        )
        row_total = jnp.sum(probs * prob_grad, axis=-1, keepdims=True)
        score_grad = (probs * (prob_grad - row_total)).astype(jnp.bfloat16)
        query_grad = jnp.einsum(
            "rhqk,rkhe->rqhe", score_grad, key_part, preferred_element_type=jnp.float32
        )
        grad_query = lax.dynamic_update_slice_in_dim(
            carry[0], query_grad.reshape(rows, length, span), start, 2
        )
        probs_low = probs.astype(jnp.bfloat16)
        value_grad = jnp.einsum(
            "rhqk,rqhe->rkhe", probs_low, grad_part, preferred_element_type=jnp.float32
        )
        key_grad = jnp.einsum(
            "rhqk,rqhe->rkhe", score_grad, query_part, preferred_element_type=jnp.float32
        )
        grad_keys = lax.dynamic_update_slice_in_dim(
            carry[1], key_grad.reshape(rows, extent, span), start, 2
        )
        grad_values = lax.dynamic_update_slice_in_dim(
            carry[2], value_grad.reshape(rows, extent, span), start, 2
        )
        return (grad_query, grad_keys, grad_values)

    start_query = jnp.zeros((rows, length, width), jnp.float32)
    start_keys = jnp.zeros((rows, extent, width), jnp.float32)
    return lax.fori_loop(0, pairs, one_pair, (start_query, start_keys, start_keys))


def attention(net, query, keys, values, target_ids, key_ids, causal):
    rows, length, width = query.shape
    if net.staged and rows == 1 and length == 2 * TILE:
        core = net.c.reshape(1)
        k_marks = key_marks_of(key_ids[0])
        q_marks = query_marks(target_ids[0])
        mixed, qx = attend(core, query[0], keys[0], values[0], q_marks, k_marks, causal)

        def back(grad):
            results = attend_back(core, qx, keys[0], values[0], grad, mixed, k_marks, causal)
            return [array[None] for array in results]

        return mixed, back
    allowed = target_ids[:, :, None] == key_ids[:, None, :]
    if causal:
        query_places = lax.axis_index("seq") * length + jnp.arange(length)
        allowed &= net.places(length)[None, None, :] <= query_places[None, :, None]
    mixed, logsum = plain_attend(query, keys, values, allowed)

    def plain_back(grad):
        query_sum, key_sum, value_sum = plain_attend_back(
            query, keys, values, allowed, logsum, grad.reshape(rows, length, width)
        )
        return [query_sum.astype(jnp.bfloat16) * HEAD_DIM ** (-0.5), key_sum, value_sum]

    return mixed.astype(jnp.bfloat16).reshape(rows * length, width), plain_back


def body(staged, hidden_in, memory, target_ids, memory_ids, out_grad, *weights):
    w = Weights(*weights)
    net = Staged() if staged else Plain()
    all_ = SimpleNamespace()
    (
        all_.self_query, all_.self_key, all_.self_value, all_.self_output, all_.cross_query,
        all_.cross_key, all_.cross_value, all_.cross_output, all_.inner_weight, all_.outer_weight,
    ), vectors = net.gather(
        [
            w.self_query, w.self_key, w.self_value, w.self_output, w.cross_query, w.cross_key,
            w.cross_value, w.cross_output, w.inner_weight, w.outer_weight,
        ],
        split_vectors(w),
    )
    (
        self_query_bias, self_value_bias, self_output_bias, first_gain, first_shift,
        cross_query_bias, cross_value_bias, cross_output_bias, second_gain, second_shift,
        inner_bias, outer_bias, third_gain, third_shift,
    ) = vectors

    rows, length, width = hidden_in.shape
    tokens = rows * length
    scale = HEAD_DIM ** (-0.5)
    flat_in = hidden_in.reshape(tokens, width)
    flat_memory = memory.reshape(tokens, width)

    def flat(array):
        return array.astype(jnp.bfloat16).reshape(tokens, width)

    def low(array):
        return array.astype(jnp.bfloat16).reshape(rows, length, width)

    row_ids, source_ids = net.gather_row(target_ids), net.gather_row(memory_ids)
    key_one = low(dense(flat_in, all_.self_key))
    value_one = low(dense(flat_in, all_.self_value) + self_value_bias)
    query_one = low((dense(flat_in, all_.self_query) + self_query_bias) * scale)
    keys_one, values_one = net.gather_row(key_one), net.gather_row(value_one)
    mixed_one, back_one = attention(
        net, query_one, keys_one, values_one, target_ids, row_ids, True
    )

    key_two = low(dense(flat_memory, all_.cross_key))
    value_two = low(dense(flat_memory, all_.cross_value) + cross_value_bias)
    keys_two, values_two = net.gather_row(key_two), net.gather_row(value_two)

    resid_one = (
        flat_in.astype(jnp.float32) + dense(mixed_one, all_.self_output) + self_output_bias
    )
    first, normed_one, inverse_one = layer_norm(resid_one, first_gain, first_shift)
    first = first.astype(jnp.bfloat16)
    query_two = low((dense(first, all_.cross_query) + cross_query_bias) * scale)
    mixed_two, back_two = attention(
        net, query_two, keys_two, values_two, target_ids, source_ids, False
    )
    resid_two = (
        first.astype(jnp.float32) + dense(mixed_two, all_.cross_output) + cross_output_bias
    )
    second, normed_two, inverse_two = layer_norm(resid_two, second_gain, second_shift)
    second = second.astype(jnp.bfloat16)
    inner = dense(second, all_.inner_weight) + inner_bias
    cumulative = 0.5 * (1.0 + lax.erf(inner * math.sqrt(0.5)))
    active = (inner * cumulative).astype(jnp.bfloat16)
    density = jnp.exp(-0.5 * inner * inner) * (1.0 / math.sqrt(2.0 * math.pi))
    slope = cumulative + inner * density
    resid_three = second.astype(jnp.float32) + dense(active, all_.outer_weight) + outer_bias
    final, normed_three, inverse_three = layer_norm(resid_three, third_gain, third_shift)
    layer_out = final.astype(jnp.bfloat16).reshape(rows, length, width)

    g, sums = SimpleNamespace(), SimpleNamespace()
    keep = (target_ids > 0).astype(jnp.float32).reshape(tokens, 1)
    upstream = out_grad.reshape(tokens, width).astype(jnp.float32) * keep
    grad_three, sums.third_gain, sums.third_shift = norm_back(
        upstream, normed_three, inverse_three, third_gain
    )
    grad_outer = grad_three.astype(jnp.bfloat16)
    sums.outer_bias = column_sum(grad_outer)
    grad_active = dense_back(grad_outer, all_.outer_weight)
    grad_inner = (grad_active * slope).astype(jnp.bfloat16)
    sums.inner_bias = column_sum(grad_inner)
    grad_second = grad_three + dense_back(grad_inner, all_.inner_weight)
    grad_two, sums.second_gain, sums.second_shift = norm_back(
        grad_second, normed_two, inverse_two, second_gain
    )
    branch_two = grad_two.astype(jnp.bfloat16)
    sums.cross_output_bias = column_sum(branch_two)
    query_grad_two, key_sum_two, value_sum_two = back_two(
        flat(dense_back(branch_two, all_.cross_output))
    )
    key_grad_two = flat(net.scatter_row(key_sum_two))
    value_grad_two = flat(net.scatter_row(value_sum_two))
    query_grad_two = flat(query_grad_two)
    sums.cross_query_bias = column_sum(query_grad_two)
    sums.cross_value_bias = column_sum(value_grad_two)
    grad_first = grad_two + dense_back(query_grad_two, all_.cross_query)
    grad_one, sums.first_gain, sums.first_shift = norm_back(
        grad_first, normed_one, inverse_one, first_gain
    )
    branch_one = grad_one.astype(jnp.bfloat16)
    sums.self_output_bias = column_sum(branch_one)
    query_grad_one, key_sum_one, value_sum_one = back_one(
        flat(dense_back(branch_one, all_.self_output))
    )
    key_grad_one = flat(net.scatter_row(key_sum_one))
    value_grad_one = flat(net.scatter_row(value_sum_one))
    query_grad_one = flat(query_grad_one)
    sums.self_query_bias = column_sum(query_grad_one)
    sums.self_value_bias = column_sum(value_grad_one)
    (
        g.outer_weight, g.inner_weight, g.cross_output, g.cross_query, g.cross_key, g.cross_value,
        g.self_output, g.self_query, g.self_key, g.self_value,
    ), (
        g.self_query_bias, g.self_value_bias, g.self_output_bias, g.first_gain, g.first_shift,
        g.cross_query_bias, g.cross_value_bias, g.cross_output_bias, g.second_gain,
        g.second_shift, g.inner_bias, g.outer_bias, g.third_gain, g.third_shift,
    ), input_grad, memory_grad = net.reduce(
        [
            (active, grad_outer), (second, grad_inner), (mixed_two, branch_two),
            (first, query_grad_two), (flat_memory, key_grad_two), (flat_memory, value_grad_two),
            (mixed_one, branch_one), (flat_in, query_grad_one), (flat_in, key_grad_one),
            (flat_in, value_grad_one),
        ],
        [
            sums.self_query_bias, sums.self_value_bias, sums.self_output_bias, sums.first_gain,
            sums.first_shift, sums.cross_query_bias, sums.cross_value_bias,
            sums.cross_output_bias, sums.second_gain, sums.second_shift, sums.inner_bias,
            sums.outer_bias, sums.third_gain, sums.third_shift,
        ],
        grad_one,
        [all_.self_query, all_.self_key, all_.self_value, all_.cross_key, all_.cross_value],
    )
    return (layer_out, low(input_grad), low(memory_grad), *Weights(**vars(g)))


def solution(mesh):
    staged = mesh.shape["fsdp"] == 16 and mesh.shape["seq"] == 2
    row, ids = P("fsdp", "seq", None), P("fsdp", "seq")
    matrix, vector = P("fsdp", None), P("fsdp")
    weights = Weights(
        matrix, vector, matrix, matrix, vector, matrix, vector, vector, vector, matrix, vector,
        matrix, matrix, vector, matrix, vector, vector, vector, matrix, vector, matrix, vector,
        vector, vector,
    )
    return jax.shard_map(
        functools.partial(body, staged),
        mesh=mesh,
        in_specs=(row, row, ids, ids, row, *weights),
        out_specs=(row, row, row, *weights),
        check_vma=False,
    )
```

```python
import functools
import math
from types import SimpleNamespace
from typing import NamedTuple

import jax
import jax.numpy as jnp
from jax import lax
from jax.experimental import pallas as pl
from jax.experimental.pallas import tpu as pltpu
from jax.sharding import PartitionSpec as P

HEAD_DIM = 64
PAIR = 2 * HEAD_DIM
SEGMENTS = 5
TILE = 256
eps_norm = 1e-05
masked_score = -1e30


class Weights(NamedTuple):
    self_query: jax.Array
    self_query_bias: jax.Array
    self_key: jax.Array
    self_value: jax.Array
    self_value_bias: jax.Array
    self_output: jax.Array
    self_output_bias: jax.Array
    first_gain: jax.Array
    first_shift: jax.Array
    cross_query: jax.Array
    cross_query_bias: jax.Array
    cross_key: jax.Array
    cross_value: jax.Array
    cross_value_bias: jax.Array
    cross_output: jax.Array
    cross_output_bias: jax.Array
    second_gain: jax.Array
    second_shift: jax.Array
    inner_weight: jax.Array
    inner_bias: jax.Array
    outer_weight: jax.Array
    outer_bias: jax.Array
    third_gain: jax.Array
    third_shift: jax.Array


def split_vectors(w):
    return [array for array in w if array.ndim == 1]


def dense(left, right):
    return jnp.dot(left, right, preferred_element_type=jnp.float32)


def dense_back(left, right):
    return lax.dot_general(
        left, right, (((1,), (1,)), ((), ())), preferred_element_type=jnp.float32
    )


def dense_grad(left, right):
    return lax.dot_general(
        left, right, (((0,), (0,)), ((), ())), preferred_element_type=jnp.float32
    )


def column_sum(values):
    return jnp.sum(values, axis=0, dtype=jnp.float32)


def layer_norm(resid, gain, shift):
    center = resid - jnp.mean(resid, axis=-1, keepdims=True)
    spread = jnp.mean(center * center, axis=-1, keepdims=True)
    inverse = lax.rsqrt(spread + eps_norm)
    normed = center * inverse
    return (normed * gain + shift, normed, inverse)


def norm_back(upstream, normed, inverse, gain):
    scaled = upstream * gain
    plain_mean = jnp.mean(scaled, axis=-1, keepdims=True)
    cross_mean = jnp.mean(scaled * normed, axis=-1, keepdims=True)
    result = inverse * (scaled - plain_mean - normed * cross_mean)
    return (result, jnp.sum(upstream * normed, axis=0), jnp.sum(upstream, axis=0))


MESH = pl.DeviceIdType.MESH


class Spot:
    def __init__(self):
        f, c = lax.axis_index("fsdp"), lax.axis_index("seq")
        self.c, self.z, self.plane = c, f // 4, f % 4
        self.other = (f, 1 - c)
        self.by_x = ((f // 2) * 2 + (1 - f % 2), c)
        self.by_y = (self.z * 4 + (self.plane + 2) % 4, c)
        self.first = (jnp.where(c == 0, self.by_x[0], self.by_y[0]), c)
        self.second = (jnp.where(c == 0, self.by_y[0], self.by_x[0]), c)
        self.plane_x = self.by_x[0] % 4
        self.plane_y = self.by_y[0] % 4
        self.plane_first = jnp.where(c == 0, self.plane_x, self.plane_y)
        self.plane_second = jnp.where(c == 0, self.plane_y, self.plane_x)
        self.plane_both = 3 - self.plane

    def at_z(self, k):
        z = (self.z + k) % 4
        return z, (z * 4 + self.plane, self.c)

    def meet(self):
        barrier = pltpu.get_barrier_semaphore()
        partners = [self.other, self.by_x, self.by_y] + [self.at_z(k)[1] for k in (1, 2, 3)]
        for partner in partners:
            pl.semaphore_signal(barrier, inc=1, device_id=partner, device_id_type=MESH)
        pl.semaphore_wait(barrier, len(partners))


class Gather:
    sems = 31
    order = (0, 1, 3, 2)

    def __init__(self, spot, shards, wholes, send, recv, local, base):
        self.spot, self.shards, self.wholes = spot, shards, wholes
        self.send, self.recv, self.local, self.base = send, recv, local, base
        self.all = range(len(shards))

    def _columns(self, j):
        half = self.wholes[j].shape[3] // 2
        return pl.ds(pl.multiple_of(self.spot.c * half, 128), half)

    def _view(self, j, p, plane):
        return self.wholes[j].at[(self.spot.z + 4 - p) % 4, plane, :, self._columns(j)]

    def _copy(self, j, n, source, target, partner):
        return pltpu.make_async_remote_copy(
            source, target, self.send.at[self.base + j, n], self.recv.at[self.base + j, n],
            device_id=partner, device_id_type=MESH,
        )

    def _z(self, j, k):
        spot = self.spot
        source = self.shards[j].at[:, self._columns(j)]
        return self._copy(j, k - 1, source, self._view(j, 0, spot.plane), spot.at_z(k)[1])

    def _near(self, j, p, way):
        spot = self.spot
        view = self._view(j, p, spot.plane)
        source = view if p else self.shards[j].at[:, self._columns(j)]
        return self._copy(j, 3 + 2 * p + way, source, view, spot.by_y if way else spot.by_x)

    def _far(self, j, p):
        view = self._view(j, p, self.spot.plane_first)
        return self._copy(j, 11 + p, view, view, self.spot.second)

    def _swap(self, j, p, n):
        spot = self.spot
        plane = (spot.plane, spot.plane_x, spot.plane_y, spot.plane_both)[n]
        view = self._view(j, p, plane)
        return self._copy(j, 15 + 4 * p + n, view, view, spot.other)

    def _locals(self):
        return [
            pltpu.make_async_copy(
                self.shards[j], self.wholes[j].at[self.spot.z, self.spot.plane],
                self.local.at[self.base + j],
            )
            for j in self.all
        ]

    def start(self):
        for k in self.order[1:2]:
            for j in self.all:
                self._z(j, k).start()
        for j in self.all:
            for way in range(2):
                self._near(j, 0, way).start()
        for k in self.order[2:]:
            for j in self.all:
                self._z(j, k).start()
        for copy in self._locals():
            copy.start()

    def advance(self, i):
        if i < 4:
            p = self.order[i]
            for j in self.all:
                self._z(j, p).wait_recv()
                self._near(j, p, 0).start()
                self._near(j, p, 1).start()
                self._swap(j, p, 0).start()
        if 1 <= i < 5:
            p = self.order[i - 1]
            for j in self.all:
                self._near(j, p, 0).wait_recv()
                self._near(j, p, 1).wait_recv()
                self._far(j, p).start()
                self._swap(j, p, 1).start()
                self._swap(j, p, 2).start()
        if 2 <= i < 6:
            p = self.order[i - 2]
            for j in self.all:
                self._far(j, p).wait_recv()
                self._swap(j, p, 3).start()

    def finish(self):
        for copy in self._locals():
            copy.wait()
        for j in self.all:
            for p in self.order:
                if p:
                    self._z(j, p).wait_send()
                self._near(j, p, 0).wait_send()
                self._near(j, p, 1).wait_send()
                self._far(j, p).wait_send()
                for n in range(0 if p else 1, 4):
                    self._swap(j, p, n).wait()
class Reduce:
    sems = 21
    order = (2, 3, 1, 0)

    def __init__(self, spot, outs, give, mine, there, far, near, line, send, recv):
        self.spot, self.outs, self.give = spot, outs, give
        self.mine, self.there, self.far, self.near, self.line = mine, there, far, near, line
        self.send, self.recv = send, recv
        self.all = range(len(outs))

    @staticmethod
    def scratch(shapes, dtypes):
        def buffers(*lead):
            return [pltpu.VMEM((*lead, r, w // 2), d) for (r, w), d in zip(shapes, dtypes)]

        n = len(shapes)
        return (
            buffers(4, 4) + buffers(4, 4) + buffers(4, 4) + buffers(4) + buffers(4, 2) + buffers(4)
            + [pltpu.SemaphoreType.DMA((n, Reduce.sems))] * 2
        )

    @staticmethod
    def unpack(spot, outs, refs):
        n = len(outs)
        groups = [refs[i * n : (i + 1) * n] for i in range(6)]
        return Reduce(spot, outs, *groups, *refs[6 * n : 6 * n + 2])

    def part(self, js):
        def some(items):
            return [items[j] for j in js]

        lists = (self.outs, self.give, self.mine, self.there, self.far, self.near, self.line)
        chosen = Reduce(self.spot, *[some(items) for items in lists], self.send, self.recv)
        chosen.base = js[0]
        return chosen

    base = 0

    def put(self, j, core_of, value, columns=None, z_first=0):
        target = self.give[j] if core_of else self.mine[j]
        rows = target.shape[2]
        block = 4 * rows
        columns = slice(None) if columns is None else columns
        for i in range(value.shape[0] // block):
            p = (z_first + i + 4 - self.spot.z) % 4
            piece = value[i * block : (i + 1) * block]
            target[p, :, :, columns] = piece.reshape(4, rows, -1).astype(target.dtype)

    def _columns(self, j, core):
        half = self.outs[j].shape[1] // 2
        return pl.ds(pl.multiple_of(core * half, 128), half)

    def _copy(self, j, n, source, target, partner):
        return pltpu.make_async_remote_copy(
            source, target, self.send.at[self.base + j, n], self.recv.at[self.base + j, n],
            device_id=partner, device_id_type=MESH,
        )

    def _cross(self, j, p):
        return self._copy(j, p, self.give[j].at[p], self.there[j].at[p], self.spot.other)

    def _far(self, j, p):
        spot = self.spot
        return self._copy(
            j, 4 + p, self.mine[j].at[p, spot.plane_both], self.far[j].at[p], spot.first
        )

    def _near(self, j, p, way):
        spot = self.spot
        plane, partner = (spot.plane_y, spot.by_y) if way else (spot.plane_x, spot.by_x)
        return self._copy(
            j, 8 + 2 * p + way, self.mine[j].at[p, plane], self.near[j].at[p, way], partner
        )

    def _line(self, j, p):
        spot = self.spot
        return self._copy(
            j, 16 + p, self.mine[j].at[p, spot.plane], self.line[j].at[p], spot.at_z(p)[1]
        )

    def _last(self, j):
        view = self.outs[j].at[:, self._columns(j, self.spot.c)]
        return self._copy(j, 20, view, view, self.spot.other)

    def start(self, j):
        for p in self.order:
            self._cross(j, p).start()

    def _sum(self, j, p, plane, *others):
        total = self.mine[j][p, plane].astype(jnp.float32)
        total = total + self.there[j][p, plane].astype(jnp.float32)
        for other in others:
            total = total + other.astype(jnp.float32)
        return total

    def _store(self, j, p, plane, total):
        self.mine[j][p, plane] = total.astype(self.mine[j].dtype)

    def advance(self, i):
        spot = self.spot
        if i < 4:
            p = self.order[i]
            for j in self.all:
                self._cross(j, p).wait_recv()
                self._store(j, p, spot.plane_both, self._sum(j, p, spot.plane_both))
                self._far(j, p).start()
        if 0 <= i - 1 < 4:
            p = self.order[i - 1]
            for j in self.all:
                self._store(j, p, spot.plane_first, self._sum(j, p, spot.plane_first))
                self._far(j, p).wait_recv()
                self._store(
                    j, p, spot.plane_second, self._sum(j, p, spot.plane_second, self.far[j][p])
                )
                self._near(j, p, 0).start()
                self._near(j, p, 1).start()
        if 0 <= i - 2 < 4:
            p = self.order[i - 2]
            for j in self.all:
                self._near(j, p, 0).wait_recv()
                self._near(j, p, 1).wait_recv()
                total = self._sum(j, p, spot.plane, self.near[j][p, 0], self.near[j][p, 1])
                if p:
                    self._store(j, p, spot.plane, total)
                    self._line(j, p).start()
                else:
                    for k in (1, 2, 3):
                        self._line(j, k).wait_recv()
                        total = total + self.line[j][k].astype(jnp.float32)
                    self.outs[j][:, self._columns(j, spot.c)] = total
                    self._last(j).start()

    def finish(self):
        for j in self.all:
            for p in self.order:
                self._cross(j, p).wait_send()
                self._far(j, p).wait_send()
                self._near(j, p, 0).wait_send()
                self._near(j, p, 1).wait_send()
                if p:
                    self._line(j, p).wait_send()
            self._last(j).wait()


def gather_kernel(groups, *refs):
    counts = [len(group) for group in groups]
    count = sum(counts)
    shards, (x_ref, memory_ref, qm_ref, own_km_one, own_km_two), refs = (
        refs[:count], refs[count : count + 5], refs[count + 5 :],
    )
    wholes, lines_ref, results, refs = (
        refs[:count], refs[count], refs[count + 1 : count + 17], refs[count + 17 :],
    )
    kept, refs = refs[:16], refs[16:]
    (
        mixed_one, qx_one, first, normed_one, inverse_one, mixed_two, qx_two, second, normed_two,
        inverse_two, k_one, v_one, k_two, v_two, km_one, km_two,
    ) = kept
    query, weight, table, send, recv, local, weight_sem, send_row, recv_row, out_sem = refs
    spot = Spot()
    length, width = x_ref.shape
    scale = HEAD_DIM ** (-0.5)
    gathers, start = [], 0
    for n in counts:
        chosen = slice(start, start + n)
        gathers.append(Gather(spot, shards[chosen], wholes[chosen], send, recv, local, start))
        start += n
    one, two, three_ = gathers

    def fetch(i):
        return pltpu.make_async_copy(wholes[i], weight.at[i if i < 3 else i - 1], weight_sem.at[i])

    def matrix(i):
        return weight[i if i < 3 else i - 1].reshape(width, width)

    def line(i):
        return lines_ref[i : i + 1, :]

    def cross(i, ref):
        return pltpu.make_async_remote_copy(
            ref.at[pl.ds(0, length)], ref.at[pl.ds(length, length)], send_row.at[i],
            recv_row.at[i], device_id=spot.other, device_id_type=MESH,
        )

    def leave(i):
        return pltpu.make_async_copy(kept[i], results[i], out_sem.at[i])

    def norm(total, gain, shift, low, normed, inverse):
        center = total - jnp.mean(total, axis=-1, keepdims=True)
        spread = jnp.mean(center * center, axis=-1, keepdims=True)
        factor = lax.rsqrt(spread + eps_norm)
        unit = center * factor
        normed[...] = unit
        inverse[...] = jnp.broadcast_to(factor, inverse.shape)
        low[...] = (unit * gain + shift).astype(jnp.bfloat16)

    def pairs(first_pair, last_pair, causal, k, v, km, mixed, qx):
        def one_pair(i, carry):
            columns = pl.ds(pl.multiple_of(i * PAIR, PAIR), PAIR)
            forward_pair(
                spot.c, causal, query.at[:, columns], k.at[:, columns], v.at[:, columns], qm_ref,
                km, mixed.at[:, columns], qx.at[pl.ds(2 * i, 2)],
            )
            return carry

        lax.fori_loop(first_pair, last_pair, one_pair, 0)

    spot.meet()
    one.start()
    two.start()
    km_one[0:length, :] = own_km_one[...]
    km_two[0:length, :] = own_km_two[...]
    marks = [cross(0, km_one), cross(1, km_two)]
    for copy in marks:
        copy.start()
    one.advance(1)
    one.advance(2)
    one.advance(3)
    one.advance(4)
    one.advance(5)
    one.finish()
    three_.start()
    for i in range(3):
        fetch(i).start()
    vector_copy = pltpu.make_async_copy(wholes[3], table, weight_sem.at[3])
    vector_copy.start()
    vector_copy.wait()
    lines = jnp.zeros(lines_ref.shape, jnp.float32)
    for f in range(16):
        i = lax.broadcasted_iota(jnp.int32, (128, width), 0)
        j = lax.broadcasted_iota(jnp.int32, (128, width), 1)
        at = ((i < 48) & (j == i + 48 * f)).astype(jnp.bfloat16)
        piece = table[f // 4, f % 4, :, 0:128].astype(jnp.bfloat16)
        lines = lines + dense(piece, at)
    lines_ref[...] = lines

    fetch(0).wait()
    fetch(1).wait()
    fetch(2).wait()
    k_one[0:length, :] = dense(x_ref[...], matrix(1)).astype(jnp.bfloat16)
    row_one = [cross(2, k_one), cross(3, v_one)]
    row_one[0].start()
    v_one[0:length, :] = (dense(x_ref[...], matrix(2)) + line(1)).astype(jnp.bfloat16)
    row_one[1].start()
    query[...] = ((dense(x_ref[...], matrix(0)) + line(0)) * scale).astype(jnp.bfloat16)
    two.advance(1)
    for copy in marks:
        copy.wait()
    for copy in row_one:
        copy.wait()
    leaving = [leave(i) for i in (10, 11, 14, 15)]
    for copy in leaving:
        copy.start()
    pairs(0, 3, True, k_one, v_one, km_one, mixed_one, qx_one)
    two.advance(2)
    pairs(3, 6, True, k_one, v_one, km_one, mixed_one, qx_one)
    for i in (0, 1):
        leaving.append(leave(i))
        leaving[-1].start()
    two.advance(3)
    two.advance(4)
    two.advance(5)
    two.finish()
    for i in range(4, 9):
        fetch(i).start()
    fetch(4).wait()
    k_two[0:length, :] = dense(memory_ref[...], matrix(4)).astype(jnp.bfloat16)
    row_two = [cross(4, k_two), cross(5, v_two)]
    row_two[0].start()
    fetch(5).wait()
    v_two[0:length, :] = (dense(memory_ref[...], matrix(5)) + line(6)).astype(jnp.bfloat16)
    row_two[1].start()
    fetch(6).wait()
    total = x_ref[...].astype(jnp.float32) + dense(mixed_one[...], matrix(6)) + line(2)
    norm(total, line(3), line(4), first, normed_one, inverse_one)
    fetch(7).wait()
    query[...] = ((dense(first[...], matrix(7)) + line(5)) * scale).astype(jnp.bfloat16)
    three_.advance(1)
    for copy in row_two:
        copy.wait()
    for i in (2, 3, 4, 12, 13):
        leaving.append(leave(i))
        leaving[-1].start()
    pairs(0, 3, False, k_two, v_two, km_two, mixed_two, qx_two)
    three_.advance(2)
    pairs(3, 6, False, k_two, v_two, km_two, mixed_two, qx_two)
    three_.advance(3)
    fetch(8).wait()
    total = first[...].astype(jnp.float32) + dense(mixed_two[...], matrix(8)) + line(7)
    norm(total, line(8), line(9), second, normed_two, inverse_two)
    for i in (5, 6, 7, 8, 9):
        leaving.append(leave(i))
        leaving[-1].start()
    three_.advance(4)
    three_.advance(5)
    three_.finish()
    for copy in leaving:
        copy.wait()


def reduce_kernel(count, *refs):
    factors, refs = refs[: 2 * count], refs[2 * count :]
    table, grad_one, wholes, refs = refs[0], refs[1], refs[2:7], refs[7:]
    outs, input_ref, memory_ref, refs = refs[: count + 1], refs[count + 1], refs[count + 2], refs[count + 3 :]
    wide, narrow, weight, total, sem, wide_sem, weight_sem = refs[-7:]
    spot = Spot()
    reduce = Reduce.unpack(spot, outs, refs[:-7])
    c = spot.c
    active, grad_outer, second, grad_inner = factors[:4]

    def load_pair(i):
        slot = 2 * (i % 3)
        return [
            pltpu.make_async_copy(factors[2 * i + n], narrow.at[slot + n], sem.at[slot + n])
            for n in range(2)
        ]

    def load_weight(i):
        return pltpu.make_async_copy(wholes[i], weight.at[i % 2], weight_sem.at[i % 2])

    early = [
        pltpu.make_async_copy(active, wide.at[0], wide_sem.at[0]),
        pltpu.make_async_copy(grad_outer, narrow.at[0], sem.at[0]),
        pltpu.make_async_copy(second, narrow.at[1], sem.at[1]),
        pltpu.make_async_copy(grad_inner, wide.at[1], wide_sem.at[1]),
    ]
    for copy in early:
        copy.start()
    for copy in load_pair(2):
        copy.start()
    spot.meet()
    for copy in early[:2]:
        copy.wait()
    width = grad_outer.shape[1]
    half = width // 2
    for core_of in (1, 0):
        start = pl.multiple_of((spot.c if core_of == 0 else 1 - spot.c) * half, 128)
        right = narrow[0, :, pl.ds(start, half)]
        for chunk in range(4):
            left = wide[0, :, chunk * width : (chunk + 1) * width]
            reduce.put(0, core_of, dense_grad(left, right), None, chunk)
        if core_of:
            reduce.start(0)
    for copy in early[2:]:
        copy.wait()
    for core_of in (1, 0):
        for chunk in range(4):
            base = (spot.c if core_of == 0 else 1 - spot.c) * 2 * width + chunk * half
            right = wide[1, :, pl.ds(pl.multiple_of(base, 128), half)]
            columns = slice(chunk * half, (chunk + 1) * half)
            reduce.put(1, core_of, dense_grad(narrow[1], right), columns)
        if core_of:
            reduce.start(1)
    first = reduce.part((0, 1))
    others = reduce.part(tuple(range(2, count + 1)))
    for copy in load_pair(3):
        copy.start()
    first.advance(0)

    for core_of in (1, 0):
        start = pl.multiple_of((spot.c if core_of == 0 else 1 - spot.c) * 128, 128)
        for z in range(4):
            p = (z + 4 - spot.z) % 4
            target = reduce.give[count] if core_of else reduce.mine[count]
            target[p] = table[z, :, :, pl.ds(start, 128)]
    reduce.start(count)
    for i in range(2, count):
        if i + 2 < count:
            for copy in load_pair(i + 2):
                copy.start()
        if i == 5:
            first.advance(1)
        for copy in load_pair(i):
            copy.wait()
        slot = 2 * (i % 3)
        left = narrow[slot].T
        for core_of in (1, 0):
            start = pl.multiple_of((spot.c if core_of == 0 else 1 - spot.c) * half, 128)
            right = narrow[slot + 1, :, pl.ds(start, half)]
            reduce.put(i, core_of, dense(left, right))
            if core_of:
                reduce.start(i)
    first.advance(2)
    others.advance(0)
    load_weight(0).start()
    load_weight(1).start()
    pairs = (count - 3, count - 2, count - 1, 4, 5)
    gone = pltpu.make_async_copy(grad_one, total, sem.at[6])
    gone.start()

    def load_right(i):
        return pltpu.make_async_copy(
            factors[2 * pairs[i] + 1], narrow.at[i % 2], sem.at[i % 2]
        )

    load_right(0).start()
    load_right(1).start()
    gone.wait()
    for i in range(5):
        load_weight(i).wait()
        load_right(i).wait()
        whole = weight[i % 2].reshape(width, width)
        product = dense_back(narrow[i % 2], whole)
        if i == 3:
            total[...] = product
        else:
            total[...] += product
        if i == 2:
            input_ref[...] = total[...].astype(jnp.bfloat16)
        if i == 4:
            memory_ref[...] = total[...].astype(jnp.bfloat16)
        if i + 2 < 5:
            load_weight(i + 2).start()
            load_right(i + 2).start()
        if i == 0:
            first.advance(3)
            others.advance(1)
        if i == 2:
            first.advance(4)
            others.advance(2)
    first.advance(5)
    others.advance(3)
    others.advance(4)
    others.advance(5)
    reduce.finish()


class Staged:
    staged = True

    def __init__(self):
        self.c = lax.axis_index("seq")
        self.parts = []

    def swap(self, array):
        pairs = [(f * 2 + c, f * 2 + 1 - c) for f in range(16) for c in range(2)]
        return lax.ppermute(array, ("fsdp", "seq"), pairs)

    def front(self, w, all_, hidden, memory, target_ids, memory_ids):
        vectors = split_vectors(w)
        narrow = [v for v in vectors if v.shape[0] == 48]
        (wide,) = [v for v in vectors if v.shape[0] != 48]
        table = jnp.concatenate([jnp.stack(narrow), wide.reshape(-1, 48)]).astype(jnp.float32)
        table = jnp.pad(table, ((0, 24 - table.shape[0]), (0, 256 - 48)))
        groups = (
            (w.self_query, w.self_key, w.self_value, table),
            (w.cross_key, w.cross_value, w.self_output, w.cross_query, w.cross_output),
            (w.inner_weight, w.outer_weight),
        )
        shards = [array for group in groups for array in group]
        count, (length, width) = len(shards), hidden.shape
        pairs = width // PAIR
        low, full = jnp.bfloat16, jnp.float32
        some = [
            ((length, width), low), ((2 * pairs, length, PAIR), low), ((length, width), low),
            ((length, width), full), ((length, 128), full),
        ]
        kept = some + some + [((2 * length, width), low)] * 4 + [((2 * length, PAIR), low)] * 2
        anywhere, near = pl.BlockSpec(memory_space=pl.ANY), pl.BlockSpec(memory_space=pltpu.VMEM)
        results = pl.pallas_call(
            functools.partial(gather_kernel, groups),
            out_shape=[jax.ShapeDtypeStruct((4, 4) + s.shape, s.dtype) for s in shards]
            + [jax.ShapeDtypeStruct((24, width), full)]
            + [jax.ShapeDtypeStruct(*k) for k in kept],
            in_specs=[anywhere] * count + [near] * 5,
            out_specs=[anywhere] * count + [near] + [anywhere] * len(kept),
            scratch_shapes=[pltpu.VMEM(*k) for k in kept]
            + [
                pltpu.VMEM((length, width), low),
                pltpu.VMEM((8, 4, 4, width // 16, width), low),
                pltpu.VMEM((4, 4, 24, 256), full),
                pltpu.SemaphoreType.DMA((count, Gather.sems)),
                pltpu.SemaphoreType.DMA((count, Gather.sems)),
                pltpu.SemaphoreType.DMA((count,)),
                pltpu.SemaphoreType.DMA((9,)),
                pltpu.SemaphoreType.DMA((6,)),
                pltpu.SemaphoreType.DMA((6,)),
                pltpu.SemaphoreType.DMA((16,)),
            ],
            compiler_params=pltpu.CompilerParams(
                collective_id=0, has_side_effects=True, vmem_limit_bytes=60 * 2**20
            ),
        )(
            *shards, hidden, memory, query_marks(target_ids[0]), key_marks_of(target_ids[0]),
            key_marks_of(memory_ids[0]),
        )
        wholes, lines, results = results[:count], results[count], results[count + 1 :]
        table = wholes[3]
        flats = [array.reshape(-1, array.shape[3]) for array in wholes]
        (
            all_.self_query, all_.self_key, all_.self_value, _, all_.cross_key, all_.cross_value,
            all_.self_output, all_.cross_query, all_.cross_output, all_.inner_weight,
            all_.outer_weight,
        ) = flats
        rows = len(narrow)
        bias = table[:, :, rows : rows + wide.shape[0] // 48, :48].reshape(-1)
        gathered, row = [], 0
        for v in vectors:
            if v.shape[0] == 48:
                gathered.append(lines[row])
                row += 1
            else:
                gathered.append(bias)
        (
            mixed_one, qx_one, first, normed_one, inverse_one, mixed_two, qx_two, second,
            normed_two, inverse_two, k_one, v_one, k_two, v_two, km_one, km_two,
        ) = results
        core = self.c.reshape(1)

        def back_one(grad):
            return attend_back(core, qx_one, k_one, v_one, grad, mixed_one, km_one, True)

        def back_two(grad):
            return attend_back(core, qx_two, k_two, v_two, grad, mixed_two, km_two, False)

        return (
            gathered, mixed_one, first, normed_one, inverse_one[:, :1], back_one, mixed_two,
            second, normed_two, inverse_two[:, :1], back_two,
        )

    def reduce(self, products, vectors, grad_one, wholes):
        narrow = [v for v in vectors if v.shape[0] == 768]
        (wide,) = [v for v in vectors if v.shape[0] != 768]
        rows = len(narrow)
        table = jnp.concatenate(
            [
                jnp.stack(narrow).reshape(rows, 16, 48).transpose(1, 0, 2),
                wide.reshape(16, -1, 48),
            ],
            axis=1,
        )
        table = jnp.pad(table, ((0, 0), (0, 24 - table.shape[1]), (0, 256 - 48)))
        table = table.reshape(4, 4, 24, 256)
        count = len(products)
        shapes = [(left.shape[1] // 16, right.shape[1]) for left, right in products] + [(24, 256)]
        kinds = [jnp.bfloat16] * count + [jnp.float32]
        tokens, width = grad_one.shape
        anywhere, near = pl.BlockSpec(memory_space=pl.ANY), pl.BlockSpec(memory_space=pltpu.VMEM)
        *results, table, input_grad, memory_grad = pl.pallas_call(
            functools.partial(reduce_kernel, count),
            out_shape=[jax.ShapeDtypeStruct(s, jnp.float32) for s in shapes]
            + [jax.ShapeDtypeStruct((tokens, width), jnp.bfloat16)] * 2,
            in_specs=[anywhere] * (2 * count) + [near] + [anywhere] * 6,
            out_specs=[near] * (count + 3),
            scratch_shapes=Reduce.scratch(shapes, kinds)
            + [
                pltpu.VMEM((2, tokens, 4 * width), jnp.bfloat16),
                pltpu.VMEM((6, tokens, width), jnp.bfloat16),
                pltpu.VMEM((2, 4, 4, width // 16, width), jnp.bfloat16),
                pltpu.VMEM((tokens, width), jnp.float32),
                pltpu.SemaphoreType.DMA((7,)),
                pltpu.SemaphoreType.DMA((2,)),
                pltpu.SemaphoreType.DMA((2,)),
            ],
            compiler_params=pltpu.CompilerParams(
                collective_id=1, has_side_effects=True, vmem_limit_bytes=60 * 2**20
            ),
        )(
            *[factor for pair in products for factor in pair],
            table,
            grad_one,
            *[w.reshape(4, 4, -1, width) for w in wholes],
        )
        sums, row = [], 0
        for v in vectors:
            if v.shape[0] == 768:
                sums.append(table[row, :48])
                row += 1
            else:
                sums.append(table[rows : rows + v.shape[0] // 768, :48].reshape(-1))
        return results, sums, input_grad, memory_grad


    def scatter_row(self, array):
        length = array.shape[0] // 2
        there = self.swap(array[length:])
        return array[:length].astype(jnp.float32) + there.astype(jnp.float32)


class Plain:
    staged = False

    def front(self, w, all_, hidden, memory, target_ids, memory_ids):
        def whole(array):
            return lax.all_gather(array, "fsdp", axis=0, tiled=True)

        all_.__dict__.update(Weights(*map(whole, w))._asdict())
        vectors = [array.astype(jnp.float32) for array in split_vectors(Weights(**vars(all_)))]
        (
            self_query_bias, self_value_bias, self_output_bias, first_gain, first_shift,
            cross_query_bias, cross_value_bias, cross_output_bias, second_gain, second_shift,
            *_,
        ) = vectors
        rows, length = target_ids.shape
        width = hidden.shape[1]
        scale = HEAD_DIM ** (-0.5)

        def low(array):
            return array.astype(jnp.bfloat16).reshape(rows, length, width)

        row_ids, source_ids = self.gather_row(target_ids), self.gather_row(memory_ids)
        query_places = lax.axis_index("seq") * length + jnp.arange(length)
        key_places = jnp.arange(row_ids.shape[1])
        allowed_self = (target_ids[:, :, None] == row_ids[:, None, :]) & (
            key_places[None, None, :] <= query_places[None, :, None]
        )
        allowed_cross = target_ids[:, :, None] == source_ids[:, None, :]

        def attention(query, keys, values, allowed):
            mixed, logsum = plain_attend(query, keys, values, allowed)

            def back(grad):
                query_sum, key_sum, value_sum = plain_attend_back(
                    query, keys, values, allowed, logsum, grad.reshape(rows, length, width)
                )
                return query_sum.astype(jnp.bfloat16) * scale, key_sum, value_sum

            return mixed.astype(jnp.bfloat16).reshape(rows * length, width), back

        key_one = self.gather_row(low(dense(hidden, all_.self_key)))
        value_one = self.gather_row(low(dense(hidden, all_.self_value) + self_value_bias))
        query_one = low((dense(hidden, all_.self_query) + self_query_bias) * scale)
        mixed_one, back_one = attention(query_one, key_one, value_one, allowed_self)
        key_two = self.gather_row(low(dense(memory, all_.cross_key)))
        value_two = self.gather_row(low(dense(memory, all_.cross_value) + cross_value_bias))
        resid_one = (
            hidden.astype(jnp.float32) + dense(mixed_one, all_.self_output) + self_output_bias
        )
        first, normed_one, inverse_one = layer_norm(resid_one, first_gain, first_shift)
        first = first.astype(jnp.bfloat16)
        query_two = low((dense(first, all_.cross_query) + cross_query_bias) * scale)
        mixed_two, back_two = attention(query_two, key_two, value_two, allowed_cross)
        resid_two = (
            first.astype(jnp.float32) + dense(mixed_two, all_.cross_output) + cross_output_bias
        )
        second, normed_two, inverse_two = layer_norm(resid_two, second_gain, second_shift)
        return (
            vectors, mixed_one, first, normed_one, inverse_one, back_one, mixed_two,
            second.astype(jnp.bfloat16), normed_two, inverse_two, back_two,
        )

    def _reduce(self, total):
        part = lax.psum_scatter(
            total.astype(jnp.bfloat16), "fsdp", scatter_dimension=0, tiled=True
        )
        return lax.psum(part, "seq").astype(jnp.float32)

    def reduce(self, products, vectors, grad_one, wholes):
        backs = [right for _, right in (*products[-3:], *products[4:6])]
        backs = [dense_back(right, whole) for right, whole in zip(backs, wholes)]
        return (
            [self._reduce(dense_grad(left, right)) for left, right in products],
            [self._reduce(v) for v in vectors],
            grad_one + backs[0] + backs[1] + backs[2],
            backs[3] + backs[4],
        )

    def gather_row(self, array):
        return lax.all_gather(array, "seq", axis=1, tiled=True)

    def scatter_row(self, array):
        return lax.psum_scatter(
            array.astype(jnp.bfloat16), "seq", scatter_dimension=1, tiled=True
        ).astype(jnp.float32)


def query_marks(ids):
    lanes = jnp.arange(PAIR)[None, :] % HEAD_DIM
    return jnp.where((lanes < SEGMENTS) & (ids[:, None] != lanes), masked_score, 0.0).astype(
        jnp.bfloat16
    )


def key_marks_of(ids):
    lanes = jnp.arange(PAIR)[None, :] % HEAD_DIM
    ones = (lanes >= SEGMENTS) & (lanes < SEGMENTS + 3)
    return (ones | (ids[:, None] == lanes)).astype(jnp.bfloat16)


def against(left, right):
    return lax.dot_general(
        left, right, (((1,), (1,)), ((), ())), preferred_element_type=jnp.float32
    )


def three(value):
    high = value.astype(jnp.bfloat16).astype(jnp.float32)
    rest = value - high
    middle = rest.astype(jnp.bfloat16).astype(jnp.float32)
    return high, middle, rest - middle


def place_three(lanes, base, value, other):
    high, middle, small = three(value)
    first = base + SEGMENTS
    return jnp.where(
        lanes == first,
        high,
        jnp.where(lanes == first + 1, middle, jnp.where(lanes == first + 2, small, other)),
    )


def plan(length, causal, later):
    half = length // 2
    result = []
    for tile in range(2):
        if not causal:
            result.append([(0, 2 * length, False)])
            continue
        ranges = [(0, half, False)] if tile else []
        ranges.append((tile * half, half, True))
        if later:
            ranges.append((length + tile * half, length - tile * half, False))
        result.append(ranges)
    return result


def each_plan(core, length, causal, run):
    if not causal:
        run(plan(length, False, False))
        return
    for later in range(2):
        @pl.when(core == later)
        def _():
            run(plan(length, True, bool(later)))


def forward_pair(core, causal, q_ref, k_ref, v_ref, qm_ref, km_ref, mixed_ref, qx_ref):
    length = q_ref.shape[0]

    def run(tiles):
        for head in range(2):
            base = HEAD_DIM * (1 - head)

            def own(lanes):
                return (lanes < HEAD_DIM) if head == 0 else (lanes >= HEAD_DIM)

            for tile, ranges in enumerate(tiles):
                rows = slice(tile * TILE, tile * TILE + TILE)
                lanes = lax.broadcasted_iota(jnp.int32, (TILE, PAIR), 1)
                q = jnp.where(own(lanes), q_ref[rows, :], qm_ref[rows, :])
                scores = []
                for start, size, diagonal in ranges:
                    keys = slice(start, start + size)
                    key_lanes = lax.broadcasted_iota(jnp.int32, (size, PAIR), 1)
                    k = jnp.where(own(key_lanes), k_ref[keys, :], km_ref[keys, :])
                    s = against(q, k)
                    if diagonal:
                        i = lax.broadcasted_iota(jnp.int32, s.shape, 0)
                        j = lax.broadcasted_iota(jnp.int32, s.shape, 1)
                        s = jnp.where(j <= i, s, masked_score)
                    scores.append(s)
                highest = functools.reduce(
                    jnp.maximum, [jnp.max(s, axis=1, keepdims=True) for s in scores]
                )
                out = jnp.zeros((TILE, PAIR), jnp.float32)
                for s, (start, size, _) in zip(scores, ranges):
                    keys = slice(start, start + size)
                    key_lanes = lax.broadcasted_iota(jnp.int32, (size, PAIR), 1)
                    v = jnp.where(own(key_lanes), v_ref[keys, :], jnp.ones((), jnp.bfloat16))
                    e = jnp.exp(s - highest).astype(jnp.bfloat16)
                    out = out + jnp.dot(e, v, preferred_element_type=jnp.float32)
                total = pltpu.roll(out, HEAD_DIM, 1)
                mixed = (out / total).astype(jnp.bfloat16)
                if head:
                    mixed = jnp.where(own(lanes), mixed, mixed_ref[rows, :])
                mixed_ref[rows, :] = mixed
                logsum = highest + jnp.log(out)
                qx = place_three(lanes, base, -logsum, q.astype(jnp.float32))
                qx_ref[head, rows, :] = qx.astype(jnp.bfloat16)

    each_plan(core, length, causal, run)


def backward_kernel(
    causal, core_ref, qx_ref, k_ref, v_ref, e_ref, o_ref, km_ref, dq_ref, dk_ref, dv_ref, dk_acc, dv_acc, dq_acc
):
    length = e_ref.shape[0]
    scale = HEAD_DIM ** (-0.5)

    def run(tiles):
        dk_acc[...] = jnp.zeros_like(dk_acc)
        dv_acc[...] = jnp.zeros_like(dv_acc)
        for head in range(2):
            base = HEAD_DIM * (1 - head)

            def own(lanes):
                return (lanes < HEAD_DIM) if head == 0 else (lanes >= HEAD_DIM)

            for tile, ranges in enumerate(tiles):
                rows = slice(tile * TILE, tile * TILE + TILE)
                lanes = lax.broadcasted_iota(jnp.int32, (TILE, PAIR), 1)
                nothing = jnp.zeros((), jnp.bfloat16)
                qx = qx_ref[head, rows, :]
                q = jnp.where(own(lanes), qx, nothing)
                e = jnp.where(own(lanes), e_ref[rows, :], nothing)
                wide = e.astype(jnp.float32)
                delta = jnp.sum(wide * o_ref[rows, :].astype(jnp.float32), axis=1, keepdims=True)
                ex = place_three(lanes, base, -delta, wide).astype(jnp.bfloat16)
                dq = jnp.zeros((HEAD_DIM, TILE), jnp.float32)
                for start, size, diagonal in ranges:
                    keys = slice(start, start + size)
                    key_lanes = lax.broadcasted_iota(jnp.int32, (size, PAIR), 1)
                    k = jnp.where(own(key_lanes), k_ref[keys, :], km_ref[keys, :])
                    v = jnp.where(own(key_lanes), v_ref[keys, :], km_ref[keys, :])
                    p = jnp.exp(against(k, qx))
                    if diagonal:
                        j = lax.broadcasted_iota(jnp.int32, p.shape, 0)
                        i = lax.broadcasted_iota(jnp.int32, p.shape, 1)
                        p = jnp.where(j <= i, p, 0.0)
                    ds = (p * against(v, ex)).astype(jnp.bfloat16)
                    p = p.astype(jnp.bfloat16)
                    dv_acc[keys, :] += jnp.dot(p, e, preferred_element_type=jnp.float32)
                    dk_acc[keys, :] += jnp.dot(ds, q, preferred_element_type=jnp.float32)
                    kt = k_ref[keys, :].T[head * HEAD_DIM : (head + 1) * HEAD_DIM, :]
                    dq = dq + jnp.dot(kt, ds, preferred_element_type=jnp.float32)
                dq_acc[head * HEAD_DIM : (head + 1) * HEAD_DIM, rows] = dq
        dq_ref[...] = (dq_acc[...].T.astype(jnp.bfloat16) * jnp.bfloat16(scale)).astype(jnp.bfloat16)
        dk_ref[...] = dk_acc[...].astype(jnp.bfloat16)
        dv_ref[...] = dv_acc[...].astype(jnp.bfloat16)

    each_plan(core_ref[0], length, causal, run)


def attend_back(core, qx, keys, values, grad, mixed, k_marks, causal):
    length, width = grad.shape
    extent = keys.shape[0]
    pairs = width // PAIR
    column = lambda rows: pl.BlockSpec((rows, PAIR), lambda i, p: (0, i))
    fixed = lambda rows: pl.BlockSpec((rows, PAIR), lambda i, p: (0, 0))
    return pl.pallas_call(
        functools.partial(backward_kernel, causal),
        out_shape=[
            jax.ShapeDtypeStruct((length, width), jnp.bfloat16),
            jax.ShapeDtypeStruct((extent, width), jnp.bfloat16),
            jax.ShapeDtypeStruct((extent, width), jnp.bfloat16),
        ],
        grid_spec=pltpu.PrefetchScalarGridSpec(
            num_scalar_prefetch=1,
            grid=(pairs,),
            in_specs=[
                pl.BlockSpec((2, length, PAIR), lambda i, p: (i, 0, 0)),
                column(extent), column(extent), column(length), column(length), fixed(extent),
            ],
            out_specs=[column(length), column(extent), column(extent)],
            scratch_shapes=[
                pltpu.VMEM((extent, PAIR), jnp.float32),
                pltpu.VMEM((extent, PAIR), jnp.float32),
                pltpu.VMEM((PAIR, length), jnp.float32),
            ],
        ),
        compiler_params=pltpu.CompilerParams(vmem_limit_bytes=48 * 2**20),
        cost_estimate=pl.CostEstimate(
            flops=40 * length * extent * width, bytes_accessed=16 * extent * width, transcendentals=0
        ),
    )(core, qx, keys, values, grad, mixed, k_marks)


def head_slice(array, start, span):
    piece = lax.dynamic_slice_in_dim(array, start, span, 2)
    return piece.reshape(array.shape[0], array.shape[1], 2, span // 2)


def plain_attend(query, keys, values, allowed):
    rows, length, width = query.shape
    span = 2 * HEAD_DIM
    pairs = width // span

    def one_pair(index, carry):
        mixed, logsum = carry
        start = index * span
        query_part = head_slice(query, start, span)
        key_part = head_slice(keys, start, span)
        value_part = head_slice(values, start, span)
        scores = jnp.einsum(
            "rqhe,rkhe->rhqk", query_part, key_part, preferred_element_type=jnp.float32
        )
        scores = jnp.where(allowed[:, None], scores, masked_score)
        highest = jnp.max(scores, axis=-1, keepdims=True)
        exponent = jnp.exp(scores - highest)
        total = jnp.sum(exponent, axis=-1, keepdims=True)
        probs = (exponent / total).astype(jnp.bfloat16)
        part = jnp.einsum("rhqk,rkhe->rqhe", probs, value_part, preferred_element_type=jnp.float32)
        mixed = lax.dynamic_update_slice_in_dim(mixed, part.reshape(rows, length, span), start, 2)
        logsum = lax.dynamic_update_slice_in_dim(
            logsum, (highest + jnp.log(total))[None, :, :, :, 0], index, 0
        )
        return (mixed, logsum)

    mixed = jnp.zeros((rows, length, width), jnp.float32)
    logsum = jnp.zeros((pairs, rows, 2, length), jnp.float32)
    return lax.fori_loop(0, pairs, one_pair, (mixed, logsum))


def plain_attend_back(query, keys, values, allowed, logsum, grad_mixed):
    rows, length, width = query.shape
    extent = keys.shape[1]
    span = 2 * HEAD_DIM
    pairs = width // span

    def one_pair(index, carry):
        start = index * span
        query_part = head_slice(query, start, span)
        key_part = head_slice(keys, start, span)
        value_part = head_slice(values, start, span)
        grad_part = head_slice(grad_mixed, start, span)
        scores = jnp.einsum(
            "rqhe,rkhe->rhqk", query_part, key_part, preferred_element_type=jnp.float32
        )
        scores = jnp.where(allowed[:, None], scores, masked_score)
        pair_logsum = lax.dynamic_index_in_dim(logsum, index, 0, keepdims=False)
        probs = jnp.exp(scores - pair_logsum[..., None])
        prob_grad = jnp.einsum(
            "rqhe,rkhe->rhqk", grad_part, value_part, preferred_element_type=jnp.float32
        )
        row_total = jnp.sum(probs * prob_grad, axis=-1, keepdims=True)
        score_grad = (probs * (prob_grad - row_total)).astype(jnp.bfloat16)
        query_grad = jnp.einsum(
            "rhqk,rkhe->rqhe", score_grad, key_part, preferred_element_type=jnp.float32
        )
        grad_query = lax.dynamic_update_slice_in_dim(
            carry[0], query_grad.reshape(rows, length, span), start, 2
        )
        probs_low = probs.astype(jnp.bfloat16)
        value_grad = jnp.einsum(
            "rhqk,rqhe->rkhe", probs_low, grad_part, preferred_element_type=jnp.float32
        )
        key_grad = jnp.einsum(
            "rhqk,rqhe->rkhe", score_grad, query_part, preferred_element_type=jnp.float32
        )
        grad_keys = lax.dynamic_update_slice_in_dim(
            carry[1], key_grad.reshape(rows, extent, span), start, 2
        )
        grad_values = lax.dynamic_update_slice_in_dim(
            carry[2], value_grad.reshape(rows, extent, span), start, 2
        )
        return (grad_query, grad_keys, grad_values)

    start_query = jnp.zeros((rows, length, width), jnp.float32)
    start_keys = jnp.zeros((rows, extent, width), jnp.float32)
    return lax.fori_loop(0, pairs, one_pair, (start_query, start_keys, start_keys))


def body(staged, hidden_in, memory, target_ids, memory_ids, out_grad, *weights):
    w = Weights(*weights)
    rows, length, width = hidden_in.shape
    staged = staged and (rows, length, width) == (1, 2 * TILE, 768)
    net = Staged() if staged else Plain()
    all_ = SimpleNamespace()
    tokens = rows * length
    flat_in = hidden_in.reshape(tokens, width)
    flat_memory = memory.reshape(tokens, width)

    def flat(array):
        return array.astype(jnp.bfloat16).reshape(tokens, width)

    def low(array):
        return array.astype(jnp.bfloat16).reshape(rows, length, width)

    (
        vectors, mixed_one, first, normed_one, inverse_one, back_one, mixed_two, second,
        normed_two, inverse_two, back_two,
    ) = net.front(w, all_, flat_in, flat_memory, target_ids, memory_ids)
    (
        self_query_bias, self_value_bias, self_output_bias, first_gain, first_shift,
        cross_query_bias, cross_value_bias, cross_output_bias, second_gain, second_shift,
        inner_bias, outer_bias, third_gain, third_shift,
    ) = vectors
    inner = dense(second, all_.inner_weight) + inner_bias
    cumulative = 0.5 * (1.0 + lax.erf(inner * math.sqrt(0.5)))
    active = (inner * cumulative).astype(jnp.bfloat16)
    density = jnp.exp(-0.5 * inner * inner) * (1.0 / math.sqrt(2.0 * math.pi))
    slope = cumulative + inner * density
    resid_three = second.astype(jnp.float32) + dense(active, all_.outer_weight) + outer_bias
    final, normed_three, inverse_three = layer_norm(resid_three, third_gain, third_shift)
    layer_out = final.astype(jnp.bfloat16).reshape(rows, length, width)

    g, sums = SimpleNamespace(), SimpleNamespace()
    keep = (target_ids > 0).astype(jnp.float32).reshape(tokens, 1)
    upstream = out_grad.reshape(tokens, width).astype(jnp.float32) * keep
    grad_three, sums.third_gain, sums.third_shift = norm_back(
        upstream, normed_three, inverse_three, third_gain
    )
    grad_outer = grad_three.astype(jnp.bfloat16)
    sums.outer_bias = column_sum(grad_outer)
    grad_active = dense_back(grad_outer, all_.outer_weight)
    grad_inner = (grad_active * slope).astype(jnp.bfloat16)
    sums.inner_bias = column_sum(grad_inner)
    grad_second = grad_three + dense_back(grad_inner, all_.inner_weight)
    grad_two, sums.second_gain, sums.second_shift = norm_back(
        grad_second, normed_two, inverse_two, second_gain
    )
    branch_two = grad_two.astype(jnp.bfloat16)
    sums.cross_output_bias = column_sum(branch_two)
    query_grad_two, key_sum_two, value_sum_two = back_two(
        flat(dense_back(branch_two, all_.cross_output))
    )
    key_grad_two = flat(net.scatter_row(key_sum_two))
    value_grad_two = flat(net.scatter_row(value_sum_two))
    query_grad_two = flat(query_grad_two)
    sums.cross_query_bias = column_sum(query_grad_two)
    sums.cross_value_bias = column_sum(value_grad_two)
    grad_first = grad_two + dense_back(query_grad_two, all_.cross_query)
    grad_one, sums.first_gain, sums.first_shift = norm_back(
        grad_first, normed_one, inverse_one, first_gain
    )
    branch_one = grad_one.astype(jnp.bfloat16)
    sums.self_output_bias = column_sum(branch_one)
    query_grad_one, key_sum_one, value_sum_one = back_one(
        flat(dense_back(branch_one, all_.self_output))
    )
    key_grad_one = flat(net.scatter_row(key_sum_one))
    value_grad_one = flat(net.scatter_row(value_sum_one))
    query_grad_one = flat(query_grad_one)
    sums.self_query_bias = column_sum(query_grad_one)
    sums.self_value_bias = column_sum(value_grad_one)
    (
        g.outer_weight, g.inner_weight, g.cross_output, g.cross_query, g.cross_key, g.cross_value,
        g.self_output, g.self_query, g.self_key, g.self_value,
    ), (
        g.self_query_bias, g.self_value_bias, g.self_output_bias, g.first_gain, g.first_shift,
        g.cross_query_bias, g.cross_value_bias, g.cross_output_bias, g.second_gain,
        g.second_shift, g.inner_bias, g.outer_bias, g.third_gain, g.third_shift,
    ), input_grad, memory_grad = net.reduce(
        [
            (active, grad_outer), (second, grad_inner), (mixed_two, branch_two),
            (first, query_grad_two), (flat_memory, key_grad_two), (flat_memory, value_grad_two),
            (mixed_one, branch_one), (flat_in, query_grad_one), (flat_in, key_grad_one),
            (flat_in, value_grad_one),
        ],
        [
            sums.self_query_bias, sums.self_value_bias, sums.self_output_bias, sums.first_gain,
            sums.first_shift, sums.cross_query_bias, sums.cross_value_bias,
            sums.cross_output_bias, sums.second_gain, sums.second_shift, sums.inner_bias,
            sums.outer_bias, sums.third_gain, sums.third_shift,
        ],
        grad_one,
        [all_.self_query, all_.self_key, all_.self_value, all_.cross_key, all_.cross_value],
    )
    return (layer_out, low(input_grad), low(memory_grad), *Weights(**vars(g)))


def solution(mesh):
    staged = mesh.shape["fsdp"] == 16 and mesh.shape["seq"] == 2
    row, ids = P("fsdp", "seq", None), P("fsdp", "seq")
    matrix, vector = P("fsdp", None), P("fsdp")
    weights = Weights(
        matrix, vector, matrix, matrix, vector, matrix, vector, vector, vector, matrix, vector,
        matrix, matrix, vector, matrix, vector, vector, vector, matrix, vector, matrix, vector,
        vector, vector,
    )
    return jax.shard_map(
        functools.partial(body, staged),
        mesh=mesh,
        in_specs=(row, row, ids, ids, row, *weights),
        out_specs=(row, row, row, *weights),
        check_vma=False,
    )
```

```python
import functools
import math
from types import SimpleNamespace
from typing import NamedTuple

import jax
import jax.numpy as jnp
from jax import lax
from jax.experimental import pallas as pl
from jax.experimental.pallas import tpu as pltpu
from jax.sharding import PartitionSpec as P

HEAD_DIM = 64
PAIR = 2 * HEAD_DIM
SEGMENTS = 5
TILE = 256
eps_norm = 1e-05
masked_score = -1e30


class Weights(NamedTuple):
    self_query: jax.Array
    self_query_bias: jax.Array
    self_key: jax.Array
    self_value: jax.Array
    self_value_bias: jax.Array
    self_output: jax.Array
    self_output_bias: jax.Array
    first_gain: jax.Array
    first_shift: jax.Array
    cross_query: jax.Array
    cross_query_bias: jax.Array
    cross_key: jax.Array
    cross_value: jax.Array
    cross_value_bias: jax.Array
    cross_output: jax.Array
    cross_output_bias: jax.Array
    second_gain: jax.Array
    second_shift: jax.Array
    inner_weight: jax.Array
    inner_bias: jax.Array
    outer_weight: jax.Array
    outer_bias: jax.Array
    third_gain: jax.Array
    third_shift: jax.Array


def split_vectors(w):
    return [array for array in w if array.ndim == 1]


def vectors_of(sums):
    return [
        sums.self_query_bias, sums.self_value_bias, sums.self_output_bias, sums.first_gain,
        sums.first_shift, sums.cross_query_bias, sums.cross_value_bias, sums.cross_output_bias,
        sums.second_gain, sums.second_shift, sums.inner_bias, sums.outer_bias, sums.third_gain,
        sums.third_shift,
    ]


def dense(left, right):
    return jnp.dot(left, right, preferred_element_type=jnp.float32)


def dense_back(left, right):
    return lax.dot_general(
        left, right, (((1,), (1,)), ((), ())), preferred_element_type=jnp.float32
    )


def dense_grad(left, right):
    return lax.dot_general(
        left, right, (((0,), (0,)), ((), ())), preferred_element_type=jnp.float32
    )


def column_sum(values):
    return jnp.sum(values, axis=0, dtype=jnp.float32)


def layer_norm(resid, gain, shift):
    center = resid - jnp.mean(resid, axis=-1, keepdims=True)
    spread = jnp.mean(center * center, axis=-1, keepdims=True)
    inverse = lax.rsqrt(spread + eps_norm)
    normed = center * inverse
    return (normed * gain + shift, normed, inverse)


def norm_back(upstream, normed, inverse, gain):
    scaled = upstream * gain
    plain_mean = jnp.mean(scaled, axis=-1, keepdims=True)
    cross_mean = jnp.mean(scaled * normed, axis=-1, keepdims=True)
    result = inverse * (scaled - plain_mean - normed * cross_mean)
    return (result, jnp.sum(upstream * normed, axis=0), jnp.sum(upstream, axis=0))


MESH = pl.DeviceIdType.MESH


class Spot:
    def __init__(self):
        f, c = lax.axis_index("fsdp"), lax.axis_index("seq")
        self.c, self.z, self.plane = c, f // 4, f % 4
        self.other = (f, 1 - c)
        self.by_x = ((f // 2) * 2 + (1 - f % 2), c)
        self.by_y = (self.z * 4 + (self.plane + 2) % 4, c)
        self.first = (jnp.where(c == 0, self.by_x[0], self.by_y[0]), c)
        self.second = (jnp.where(c == 0, self.by_y[0], self.by_x[0]), c)
        self.plane_x = self.by_x[0] % 4
        self.plane_y = self.by_y[0] % 4
        self.plane_first = jnp.where(c == 0, self.plane_x, self.plane_y)
        self.plane_second = jnp.where(c == 0, self.plane_y, self.plane_x)
        self.plane_both = 3 - self.plane

    def at_z(self, k):
        z = (self.z + k) % 4
        return z, (z * 4 + self.plane, self.c)

    def meet(self):
        barrier = pltpu.get_barrier_semaphore()
        partners = [self.other, self.by_x, self.by_y] + [self.at_z(k)[1] for k in (1, 2, 3)]
        for partner in partners:
            pl.semaphore_signal(barrier, inc=1, device_id=partner, device_id_type=MESH)
        pl.semaphore_wait(barrier, len(partners))


class Gather:
    sems = 31
    order = (0, 1, 3, 2)

    def __init__(self, spot, shards, wholes, send, recv, local, base):
        self.spot, self.shards, self.wholes = spot, shards, wholes
        self.send, self.recv, self.local, self.base = send, recv, local, base
        self.all = range(len(shards))

    def _columns(self, j):
        half = self.wholes[j].shape[3] // 2
        return pl.ds(pl.multiple_of(self.spot.c * half, 128), half)

    def _view(self, j, p, plane):
        return self.wholes[j].at[(self.spot.z + 4 - p) % 4, plane, :, self._columns(j)]

    def _copy(self, j, n, source, target, partner):
        return pltpu.make_async_remote_copy(
            source, target, self.send.at[self.base + j, n], self.recv.at[self.base + j, n],
            device_id=partner, device_id_type=MESH,
        )

    def _z(self, j, k):
        spot = self.spot
        source = self.shards[j].at[:, self._columns(j)]
        return self._copy(j, k - 1, source, self._view(j, 0, spot.plane), spot.at_z(k)[1])

    def _near(self, j, p, way):
        spot = self.spot
        view = self._view(j, p, spot.plane)
        source = view if p else self.shards[j].at[:, self._columns(j)]
        return self._copy(j, 3 + 2 * p + way, source, view, spot.by_y if way else spot.by_x)

    def _far(self, j, p):
        view = self._view(j, p, self.spot.plane_first)
        return self._copy(j, 11 + p, view, view, self.spot.second)

    def _swap(self, j, p, n):
        spot = self.spot
        plane = (spot.plane, spot.plane_x, spot.plane_y, spot.plane_both)[n]
        view = self._view(j, p, plane)
        return self._copy(j, 15 + 4 * p + n, view, view, spot.other)

    def _locals(self):
        return [
            pltpu.make_async_copy(
                self.shards[j], self.wholes[j].at[self.spot.z, self.spot.plane],
                self.local.at[self.base + j],
            )
            for j in self.all
        ]

    def start(self):
        for k in self.order[1:2]:
            for j in self.all:
                self._z(j, k).start()
        for j in self.all:
            for way in range(2):
                self._near(j, 0, way).start()
        for k in self.order[2:]:
            for j in self.all:
                self._z(j, k).start()
        for copy in self._locals():
            copy.start()

    def advance(self, i):
        if i < 4:
            p = self.order[i]
            for j in self.all:
                self._z(j, p).wait_recv()
                self._near(j, p, 0).start()
                self._near(j, p, 1).start()
                self._swap(j, p, 0).start()
        if 1 <= i < 5:
            p = self.order[i - 1]
            for j in self.all:
                self._near(j, p, 0).wait_recv()
                self._near(j, p, 1).wait_recv()
                self._far(j, p).start()
                self._swap(j, p, 1).start()
                self._swap(j, p, 2).start()
        if 2 <= i < 6:
            p = self.order[i - 2]
            for j in self.all:
                self._far(j, p).wait_recv()
                self._swap(j, p, 3).start()

    def finish(self):
        for copy in self._locals():
            copy.wait()
        for j in self.all:
            for p in self.order:
                if p:
                    self._z(j, p).wait_send()
                self._near(j, p, 0).wait_send()
                self._near(j, p, 1).wait_send()
                self._far(j, p).wait_send()
                for n in range(0 if p else 1, 4):
                    self._swap(j, p, n).wait()
class Reduce:
    sems = 21
    order = (2, 3, 1, 0)

    def __init__(self, spot, outs, give, mine, there, far, near, line, send, recv):
        self.spot, self.outs, self.give = spot, outs, give
        self.mine, self.there, self.far, self.near, self.line = mine, there, far, near, line
        self.send, self.recv = send, recv
        self.all = range(len(outs))

    @staticmethod
    def scratch(shapes, dtypes, shared=0):
        def buffers(*lead):
            return [pltpu.VMEM((*lead, r, w // 2), d) for (r, w), d in zip(shapes, dtypes)]

        n = len(shapes)
        return (
            buffers(4, 4)[: n - shared] + buffers(4, 4) + buffers(4, 4) + buffers(4)
            + buffers(4, 2) + buffers(3) + [pltpu.SemaphoreType.DMA((n, Reduce.sems))] * 2
        )

    @staticmethod
    def unpack(spot, outs, refs, shared=0):
        n = len(outs)
        give, refs = list(refs[: n - shared]), refs[n - shared :]
        for i in range(shared):
            half = outs[n - shared + i].shape[1] // 2
            give.append(give[n - shared - 1].at[:, :, :, pl.ds(i * half, half)])
        groups = [refs[i * n : (i + 1) * n] for i in range(5)]
        return Reduce(spot, outs, give, *groups, *refs[5 * n : 5 * n + 2])

    def free(self, j):
        for p in self.order:
            self._cross(j, p).wait_send()
        self.freed = (j,)

    freed = ()

    def part(self, js):
        def some(items):
            return [items[j] for j in js]

        lists = (self.outs, self.give, self.mine, self.there, self.far, self.near, self.line)
        chosen = Reduce(self.spot, *[some(items) for items in lists], self.send, self.recv)
        chosen.base = js[0]
        return chosen

    base = 0

    def put(self, j, core_of, value, columns=None, z_first=0):
        target = self.give[j] if core_of else self.mine[j]
        rows = target.shape[2]
        block = 4 * rows
        columns = slice(None) if columns is None else columns
        for i in range(value.shape[0] // block):
            p = (z_first + i + 4 - self.spot.z) % 4
            piece = value[i * block : (i + 1) * block]
            target[p, :, :, columns] = piece.reshape(4, rows, -1).astype(target.dtype)

    def _columns(self, j, core):
        half = self.outs[j].shape[1] // 2
        return pl.ds(pl.multiple_of(core * half, 128), half)

    def _copy(self, j, n, source, target, partner):
        return pltpu.make_async_remote_copy(
            source, target, self.send.at[self.base + j, n], self.recv.at[self.base + j, n],
            device_id=partner, device_id_type=MESH,
        )

    def _cross(self, j, p):
        return self._copy(j, p, self.give[j].at[p], self.there[j].at[p], self.spot.other)

    def _far(self, j, p):
        spot = self.spot
        return self._copy(
            j, 4 + p, self.mine[j].at[p, spot.plane_both], self.far[j].at[p], spot.first
        )

    def _near(self, j, p, way):
        spot = self.spot
        plane, partner = (spot.plane_y, spot.by_y) if way else (spot.plane_x, spot.by_x)
        return self._copy(
            j, 8 + 2 * p + way, self.mine[j].at[p, plane], self.near[j].at[p, way], partner
        )

    def _line(self, j, p):
        spot = self.spot
        return self._copy(
            j, 16 + p, self.mine[j].at[p, spot.plane], self.line[j].at[p - 1], spot.at_z(p)[1]
        )

    def _last(self, j):
        view = self.outs[j].at[:, self._columns(j, self.spot.c)]
        return self._copy(j, 20, view, view, self.spot.other)

    def start(self, j):
        for p in self.order:
            self._cross(j, p).start()

    def _sum(self, j, p, plane, *others):
        total = self.mine[j][p, plane].astype(jnp.float32)
        total = total + self.there[j][p, plane].astype(jnp.float32)
        for other in others:
            total = total + other.astype(jnp.float32)
        return total

    def _store(self, j, p, plane, total):
        self.mine[j][p, plane] = total.astype(self.mine[j].dtype)

    def advance(self, i):
        spot = self.spot
        if i < 4:
            p = self.order[i]
            for j in self.all:
                self._cross(j, p).wait_recv()
                self._store(j, p, spot.plane_both, self._sum(j, p, spot.plane_both))
                self._far(j, p).start()
        if 0 <= i - 1 < 4:
            p = self.order[i - 1]
            for j in self.all:
                self._store(j, p, spot.plane_first, self._sum(j, p, spot.plane_first))
                self._far(j, p).wait_recv()
                self._store(
                    j, p, spot.plane_second, self._sum(j, p, spot.plane_second, self.far[j][p])
                )
                self._near(j, p, 0).start()
                self._near(j, p, 1).start()
        if 0 <= i - 2 < 4:
            p = self.order[i - 2]
            for j in self.all:
                self._near(j, p, 0).wait_recv()
                self._near(j, p, 1).wait_recv()
                total = self._sum(j, p, spot.plane, self.near[j][p, 0], self.near[j][p, 1])
                if p:
                    self._store(j, p, spot.plane, total)
                    self._line(j, p).start()
                else:
                    for k in (1, 2, 3):
                        self._line(j, k).wait_recv()
                        total = total + self.line[j][k - 1].astype(jnp.float32)
                    self.outs[j][:, self._columns(j, spot.c)] = total
                    self._last(j).start()

    def finish(self):
        for j in self.all:
            for p in self.order:
                if j not in self.freed:
                    self._cross(j, p).wait_send()
                self._far(j, p).wait_send()
                self._near(j, p, 0).wait_send()
                self._near(j, p, 1).wait_send()
                if p:
                    self._line(j, p).wait_send()
            self._last(j).wait()


def gather_kernel(groups, *refs):
    counts = [len(group) for group in groups]
    count = sum(counts)
    shards, (x_ref, memory_ref, qm_ref, own_km_one, own_km_two, grad_ref), refs = (
        refs[:count], refs[count : count + 6], refs[count + 6 :],
    )
    wholes, (lines_ref, sums_ref), results, refs = (
        refs[:count], refs[count : count + 2], refs[count + 2 : count + 22], refs[count + 22 :],
    )
    kept, refs = refs[:20], refs[20:]
    (
        mixed_one, qx_one, first, normed_one, inverse_one, mixed_two, qx_two, second, active,
        grad_inner, k_one, v_one, k_two, v_two, km_one, km_two, layer_out, grad_outer, grad_two,
        branch_two,
    ) = kept
    (
        normed_two, inverse_two, slope, outer, query, weight, table, send, recv, local, weight_sem,
        send_row, recv_row, out_sem,
    ) = refs
    spot = Spot()
    length, width = x_ref.shape
    scale = HEAD_DIM ** (-0.5)
    gathers, start = [], 0
    for n in counts:
        chosen = slice(start, start + n)
        gathers.append(Gather(spot, shards[chosen], wholes[chosen], send, recv, local, start))
        start += n
    one, two, three_, four = gathers

    def fetch(i):
        return pltpu.make_async_copy(wholes[i], weight.at[i if i < 3 else i - 1], weight_sem.at[i])

    def matrix(i):
        return weight[i if i < 3 else i - 1].reshape(width, width)

    def line(i):
        return lines_ref[i : i + 1, :]

    def cross(i, ref):
        return pltpu.make_async_remote_copy(
            ref.at[pl.ds(0, length)], ref.at[pl.ds(length, length)], send_row.at[i],
            recv_row.at[i], device_id=spot.other, device_id_type=MESH,
        )

    def leave(i):
        return pltpu.make_async_copy(kept[i], results[i], out_sem.at[i])

    def norm(total, gain, shift, low, normed, inverse):
        center = total - jnp.mean(total, axis=-1, keepdims=True)
        spread = jnp.mean(center * center, axis=-1, keepdims=True)
        factor = lax.rsqrt(spread + eps_norm)
        unit = center * factor
        normed[...] = unit
        inverse[...] = jnp.broadcast_to(factor, inverse.shape)
        low[...] = (unit * gain + shift).astype(jnp.bfloat16)

    def pairs(first_pair, last_pair, causal, k, v, km, mixed, qx):
        def one_pair(i, carry):
            columns = pl.ds(pl.multiple_of(i * PAIR, PAIR), PAIR)
            forward_pair(
                spot.c, causal, query.at[:, columns], k.at[:, columns], v.at[:, columns], qm_ref,
                km, mixed.at[:, columns], qx.at[pl.ds(2 * i, 2)],
            )
            return carry

        lax.fori_loop(first_pair, last_pair, one_pair, 0)

    spot.meet()
    one.start()
    two.start()
    km_one[0:length, :] = own_km_one[...]
    km_two[0:length, :] = own_km_two[...]
    marks = [cross(0, km_one), cross(1, km_two)]
    for copy in marks:
        copy.start()
    one.advance(1)
    one.advance(2)
    one.advance(3)
    one.advance(4)
    one.advance(5)
    one.finish()
    three_.start()
    for i in range(3):
        fetch(i).start()
    vector_copy = pltpu.make_async_copy(wholes[3], table, weight_sem.at[3])
    vector_copy.start()
    vector_copy.wait()
    lines = jnp.zeros(lines_ref.shape, jnp.float32)
    bias = jnp.zeros((8, width), jnp.float32)
    for f in range(16):
        i = lax.broadcasted_iota(jnp.int32, (128, width), 0)
        j = lax.broadcasted_iota(jnp.int32, (128, width), 1)
        at = ((i < 48) & (j == i + 48 * f)).astype(jnp.bfloat16)
        piece = table[f // 4, f % 4, :, 0:128].astype(jnp.bfloat16)
        lines = lines + dense(piece, at)
        piece = [table[q, f // 4, 13 + f % 4 : 14 + f % 4, 0:128] for q in range(4)]
        bias = bias + dense(jnp.concatenate(piece + piece).astype(jnp.bfloat16), at)
    lines_ref[...] = lines

    fetch(0).wait()
    fetch(1).wait()
    fetch(2).wait()
    k_one[0:length, :] = dense(x_ref[...], matrix(1)).astype(jnp.bfloat16)
    row_one = [cross(2, k_one), cross(3, v_one)]
    row_one[0].start()
    v_one[0:length, :] = (dense(x_ref[...], matrix(2)) + line(1)).astype(jnp.bfloat16)
    row_one[1].start()
    query[...] = ((dense(x_ref[...], matrix(0)) + line(0)) * scale).astype(jnp.bfloat16)
    two.advance(1)
    for copy in marks:
        copy.wait()
    for copy in row_one:
        copy.wait()
    leaving = [leave(i) for i in (10, 11, 14, 15)]
    for copy in leaving:
        copy.start()
    pairs(0, 3, True, k_one, v_one, km_one, mixed_one, qx_one)
    two.advance(2)
    pairs(3, 6, True, k_one, v_one, km_one, mixed_one, qx_one)
    for i in (0, 1):
        leaving.append(leave(i))
        leaving[-1].start()
    two.advance(3)
    two.advance(4)
    two.advance(5)
    two.finish()
    for i in range(4, 9):
        fetch(i).start()
    fetch(4).wait()
    k_two[0:length, :] = dense(memory_ref[...], matrix(4)).astype(jnp.bfloat16)
    row_two = [cross(4, k_two), cross(5, v_two)]
    row_two[0].start()
    fetch(5).wait()
    v_two[0:length, :] = (dense(memory_ref[...], matrix(5)) + line(6)).astype(jnp.bfloat16)
    row_two[1].start()
    fetch(6).wait()
    total = x_ref[...].astype(jnp.float32) + dense(mixed_one[...], matrix(6)) + line(2)
    norm(total, line(3), line(4), first, normed_one, inverse_one)
    fetch(7).wait()
    query[...] = ((dense(first[...], matrix(7)) + line(5)) * scale).astype(jnp.bfloat16)
    three_.advance(1)
    for copy in row_two:
        copy.wait()
    for i in (2, 3, 4, 12, 13):
        leaving.append(leave(i))
        leaving[-1].start()
    pairs(0, 3, False, k_two, v_two, km_two, mixed_two, qx_two)
    three_.advance(2)
    pairs(3, 6, False, k_two, v_two, km_two, mixed_two, qx_two)
    three_.advance(3)
    four.start()
    fetch(8).wait()
    total = first[...].astype(jnp.float32) + dense(mixed_two[...], matrix(8)) + line(7)
    norm(total, line(8), line(9), second, normed_two, inverse_two)
    three_.advance(4)
    three_.advance(5)
    three_.finish()
    chunks = [slice(q * width, (q + 1) * width) for q in range(4)]
    inner = [
        pltpu.make_async_copy(wholes[9].at[:, :, :, chunks[q]], weight.at[q], weight_sem.at[q])
        for q in range(4)
    ]
    for copy in inner:
        copy.start()
    for i in (5, 6, 7):
        leaving.append(leave(i))
        leaving[-1].start()
    four.advance(1)
    for q in range(4):
        inner[q].wait()
        value = dense(second[...], weight[q].reshape(width, width)) + bias[q : q + 1, :]
        cumulative = 0.5 * (1.0 + lax.erf(value * math.sqrt(0.5)))
        active[:, chunks[q]] = (value * cumulative).astype(jnp.bfloat16)
        density = jnp.exp(-0.5 * value * value) * (1.0 / math.sqrt(2.0 * math.pi))
        slope[:, chunks[q]] = cumulative + value * density
        if q < 3:
            four.advance(q + 2)
    four.advance(5)
    four.finish()
    last = pltpu.make_async_copy(wholes[10], outer, weight_sem.at[4])
    last.start()
    leaving.append(leave(8))
    leaving[-1].start()

    def add_row(i, values):
        sums_ref[i : i + 1, :] = jnp.sum(values.astype(jnp.float32), axis=0, keepdims=True)

    def back(grad, normed, factor, gain):
        scaled = grad * gain
        plain_mean = jnp.mean(scaled, axis=-1, keepdims=True)
        cross_mean = jnp.mean(scaled * normed, axis=-1, keepdims=True)
        return factor * (scaled - plain_mean - normed * cross_mean)

    last.wait()
    total = second[...].astype(jnp.float32) + line(10)
    for q in range(4):
        total = total + dense(active[:, chunks[q]], outer[q].reshape(width, width))
    center = total - jnp.mean(total, axis=-1, keepdims=True)
    factor = lax.rsqrt(jnp.mean(center * center, axis=-1, keepdims=True) + eps_norm)
    unit = center * factor
    layer_out[...] = (unit * line(11) + line(12)).astype(jnp.bfloat16)
    keep = jnp.where(qm_ref[:, 0:1].astype(jnp.float32) < 0.0, 1.0, 0.0)
    upstream = grad_ref[...].astype(jnp.float32) * keep
    add_row(0, upstream * unit)
    add_row(1, upstream)
    grad_three = back(upstream, unit, factor, line(11))
    grad_outer[...] = grad_three.astype(jnp.bfloat16)
    add_row(2, grad_outer[...])
    for i in (16, 17):
        leaving.append(leave(i))
        leaving[-1].start()
    grad = grad_three
    for q in range(4):
        value = dense_back(grad_outer[...], outer[q].reshape(width, width))
        piece = (value * slope[:, chunks[q]]).astype(jnp.bfloat16)
        grad_inner[:, chunks[q]] = piece
        add_row(8 + q, piece)
        grad = grad + dense_back(piece, weight[q].reshape(width, width))
    leaving.append(leave(9))
    leaving[-1].start()
    unit = normed_two[...]
    add_row(3, grad * unit)
    add_row(4, grad)
    grad_two[...] = back(grad, unit, inverse_two[:, 0:1], line(8))
    branch_two[...] = grad_two[...].astype(jnp.bfloat16)
    for i in (18, 19):
        leaving.append(leave(i))
        leaving[-1].start()
    add_row(5, branch_two[...])
    for copy in leaving:
        copy.wait()


def back_kernel(*refs):
    active, grad_outer, second, grad_inner = refs[:4]
    branch_two, grad_two, normed_one, inverse_one, lines_ref, first, memory = refs[4:11]
    attends = (refs[11:16], refs[16:21])
    wholes = refs[21:24]
    outs, refs = refs[24:30], refs[30:]
    (grad_one, branch_one, dq_two, kg_two, vg_two, dq_one, kg_one, vg_one, sums_ref), refs = (
        refs[:9], refs[9:],
    )
    (
        wide, narrow, qx, k, v, mixed, km, e, dk, dv, dk_there, dv_there, weight, dk_acc, dv_acc,
        dq_acc, sem, send_row, recv_row,
    ) = refs[-19:]
    spot = Spot()
    reduce = Reduce.unpack(spot, outs, refs[:-19], 4)
    length, width = branch_two.shape
    half = width // 2

    def load(source, target, i):
        return pltpu.make_async_copy(source, target, sem.at[i])

    def load_attend(i):
        targets = (qx, k, v, mixed, km)
        return [load(source, target, 4 + n) for n, (source, target) in enumerate(zip(attends[i], targets))]

    early = [
        load(active, wide.at[0], 0), load(grad_outer, narrow.at[0], 1),
        load(second, narrow.at[1], 2), load(grad_inner, wide.at[1], 3),
    ]
    for copy in early:
        copy.start()
    attend = load_attend(0)
    matrices = [load(wholes[i], weight.at[i], 9 + i) for i in range(3)]
    for copy in attend + matrices:
        copy.start()
    spot.meet()
    for copy in early[:2]:
        copy.wait()
    for core_of in (1, 0):
        start = pl.multiple_of((spot.c if core_of == 0 else 1 - spot.c) * half, 128)
        right = narrow[0, :, pl.ds(start, half)]
        for chunk in range(4):
            left = wide[0, :, chunk * width : (chunk + 1) * width]
            reduce.put(0, core_of, dense_grad(left, right), None, chunk)
        if core_of:
            reduce.start(0)
    for copy in early[2:]:
        copy.wait()
    for core_of in (1, 0):
        for chunk in range(4):
            base = (spot.c if core_of == 0 else 1 - spot.c) * 2 * width + chunk * half
            right = wide[1, :, pl.ds(pl.multiple_of(base, 128), half)]
            columns = slice(chunk * half, (chunk + 1) * half)
            reduce.put(1, core_of, dense_grad(narrow[1], right), columns)
        if core_of:
            reduce.start(1)
    ffn, others = reduce.part((0, 1)), reduce.part((2, 3, 4, 5))

    def multiply(j, left, right):
        for core_of in (1, 0):
            start = pl.multiple_of((spot.c if core_of == 0 else 1 - spot.c) * half, 128)
            reduce.put(j, core_of, dense_grad(left[...], right[:, pl.ds(start, half)]))
            if core_of:
                reduce.start(j)

    def matrix(i):
        return weight[i].reshape(width, width)

    def pairs(first_pair, last_pair, causal, dq):
        def one_pair(i, carry):
            columns = pl.ds(pl.multiple_of(i * PAIR, PAIR), PAIR)
            backward_pair(
                spot.c, causal, qx.at[pl.ds(2 * i, 2)], k.at[:, columns], v.at[:, columns],
                e.at[:, columns], mixed.at[:, columns], km, dq.at[:, columns], dk.at[:, columns],
                dv.at[:, columns], dk_acc, dv_acc, dq_acc,
            )
            return carry

        lax.fori_loop(first_pair, last_pair, one_pair, 0)

    def cross(i):
        source, target = ((dk, dk_there), (dv, dv_there))[i % 2]
        return pltpu.make_async_remote_copy(
            source.at[pl.ds(length, length)], target, send_row.at[i], recv_row.at[i],
            device_id=spot.other, device_id_type=MESH,
        )

    def left(own, out, n):
        return load(own.at[pl.ds(0, length)], out, 12 + n)

    def join(i, kg, vg):
        for n, (own, there, out) in enumerate(((dk, dk_there, kg), (dv, dv_there, vg))):
            cross(2 * i + n).wait()
            total = own[0:length, :].astype(jnp.float32) + there[...].astype(jnp.float32)
            own[0:length, :] = total.astype(jnp.bfloat16)
            left(own, out, n).start()

    def add_row(i, values):
        sums_ref[i : i + 1, :] = jnp.sum(values.astype(jnp.float32), axis=0, keepdims=True)

    factors = [load(first, narrow.at[0], 1), load(memory, narrow.at[1], 2)]
    for copy in factors:
        copy.start()
    ffn.advance(0)
    for copy in attend + matrices:
        copy.wait()
    e[...] = dense_back(branch_two[...], matrix(0)).astype(jnp.bfloat16)
    pairs(0, 2, False, dq_two)
    ffn.advance(1)
    for copy in factors:
        copy.wait()
    reduce.free(1)
    multiply(2, mixed, branch_two)
    pairs(2, 4, False, dq_two)
    ffn.advance(2)
    pairs(4, 6, False, dq_two)
    cross(0).start()
    cross(1).start()
    attend = load_attend(1)
    for copy in attend:
        copy.start()
    ffn.advance(3)
    multiply(3, narrow.at[0], dq_two)
    join(0, kg_two, vg_two)
    key_part, value_part = dk.at[pl.ds(0, length)], dv.at[pl.ds(0, length)]
    multiply(4, narrow.at[1], key_part)
    multiply(5, narrow.at[1], value_part)
    add_row(4, value_part[...])
    grad = grad_two[...] + dense_back(dq_two[...], matrix(1))
    normed = normed_one[...]
    add_row(0, grad * normed)
    add_row(1, grad)
    scaled = grad * lines_ref[3:4, :]
    plain_mean = jnp.mean(scaled, axis=-1, keepdims=True)
    cross_mean = jnp.mean(scaled * normed, axis=-1, keepdims=True)
    grad_one[...] = inverse_one[:, 0:1] * (scaled - plain_mean - normed * cross_mean)
    branch_one[...] = grad_one[...].astype(jnp.bfloat16)
    ffn.advance(4)
    others.advance(0)
    e[...] = dense_back(branch_one[...], matrix(2)).astype(jnp.bfloat16)
    for copy in attend:
        copy.wait()
    left(dk, kg_two, 0).wait()
    left(dv, vg_two, 1).wait()
    pairs(0, 2, True, dq_one)
    ffn.advance(5)
    others.advance(1)
    pairs(2, 4, True, dq_one)
    others.advance(2)
    pairs(4, 6, True, dq_one)
    cross(2).start()
    cross(3).start()
    others.advance(3)
    add_row(2, branch_one[...])
    add_row(3, dq_two[...])
    add_row(5, dq_one[...])
    others.advance(4)
    join(1, kg_one, vg_one)
    add_row(6, value_part[...])
    others.advance(5)
    reduce.finish()
    left(dk, kg_one, 0).wait()
    left(dv, vg_one, 1).wait()


def reduce_kernel(count, *refs):
    factors, refs = refs[: 2 * count], refs[2 * count :]
    (table, grad_one, key_two, value_two), wholes, refs = refs[:4], refs[4:9], refs[9:]
    outs, (input_ref, memory_ref), refs = (
        refs[: count + 1], refs[count + 1 : count + 3], refs[count + 3 :],
    )
    weight, refs = refs[-1], refs[:-1]
    sem, refs = refs[-1], refs[:-1]
    spot = Spot()
    reduce = Reduce.unpack(spot, outs, refs)
    width = factors[0].shape[1]
    half = width // 2
    copies = [pltpu.make_async_copy(wholes[i], weight.at[i], sem.at[i]) for i in range(5)]
    for copy in copies:
        copy.start()
    spot.meet()
    for core_of in (1, 0):
        start = pl.multiple_of((spot.c if core_of == 0 else 1 - spot.c) * 128, 128)
        for z in range(4):
            p = (z + 4 - spot.z) % 4
            target = reduce.give[count] if core_of else reduce.mine[count]
            target[p] = table[z, :, :, pl.ds(start, 128)]
    reduce.start(count)
    for core_of in (1, 0):
        start = pl.multiple_of((spot.c if core_of == 0 else 1 - spot.c) * half, 128)
        for i in range(count):
            right = factors[2 * i + 1][:, pl.ds(start, half)]
            reduce.put(i, core_of, dense_grad(factors[2 * i][...], right))
            if core_of:
                reduce.start(i)
    reduce.advance(0)
    for copy in copies:
        copy.wait()

    def product(i, factor):
        return dense_back(factor[...], weight[i].reshape(width, width))

    total = grad_one[...] + product(0, factors[-5])
    reduce.advance(1)
    total = total + product(1, factors[-3]) + product(2, factors[-1])
    input_ref[...] = total.astype(jnp.bfloat16)
    reduce.advance(2)
    memory_ref[...] = (product(3, key_two) + product(4, value_two)).astype(jnp.bfloat16)
    reduce.advance(3)
    reduce.advance(4)
    reduce.advance(5)
    reduce.finish()


def hand_on(*refs):
    count = len(refs) // 2
    for source, target in zip(refs[:count], refs[count:]):
        target[...] = source[...]


class Staged:
    staged = True

    def __init__(self):
        self.c = lax.axis_index("seq")
        self.parts = []

    def swap(self, array):
        pairs = [(f * 2 + c, f * 2 + 1 - c) for f in range(16) for c in range(2)]
        return lax.ppermute(array, ("fsdp", "seq"), pairs)

    def front(self, w, all_, sums, hidden, memory, target_ids, memory_ids, out_grad):
        vectors = split_vectors(w)
        narrow = [v for v in vectors if v.shape[0] == 48]
        (wide,) = [v for v in vectors if v.shape[0] != 48]
        table = jnp.concatenate([jnp.stack(narrow), wide.reshape(-1, 48)]).astype(jnp.float32)
        table = jnp.pad(table, ((0, 24 - table.shape[0]), (0, 256 - 48)))
        groups = (
            (w.self_query, w.self_key, w.self_value, table),
            (w.cross_key, w.cross_value, w.self_output, w.cross_query, w.cross_output),
            (w.inner_weight,),
            (w.outer_weight,),
        )
        shards = [array for group in groups for array in group]
        count, (length, width) = len(shards), hidden.shape
        pairs = width // PAIR
        low, full = jnp.bfloat16, jnp.float32
        some = [
            ((length, width), low), ((2 * pairs, length, PAIR), low), ((length, width), low),
            ((length, width), full), ((length, 128), full),
        ]
        wide_state = ((length, w.inner_weight.shape[1]), low)
        kept = some + some[:3] + [wide_state] * 2 + [((2 * length, width), low)] * 4
        kept += [((2 * length, PAIR), low)] * 2 + [some[0], some[0], some[3], some[0]]
        anywhere, near = pl.BlockSpec(memory_space=pl.ANY), pl.BlockSpec(memory_space=pltpu.VMEM)
        results = pl.pallas_call(
            functools.partial(gather_kernel, groups),
            out_shape=[jax.ShapeDtypeStruct((4, 4) + s.shape, s.dtype) for s in shards]
            + [jax.ShapeDtypeStruct((24, width), full), jax.ShapeDtypeStruct((16, width), full)]
            + [jax.ShapeDtypeStruct(*k) for k in kept],
            in_specs=[anywhere] * count + [near] * 6,
            out_specs=[anywhere] * count + [near] * 2 + [anywhere] * len(kept),
            scratch_shapes=[pltpu.VMEM(*k) for k in kept]
            + [
                pltpu.VMEM(*some[3]),
                pltpu.VMEM(*some[4]),
                pltpu.VMEM(wide_state[0], full),
                pltpu.VMEM((4, 4, *w.outer_weight.shape), low),
                pltpu.VMEM((length, width), low),
                pltpu.VMEM((8, 4, 4, width // 16, width), low),
                pltpu.VMEM((4, 4, 24, 256), full),
                pltpu.SemaphoreType.DMA((count, Gather.sems)),
                pltpu.SemaphoreType.DMA((count, Gather.sems)),
                pltpu.SemaphoreType.DMA((count,)),
                pltpu.SemaphoreType.DMA((9,)),
                pltpu.SemaphoreType.DMA((6,)),
                pltpu.SemaphoreType.DMA((6,)),
                pltpu.SemaphoreType.DMA((20,)),
            ],
            compiler_params=pltpu.CompilerParams(
                collective_id=0, has_side_effects=True, vmem_limit_bytes=60 * 2**20
            ),
        )(
            *shards, hidden, memory, query_marks(target_ids[0]), key_marks_of(target_ids[0]),
            key_marks_of(memory_ids[0]), out_grad,
        )
        wholes, (lines, summed), results = (
            results[:count], results[count : count + 2], results[count + 2 :],
        )
        flats = [array.reshape(-1, array.shape[3]) for array in wholes]
        (
            all_.self_query, all_.self_key, all_.self_value, _, all_.cross_key, all_.cross_value,
            all_.self_output, all_.cross_query, all_.cross_output, all_.inner_weight,
            all_.outer_weight,
        ) = flats
        (
            mixed_one, qx_one, first, normed_one, inverse_one, mixed_two, qx_two, second, active,
            grad_inner, k_one, v_one, k_two, v_two, km_one, km_two, layer_out, grad_outer,
            grad_two, branch_two,
        ) = results
        (
            sums.third_gain, sums.third_shift, sums.outer_bias, sums.second_gain,
            sums.second_shift, sums.cross_output_bias,
        ) = summed[:6]
        sums.inner_bias = summed[8:12].reshape(-1)
        self.kept = (
            (qx_two, k_two, v_two, mixed_two, km_two), (qx_one, k_one, v_one, mixed_one, km_one),
            normed_one, inverse_one, lines, branch_two,
        )
        self.first, self.all, self.inputs = first, all_, (hidden, memory)
        return layer_out, active, grad_outer, second, grad_inner, grad_two

    def back(self, g, sums, active, grad_outer, second, grad_inner, grad_two):
        two, one, normed_one, inverse_one, lines, branch_two = self.kept
        all_ = self.all
        length, width = branch_two.shape
        anywhere, near = pl.BlockSpec(memory_space=pl.ANY), pl.BlockSpec(memory_space=pltpu.VMEM)
        low, full = jnp.bfloat16, jnp.float32
        shapes = [(active.shape[1] // 16, width), (width // 16, active.shape[1])]
        shapes += [(width // 16, width)] * 4
        hidden, memory = self.inputs

        def blocks(array):
            return array.reshape(4, 4, -1, width)

        state = ((length, width), low)
        row = ((2 * length, width), low)
        outs = [((length, width), full)] + [state] * 7 + [((8, width), full)]
        (
            g.outer_weight, g.inner_weight, g.cross_output, g.cross_query, g.cross_key,
            g.cross_value, grad_one, branch_one, query_two, key_two, value_two, query_one, key_one,
            value_one, lines_sum,
        ) = pl.pallas_call(
            back_kernel,
            out_shape=[jax.ShapeDtypeStruct(s, full) for s in shapes]
            + [jax.ShapeDtypeStruct(*o) for o in outs],
            in_specs=[anywhere] * 4 + [near] * 5 + [anywhere] * 15,
            out_specs=[near] * 9 + [anywhere] * 2 + [near] + [anywhere] * 2 + [near],
            scratch_shapes=Reduce.scratch(shapes, [low] * 6, 4)
            + [
                pltpu.VMEM((2, length, 4 * width), low),
                pltpu.VMEM((2, length, width), low),
                pltpu.VMEM((width // HEAD_DIM, length, PAIR), low),
                pltpu.VMEM(*row), pltpu.VMEM(*row), pltpu.VMEM(*state),
                pltpu.VMEM((2 * length, PAIR), low),
                pltpu.VMEM(*state), pltpu.VMEM(*row), pltpu.VMEM(*row),
                pltpu.VMEM(*state), pltpu.VMEM(*state),
                pltpu.VMEM((3, 4, 4, width // 16, width), low),
                pltpu.VMEM((2 * length, PAIR), full), pltpu.VMEM((2 * length, PAIR), full),
                pltpu.VMEM((PAIR, length), full),
                pltpu.SemaphoreType.DMA((14,)),
                pltpu.SemaphoreType.DMA((4,)),
                pltpu.SemaphoreType.DMA((4,)),
            ],
            compiler_params=pltpu.CompilerParams(
                collective_id=2, has_side_effects=True, vmem_limit_bytes=61 * 2**20
            ),
        )(
            active, grad_outer, second, grad_inner, branch_two, grad_two, normed_one, inverse_one,
            lines, self.first, memory, *two, *one,
            blocks(all_.cross_output), blocks(all_.cross_query), blocks(all_.self_output),
        )
        (
            sums.first_gain, sums.first_shift, sums.self_output_bias, sums.cross_query_bias,
            sums.cross_value_bias, sums.self_query_bias, sums.self_value_bias, _,
        ) = lines_sum
        products = [
            (one[3], branch_one), (hidden, query_one), (hidden, key_one), (hidden, value_one),
        ]
        weights = (
            all_.self_query, all_.self_key, all_.self_value, all_.cross_key, all_.cross_value
        )
        vectors = vectors_of(sums)
        narrow = [v for v in vectors if v.shape[0] == 768]
        (wide,) = [v for v in vectors if v.shape[0] != 768]
        rows = len(narrow)
        table = jnp.concatenate(
            [
                jnp.stack(narrow).reshape(rows, 16, 48).transpose(1, 0, 2),
                wide.reshape(16, -1, 48),
            ],
            axis=1,
        )
        table = jnp.pad(table, ((0, 0), (0, 24 - table.shape[1]), (0, 256 - 48)))
        count = len(products)
        shapes = [(width // 16, width)] * count + [(24, 256)]
        *results, table, input_grad, memory_grad = pl.pallas_call(
            functools.partial(reduce_kernel, count),
            out_shape=[jax.ShapeDtypeStruct(s, full) for s in shapes]
            + [jax.ShapeDtypeStruct(*state)] * 2,
            in_specs=[near] * (2 * count + 4) + [anywhere] * 5,
            out_specs=[near] * (count + 3),
            scratch_shapes=Reduce.scratch(shapes, [low] * count + [full])
            + [
                pltpu.SemaphoreType.DMA((5,)),
                pltpu.VMEM((5, 4, 4, width // 16, width), low),
            ],
            compiler_params=pltpu.CompilerParams(
                collective_id=1, has_side_effects=True, vmem_limit_bytes=60 * 2**20
            ),
        )(
            *[factor for pair in products for factor in pair], table.reshape(4, 4, 24, 256),
            grad_one, key_two, value_two, *[blocks(array) for array in weights],
        )
        g.self_output, g.self_query, g.self_key, g.self_value = results
        reduced, row = [], 0
        for v in vectors:
            if v.shape[0] == 768:
                reduced.append(table[row, :48])
                row += 1
            else:
                reduced.append(table[rows : rows + v.shape[0] // 768, :48].reshape(-1))
        done = (
            g.self_query, g.self_key, g.self_value, g.self_output, g.cross_query, g.cross_key,
            g.cross_value, g.cross_output, g.inner_weight, g.outer_weight, input_grad, memory_grad,
        )
        (
            g.self_query, g.self_key, g.self_value, g.self_output, g.cross_query, g.cross_key,
            g.cross_value, g.cross_output, g.inner_weight, g.outer_weight, input_grad, memory_grad,
        ) = pl.pallas_call(
            hand_on,
            out_shape=[jax.ShapeDtypeStruct(array.shape, array.dtype) for array in done],
            in_specs=[near] * len(done),
            out_specs=[near] * len(done),
        )(*done)
        return reduced, input_grad, memory_grad


class Plain:
    staged = False

    def front(self, w, all_, sums, hidden, memory, target_ids, memory_ids, out_grad):
        def whole(array):
            return lax.all_gather(array, "fsdp", axis=0, tiled=True)

        all_.__dict__.update(Weights(*map(whole, w))._asdict())
        vectors = [array.astype(jnp.float32) for array in split_vectors(Weights(**vars(all_)))]
        (
            self_query_bias, self_value_bias, self_output_bias, first_gain, first_shift,
            cross_query_bias, cross_value_bias, cross_output_bias, second_gain, second_shift,
            inner_bias, outer_bias, third_gain, third_shift,
        ) = vectors
        rows, length = target_ids.shape
        width = hidden.shape[1]
        scale = HEAD_DIM ** (-0.5)

        def low(array):
            return array.astype(jnp.bfloat16).reshape(rows, length, width)

        row_ids, source_ids = self.gather_row(target_ids), self.gather_row(memory_ids)
        query_places = lax.axis_index("seq") * length + jnp.arange(length)
        key_places = jnp.arange(row_ids.shape[1])
        allowed_self = (target_ids[:, :, None] == row_ids[:, None, :]) & (
            key_places[None, None, :] <= query_places[None, :, None]
        )
        allowed_cross = target_ids[:, :, None] == source_ids[:, None, :]

        def attention(query, keys, values, allowed):
            mixed, logsum = plain_attend(query, keys, values, allowed)

            def back(grad):
                query_sum, key_sum, value_sum = plain_attend_back(
                    query, keys, values, allowed, logsum, grad.reshape(rows, length, width)
                )
                return query_sum.astype(jnp.bfloat16) * scale, key_sum, value_sum

            return mixed.astype(jnp.bfloat16).reshape(rows * length, width), back

        key_one = self.gather_row(low(dense(hidden, all_.self_key)))
        value_one = self.gather_row(low(dense(hidden, all_.self_value) + self_value_bias))
        query_one = low((dense(hidden, all_.self_query) + self_query_bias) * scale)
        mixed_one, back_one = attention(query_one, key_one, value_one, allowed_self)
        key_two = self.gather_row(low(dense(memory, all_.cross_key)))
        value_two = self.gather_row(low(dense(memory, all_.cross_value) + cross_value_bias))
        resid_one = (
            hidden.astype(jnp.float32) + dense(mixed_one, all_.self_output) + self_output_bias
        )
        first, normed_one, inverse_one = layer_norm(resid_one, first_gain, first_shift)
        first = first.astype(jnp.bfloat16)
        query_two = low((dense(first, all_.cross_query) + cross_query_bias) * scale)
        mixed_two, back_two = attention(query_two, key_two, value_two, allowed_cross)
        resid_two = (
            first.astype(jnp.float32) + dense(mixed_two, all_.cross_output) + cross_output_bias
        )
        second, normed_two, inverse_two = layer_norm(resid_two, second_gain, second_shift)
        self.kept = (
            hidden, memory, all_, mixed_one, first, normed_one, inverse_one, first_gain, back_one,
            mixed_two, back_two,
        )
        second = second.astype(jnp.bfloat16)
        inner = dense(second, all_.inner_weight) + inner_bias
        cumulative = 0.5 * (1.0 + lax.erf(inner * math.sqrt(0.5)))
        active = (inner * cumulative).astype(jnp.bfloat16)
        density = jnp.exp(-0.5 * inner * inner) * (1.0 / math.sqrt(2.0 * math.pi))
        slope = cumulative + inner * density
        resid_three = second.astype(jnp.float32) + dense(active, all_.outer_weight) + outer_bias
        final, normed_three, inverse_three = layer_norm(resid_three, third_gain, third_shift)

        keep = (target_ids > 0).astype(jnp.float32).reshape(-1, 1)
        upstream = out_grad.astype(jnp.float32) * keep
        grad_three, sums.third_gain, sums.third_shift = norm_back(
            upstream, normed_three, inverse_three, third_gain
        )
        grad_outer = grad_three.astype(jnp.bfloat16)
        sums.outer_bias = column_sum(grad_outer)
        grad_active = dense_back(grad_outer, all_.outer_weight)
        grad_inner = (grad_active * slope).astype(jnp.bfloat16)
        sums.inner_bias = column_sum(grad_inner)
        grad_second = grad_three + dense_back(grad_inner, all_.inner_weight)
        grad_two, sums.second_gain, sums.second_shift = norm_back(
            grad_second, normed_two, inverse_two, second_gain
        )
        return final, active, grad_outer, second, grad_inner, grad_two

    def _reduce(self, total):
        part = lax.psum_scatter(
            total.astype(jnp.bfloat16), "fsdp", scatter_dimension=0, tiled=True
        )
        return lax.psum(part, "seq").astype(jnp.float32)

    def back(self, g, sums, active, grad_outer, second, grad_inner, grad_two):
        (
            hidden, memory, all_, mixed_one, first, normed_one, inverse_one, first_gain, back_one,
            mixed_two, back_two,
        ) = self.kept
        shape = grad_two.shape

        def flat(array):
            return array.astype(jnp.bfloat16).reshape(shape)

        branch_two = grad_two.astype(jnp.bfloat16)
        sums.cross_output_bias = column_sum(branch_two)
        query_grad_two, key_sum, value_sum = back_two(
            flat(dense_back(branch_two, all_.cross_output))
        )
        key_grad_two = flat(self.scatter_row(key_sum))
        value_grad_two = flat(self.scatter_row(value_sum))
        query_grad_two = flat(query_grad_two)
        sums.cross_query_bias = column_sum(query_grad_two)
        sums.cross_value_bias = column_sum(value_grad_two)
        grad_first = grad_two + dense_back(query_grad_two, all_.cross_query)
        grad_one, sums.first_gain, sums.first_shift = norm_back(
            grad_first, normed_one, inverse_one, first_gain
        )
        branch_one = grad_one.astype(jnp.bfloat16)
        sums.self_output_bias = column_sum(branch_one)
        query_grad_one, key_sum, value_sum = back_one(
            flat(dense_back(branch_one, all_.self_output))
        )
        key_grad_one = flat(self.scatter_row(key_sum))
        value_grad_one = flat(self.scatter_row(value_sum))
        query_grad_one = flat(query_grad_one)
        sums.self_query_bias = column_sum(query_grad_one)
        sums.self_value_bias = column_sum(value_grad_one)
        g.outer_weight = self._reduce(dense_grad(active, grad_outer))
        g.inner_weight = self._reduce(dense_grad(second, grad_inner))
        g.cross_output = self._reduce(dense_grad(mixed_two, branch_two))
        g.cross_query = self._reduce(dense_grad(first, query_grad_two))
        g.cross_key = self._reduce(dense_grad(memory, key_grad_two))
        g.cross_value = self._reduce(dense_grad(memory, value_grad_two))
        g.self_output = self._reduce(dense_grad(mixed_one, branch_one))
        g.self_query = self._reduce(dense_grad(hidden, query_grad_one))
        g.self_key = self._reduce(dense_grad(hidden, key_grad_one))
        g.self_value = self._reduce(dense_grad(hidden, value_grad_one))
        input_grad = (
            grad_one
            + dense_back(query_grad_one, all_.self_query)
            + dense_back(key_grad_one, all_.self_key)
            + dense_back(value_grad_one, all_.self_value)
        )
        memory_grad = dense_back(key_grad_two, all_.cross_key) + dense_back(
            value_grad_two, all_.cross_value
        )
        return [self._reduce(v) for v in vectors_of(sums)], input_grad, memory_grad

    def gather_row(self, array):
        return lax.all_gather(array, "seq", axis=1, tiled=True)

    def scatter_row(self, array):
        return lax.psum_scatter(
            array.astype(jnp.bfloat16), "seq", scatter_dimension=1, tiled=True
        ).astype(jnp.float32)


def query_marks(ids):
    lanes = jnp.arange(PAIR)[None, :] % HEAD_DIM
    return jnp.where((lanes < SEGMENTS) & (ids[:, None] != lanes), masked_score, 0.0).astype(
        jnp.bfloat16
    )


def key_marks_of(ids):
    lanes = jnp.arange(PAIR)[None, :] % HEAD_DIM
    ones = (lanes >= SEGMENTS) & (lanes < SEGMENTS + 3)
    return (ones | (ids[:, None] == lanes)).astype(jnp.bfloat16)


def against(left, right):
    return lax.dot_general(
        left, right, (((1,), (1,)), ((), ())), preferred_element_type=jnp.float32
    )


def three(value):
    high = value.astype(jnp.bfloat16).astype(jnp.float32)
    rest = value - high
    middle = rest.astype(jnp.bfloat16).astype(jnp.float32)
    return high, middle, rest - middle


def place_three(lanes, base, value, other):
    high, middle, small = three(value)
    first = base + SEGMENTS
    return jnp.where(
        lanes == first,
        high,
        jnp.where(lanes == first + 1, middle, jnp.where(lanes == first + 2, small, other)),
    )


def plan(length, causal, later):
    half = length // 2
    result = []
    for tile in range(2):
        if not causal:
            result.append([(0, 2 * length, False)])
            continue
        ranges = [(0, half, False)] if tile else []
        ranges.append((tile * half, half, True))
        if later:
            ranges.append((length + tile * half, length - tile * half, False))
        result.append(ranges)
    return result


def each_plan(core, length, causal, run):
    if not causal:
        run(plan(length, False, False))
        return
    for later in range(2):
        @pl.when(core == later)
        def _():
            run(plan(length, True, bool(later)))


def forward_pair(core, causal, q_ref, k_ref, v_ref, qm_ref, km_ref, mixed_ref, qx_ref):
    length = q_ref.shape[0]

    def run(tiles):
        for head in range(2):
            base = HEAD_DIM * (1 - head)

            def own(lanes):
                return (lanes < HEAD_DIM) if head == 0 else (lanes >= HEAD_DIM)

            for tile, ranges in enumerate(tiles):
                rows = slice(tile * TILE, tile * TILE + TILE)
                lanes = lax.broadcasted_iota(jnp.int32, (TILE, PAIR), 1)
                q = jnp.where(own(lanes), q_ref[rows, :], qm_ref[rows, :])
                scores = []
                for start, size, diagonal in ranges:
                    keys = slice(start, start + size)
                    key_lanes = lax.broadcasted_iota(jnp.int32, (size, PAIR), 1)
                    k = jnp.where(own(key_lanes), k_ref[keys, :], km_ref[keys, :])
                    s = against(q, k)
                    if diagonal:
                        i = lax.broadcasted_iota(jnp.int32, s.shape, 0)
                        j = lax.broadcasted_iota(jnp.int32, s.shape, 1)
                        s = jnp.where(j <= i, s, masked_score)
                    scores.append(s)
                highest = functools.reduce(
                    jnp.maximum, [jnp.max(s, axis=1, keepdims=True) for s in scores]
                )
                out = jnp.zeros((TILE, PAIR), jnp.float32)
                for s, (start, size, _) in zip(scores, ranges):
                    keys = slice(start, start + size)
                    key_lanes = lax.broadcasted_iota(jnp.int32, (size, PAIR), 1)
                    v = jnp.where(own(key_lanes), v_ref[keys, :], jnp.ones((), jnp.bfloat16))
                    e = jnp.exp(s - highest).astype(jnp.bfloat16)
                    out = out + jnp.dot(e, v, preferred_element_type=jnp.float32)
                total = pltpu.roll(out, HEAD_DIM, 1)
                mixed = (out / total).astype(jnp.bfloat16)
                if head:
                    mixed = jnp.where(own(lanes), mixed, mixed_ref[rows, :])
                mixed_ref[rows, :] = mixed
                logsum = highest + jnp.log(out)
                qx = place_three(lanes, base, -logsum, q.astype(jnp.float32))
                qx_ref[head, rows, :] = qx.astype(jnp.bfloat16)

    each_plan(core, length, causal, run)


def backward_pair(
    core, causal, qx_ref, k_ref, v_ref, e_ref, o_ref, km_ref, dq_ref, dk_ref, dv_ref, dk_acc,
    dv_acc, dq_acc,
):
    length = e_ref.shape[0]
    scale = HEAD_DIM ** (-0.5)

    def run(tiles):
        dk_acc[...] = jnp.zeros_like(dk_acc)
        dv_acc[...] = jnp.zeros_like(dv_acc)
        for head in range(2):
            base = HEAD_DIM * (1 - head)

            def own(lanes):
                return (lanes < HEAD_DIM) if head == 0 else (lanes >= HEAD_DIM)

            for tile, ranges in enumerate(tiles):
                rows = slice(tile * TILE, tile * TILE + TILE)
                lanes = lax.broadcasted_iota(jnp.int32, (TILE, PAIR), 1)
                nothing = jnp.zeros((), jnp.bfloat16)
                qx = qx_ref[head, rows, :]
                q = jnp.where(own(lanes), qx, nothing)
                e = jnp.where(own(lanes), e_ref[rows, :], nothing)
                wide = e.astype(jnp.float32)
                delta = jnp.sum(wide * o_ref[rows, :].astype(jnp.float32), axis=1, keepdims=True)
                ex = place_three(lanes, base, -delta, wide).astype(jnp.bfloat16)
                dq = jnp.zeros((HEAD_DIM, TILE), jnp.float32)
                for start, size, diagonal in ranges:
                    keys = slice(start, start + size)
                    key_lanes = lax.broadcasted_iota(jnp.int32, (size, PAIR), 1)
                    k = jnp.where(own(key_lanes), k_ref[keys, :], km_ref[keys, :])
                    v = jnp.where(own(key_lanes), v_ref[keys, :], km_ref[keys, :])
                    p = jnp.exp(against(k, qx))
                    if diagonal:
                        j = lax.broadcasted_iota(jnp.int32, p.shape, 0)
                        i = lax.broadcasted_iota(jnp.int32, p.shape, 1)
                        p = jnp.where(j <= i, p, 0.0)
                    ds = (p * against(v, ex)).astype(jnp.bfloat16)
                    p = p.astype(jnp.bfloat16)
                    dv_acc[keys, :] += jnp.dot(p, e, preferred_element_type=jnp.float32)
                    dk_acc[keys, :] += jnp.dot(ds, q, preferred_element_type=jnp.float32)
                    kt = k_ref[keys, :].T[head * HEAD_DIM : (head + 1) * HEAD_DIM, :]
                    dq = dq + jnp.dot(kt, ds, preferred_element_type=jnp.float32)
                dq_acc[head * HEAD_DIM : (head + 1) * HEAD_DIM, rows] = dq
        dq_ref[...] = (dq_acc[...].T.astype(jnp.bfloat16) * jnp.bfloat16(scale)).astype(jnp.bfloat16)
        dk_ref[...] = dk_acc[...].astype(jnp.bfloat16)
        dv_ref[...] = dv_acc[...].astype(jnp.bfloat16)

    each_plan(core, length, causal, run)


def head_slice(array, start, span):
    piece = lax.dynamic_slice_in_dim(array, start, span, 2)
    return piece.reshape(array.shape[0], array.shape[1], 2, span // 2)


def plain_attend(query, keys, values, allowed):
    rows, length, width = query.shape
    span = 2 * HEAD_DIM
    pairs = width // span

    def one_pair(index, carry):
        mixed, logsum = carry
        start = index * span
        query_part = head_slice(query, start, span)
        key_part = head_slice(keys, start, span)
        value_part = head_slice(values, start, span)
        scores = jnp.einsum(
            "rqhe,rkhe->rhqk", query_part, key_part, preferred_element_type=jnp.float32
        )
        scores = jnp.where(allowed[:, None], scores, masked_score)
        highest = jnp.max(scores, axis=-1, keepdims=True)
        exponent = jnp.exp(scores - highest)
        total = jnp.sum(exponent, axis=-1, keepdims=True)
        probs = (exponent / total).astype(jnp.bfloat16)
        part = jnp.einsum("rhqk,rkhe->rqhe", probs, value_part, preferred_element_type=jnp.float32)
        mixed = lax.dynamic_update_slice_in_dim(mixed, part.reshape(rows, length, span), start, 2)
        logsum = lax.dynamic_update_slice_in_dim(
            logsum, (highest + jnp.log(total))[None, :, :, :, 0], index, 0
        )
        return (mixed, logsum)

    mixed = jnp.zeros((rows, length, width), jnp.float32)
    logsum = jnp.zeros((pairs, rows, 2, length), jnp.float32)
    return lax.fori_loop(0, pairs, one_pair, (mixed, logsum))


def plain_attend_back(query, keys, values, allowed, logsum, grad_mixed):
    rows, length, width = query.shape
    extent = keys.shape[1]
    span = 2 * HEAD_DIM
    pairs = width // span

    def one_pair(index, carry):
        start = index * span
        query_part = head_slice(query, start, span)
        key_part = head_slice(keys, start, span)
        value_part = head_slice(values, start, span)
        grad_part = head_slice(grad_mixed, start, span)
        scores = jnp.einsum(
            "rqhe,rkhe->rhqk", query_part, key_part, preferred_element_type=jnp.float32
        )
        scores = jnp.where(allowed[:, None], scores, masked_score)
        pair_logsum = lax.dynamic_index_in_dim(logsum, index, 0, keepdims=False)
        probs = jnp.exp(scores - pair_logsum[..., None])
        prob_grad = jnp.einsum(
            "rqhe,rkhe->rhqk", grad_part, value_part, preferred_element_type=jnp.float32
        )
        row_total = jnp.sum(probs * prob_grad, axis=-1, keepdims=True)
        score_grad = (probs * (prob_grad - row_total)).astype(jnp.bfloat16)
        query_grad = jnp.einsum(
            "rhqk,rkhe->rqhe", score_grad, key_part, preferred_element_type=jnp.float32
        )
        grad_query = lax.dynamic_update_slice_in_dim(
            carry[0], query_grad.reshape(rows, length, span), start, 2
        )
        probs_low = probs.astype(jnp.bfloat16)
        value_grad = jnp.einsum(
            "rhqk,rqhe->rkhe", probs_low, grad_part, preferred_element_type=jnp.float32
        )
        key_grad = jnp.einsum(
            "rhqk,rqhe->rkhe", score_grad, query_part, preferred_element_type=jnp.float32
        )
        grad_keys = lax.dynamic_update_slice_in_dim(
            carry[1], key_grad.reshape(rows, extent, span), start, 2
        )
        grad_values = lax.dynamic_update_slice_in_dim(
            carry[2], value_grad.reshape(rows, extent, span), start, 2
        )
        return (grad_query, grad_keys, grad_values)

    start_query = jnp.zeros((rows, length, width), jnp.float32)
    start_keys = jnp.zeros((rows, extent, width), jnp.float32)
    return lax.fori_loop(0, pairs, one_pair, (start_query, start_keys, start_keys))


def body(staged, hidden_in, memory, target_ids, memory_ids, out_grad, *weights):
    w = Weights(*weights)
    rows, length, width = hidden_in.shape
    staged = staged and (rows, length, width) == (1, 2 * TILE, 768)
    net = Staged() if staged else Plain()
    all_ = SimpleNamespace()
    tokens = rows * length
    flat_in = hidden_in.reshape(tokens, width)
    flat_memory = memory.reshape(tokens, width)

    def low(array):
        return array.astype(jnp.bfloat16).reshape(rows, length, width)

    sums = SimpleNamespace()
    layer_out, *states = net.front(
        w, all_, sums, flat_in, flat_memory, target_ids, memory_ids,
        out_grad.reshape(tokens, width),
    )
    g = SimpleNamespace()
    (
        g.self_query_bias, g.self_value_bias, g.self_output_bias, g.first_gain, g.first_shift,
        g.cross_query_bias, g.cross_value_bias, g.cross_output_bias, g.second_gain,
        g.second_shift, g.inner_bias, g.outer_bias, g.third_gain, g.third_shift,
    ), input_grad, memory_grad = net.back(g, sums, *states)
    return (low(layer_out), low(input_grad), low(memory_grad), *Weights(**vars(g)))


def solution(mesh):
    staged = mesh.shape["fsdp"] == 16 and mesh.shape["seq"] == 2
    row, ids = P("fsdp", "seq", None), P("fsdp", "seq")
    matrix, vector = P("fsdp", None), P("fsdp")
    weights = Weights(
        matrix, vector, matrix, matrix, vector, matrix, vector, vector, vector, matrix, vector,
        matrix, matrix, vector, matrix, vector, vector, vector, matrix, vector, matrix, vector,
        vector, vector,
    )
    return jax.shard_map(
        functools.partial(body, staged),
        mesh=mesh,
        in_specs=(row, row, ids, ids, row, *weights),
        out_specs=(row, row, row, *weights),
        check_vma=False,
    )
```

```python
import functools
import math
from types import SimpleNamespace
from typing import NamedTuple

import jax
import jax.numpy as jnp
from jax import lax
from jax.experimental import pallas as pl
from jax.experimental.pallas import tpu as pltpu
from jax.sharding import PartitionSpec as P

HEAD_DIM = 64
PAIR = 2 * HEAD_DIM
SEGMENTS = 5
TILE = 256
eps_norm = 1e-05
masked_score = -1e30


class Weights(NamedTuple):
    self_query: jax.Array
    self_query_bias: jax.Array
    self_key: jax.Array
    self_value: jax.Array
    self_value_bias: jax.Array
    self_output: jax.Array
    self_output_bias: jax.Array
    first_gain: jax.Array
    first_shift: jax.Array
    cross_query: jax.Array
    cross_query_bias: jax.Array
    cross_key: jax.Array
    cross_value: jax.Array
    cross_value_bias: jax.Array
    cross_output: jax.Array
    cross_output_bias: jax.Array
    second_gain: jax.Array
    second_shift: jax.Array
    inner_weight: jax.Array
    inner_bias: jax.Array
    outer_weight: jax.Array
    outer_bias: jax.Array
    third_gain: jax.Array
    third_shift: jax.Array


def split_vectors(w):
    return [array for array in w if array.ndim == 1]


def vectors_of(sums):
    return [
        sums.self_query_bias, sums.self_value_bias, sums.self_output_bias, sums.first_gain,
        sums.first_shift, sums.cross_query_bias, sums.cross_value_bias, sums.cross_output_bias,
        sums.second_gain, sums.second_shift, sums.inner_bias, sums.outer_bias, sums.third_gain,
        sums.third_shift,
    ]


def dense(left, right):
    return jnp.dot(left, right, preferred_element_type=jnp.float32)


def dense_back(left, right):
    return lax.dot_general(
        left, right, (((1,), (1,)), ((), ())), preferred_element_type=jnp.float32
    )


def dense_grad(left, right):
    return lax.dot_general(
        left, right, (((0,), (0,)), ((), ())), preferred_element_type=jnp.float32
    )


def column_sum(values):
    return jnp.sum(values, axis=0, dtype=jnp.float32)


def layer_norm(resid, gain, shift):
    center = resid - jnp.mean(resid, axis=-1, keepdims=True)
    spread = jnp.mean(center * center, axis=-1, keepdims=True)
    inverse = lax.rsqrt(spread + eps_norm)
    normed = center * inverse
    return (normed * gain + shift, normed, inverse)


def norm_back(upstream, normed, inverse, gain):
    scaled = upstream * gain
    plain_mean = jnp.mean(scaled, axis=-1, keepdims=True)
    cross_mean = jnp.mean(scaled * normed, axis=-1, keepdims=True)
    result = inverse * (scaled - plain_mean - normed * cross_mean)
    return (result, jnp.sum(upstream * normed, axis=0), jnp.sum(upstream, axis=0))


MESH = pl.DeviceIdType.MESH


class Spot:
    def __init__(self):
        f, c = lax.axis_index("fsdp"), lax.axis_index("seq")
        self.c, self.z, self.plane = c, f // 4, f % 4
        self.other = (f, 1 - c)
        self.by_x = ((f // 2) * 2 + (1 - f % 2), c)
        self.by_y = (self.z * 4 + (self.plane + 2) % 4, c)
        self.first = (jnp.where(c == 0, self.by_x[0], self.by_y[0]), c)
        self.second = (jnp.where(c == 0, self.by_y[0], self.by_x[0]), c)
        self.plane_x = self.by_x[0] % 4
        self.plane_y = self.by_y[0] % 4
        self.plane_first = jnp.where(c == 0, self.plane_x, self.plane_y)
        self.plane_second = jnp.where(c == 0, self.plane_y, self.plane_x)
        self.plane_both = 3 - self.plane

    def at_z(self, k):
        z = (self.z + k) % 4
        return z, (z * 4 + self.plane, self.c)

    def meet(self):
        barrier = pltpu.get_barrier_semaphore()
        partners = [self.other, self.by_x, self.by_y] + [self.at_z(k)[1] for k in (1, 2, 3)]
        for partner in partners:
            pl.semaphore_signal(barrier, inc=1, device_id=partner, device_id_type=MESH)
        pl.semaphore_wait(barrier, len(partners))


class Gather:
    sems = 31
    order = (0, 1, 3, 2)

    def __init__(self, spot, shards, wholes, send, recv, local, base):
        self.spot, self.shards, self.wholes = spot, shards, wholes
        self.send, self.recv, self.local, self.base = send, recv, local, base
        self.all = range(len(shards))

    def _columns(self, j):
        half = self.wholes[j].shape[3] // 2
        return pl.ds(pl.multiple_of(self.spot.c * half, 128), half)

    def _view(self, j, p, plane):
        return self.wholes[j].at[(self.spot.z + 4 - p) % 4, plane, :, self._columns(j)]

    def _copy(self, j, n, source, target, partner):
        return pltpu.make_async_remote_copy(
            source, target, self.send.at[self.base + j, n], self.recv.at[self.base + j, n],
            device_id=partner, device_id_type=MESH,
        )

    def _z(self, j, k):
        spot = self.spot
        source = self.shards[j].at[:, self._columns(j)]
        return self._copy(j, k - 1, source, self._view(j, 0, spot.plane), spot.at_z(k)[1])

    def _near(self, j, p, way):
        spot = self.spot
        view = self._view(j, p, spot.plane)
        source = view if p else self.shards[j].at[:, self._columns(j)]
        return self._copy(j, 3 + 2 * p + way, source, view, spot.by_y if way else spot.by_x)

    def _far(self, j, p):
        view = self._view(j, p, self.spot.plane_first)
        return self._copy(j, 11 + p, view, view, self.spot.second)

    def _swap(self, j, p, n):
        spot = self.spot
        plane = (spot.plane, spot.plane_x, spot.plane_y, spot.plane_both)[n]
        view = self._view(j, p, plane)
        return self._copy(j, 15 + 4 * p + n, view, view, spot.other)

    def _locals(self):
        return [
            pltpu.make_async_copy(
                self.shards[j], self.wholes[j].at[self.spot.z, self.spot.plane],
                self.local.at[self.base + j],
            )
            for j in self.all
        ]

    def start(self):
        for k in self.order[1:2]:
            for j in self.all:
                self._z(j, k).start()
        for j in self.all:
            for way in range(2):
                self._near(j, 0, way).start()
        for k in self.order[2:]:
            for j in self.all:
                self._z(j, k).start()
        for copy in self._locals():
            copy.start()

    def advance(self, i):
        if i < 4:
            p = self.order[i]
            for j in self.all:
                self._z(j, p).wait_recv()
                self._near(j, p, 0).start()
                self._near(j, p, 1).start()
                self._swap(j, p, 0).start()
        if 1 <= i < 5:
            p = self.order[i - 1]
            for j in self.all:
                self._near(j, p, 0).wait_recv()
                self._near(j, p, 1).wait_recv()
                self._far(j, p).start()
                self._swap(j, p, 1).start()
                self._swap(j, p, 2).start()
        if 2 <= i < 6:
            p = self.order[i - 2]
            for j in self.all:
                self._far(j, p).wait_recv()
                self._swap(j, p, 3).start()

    def finish(self):
        for copy in self._locals():
            copy.wait()
        for j in self.all:
            for p in self.order:
                if p:
                    self._z(j, p).wait_send()
                self._near(j, p, 0).wait_send()
                self._near(j, p, 1).wait_send()
                self._far(j, p).wait_send()
                for n in range(0 if p else 1, 4):
                    self._swap(j, p, n).wait()
class Reduce:
    sems = 21
    order = (2, 3, 1, 0)

    def __init__(self, spot, outs, give, mine, there, far, near, line, send, recv):
        self.spot, self.outs, self.give = spot, outs, give
        self.mine, self.there, self.far, self.near, self.line = mine, there, far, near, line
        self.send, self.recv = send, recv
        self.all = range(len(outs))

    @staticmethod
    def scratch(shapes, dtypes, shared=0):
        def buffers(*lead):
            return [pltpu.VMEM((*lead, r, w // 2), d) for (r, w), d in zip(shapes, dtypes)]

        n = len(shapes)
        return (
            buffers(4, 4)[: n - shared] + buffers(4, 4) + buffers(4, 4) + buffers(4)
            + buffers(4, 2) + buffers(3) + [pltpu.SemaphoreType.DMA((n, Reduce.sems))] * 2
        )

    @staticmethod
    def unpack(spot, outs, refs, shared=0):
        n = len(outs)
        give, refs = list(refs[: n - shared]), refs[n - shared :]
        for i in range(shared):
            half = outs[n - shared + i].shape[1] // 2
            give.append(give[n - shared - 1].at[:, :, :, pl.ds(i * half, half)])
        groups = [refs[i * n : (i + 1) * n] for i in range(5)]
        return Reduce(spot, outs, give, *groups, *refs[5 * n : 5 * n + 2])

    def free(self, j):
        for p in self.order:
            self._cross(j, p).wait_send()
        self.freed = (j,)

    freed = ()

    def part(self, js):
        def some(items):
            return [items[j] for j in js]

        lists = (self.outs, self.give, self.mine, self.there, self.far, self.near, self.line)
        chosen = Reduce(self.spot, *[some(items) for items in lists], self.send, self.recv)
        chosen.base = js[0]
        return chosen

    base = 0

    def put(self, j, core_of, value, columns=None, z_first=0):
        target = self.give[j] if core_of else self.mine[j]
        rows = target.shape[2]
        block = 4 * rows
        columns = slice(None) if columns is None else columns
        for i in range(value.shape[0] // block):
            p = (z_first + i + 4 - self.spot.z) % 4
            piece = value[i * block : (i + 1) * block]
            target[p, :, :, columns] = piece.reshape(4, rows, -1).astype(target.dtype)

    def _columns(self, j, core):
        half = self.outs[j].shape[1] // 2
        return pl.ds(pl.multiple_of(core * half, 128), half)

    def _copy(self, j, n, source, target, partner):
        return pltpu.make_async_remote_copy(
            source, target, self.send.at[self.base + j, n], self.recv.at[self.base + j, n],
            device_id=partner, device_id_type=MESH,
        )

    def _cross(self, j, p):
        return self._copy(j, p, self.give[j].at[p], self.there[j].at[p], self.spot.other)

    def _far(self, j, p):
        spot = self.spot
        return self._copy(
            j, 4 + p, self.mine[j].at[p, spot.plane_both], self.far[j].at[p], spot.first
        )

    def _near(self, j, p, way):
        spot = self.spot
        plane, partner = (spot.plane_y, spot.by_y) if way else (spot.plane_x, spot.by_x)
        return self._copy(
            j, 8 + 2 * p + way, self.mine[j].at[p, plane], self.near[j].at[p, way], partner
        )

    def _line(self, j, p):
        spot = self.spot
        return self._copy(
            j, 16 + p, self.mine[j].at[p, spot.plane], self.line[j].at[p - 1], spot.at_z(p)[1]
        )

    def _last(self, j):
        view = self.outs[j].at[:, self._columns(j, self.spot.c)]
        return self._copy(j, 20, view, view, self.spot.other)

    def start(self, j):
        for p in self.order:
            self._cross(j, p).start()

    def _sum(self, j, p, plane, *others):
        total = self.mine[j][p, plane].astype(jnp.float32)
        total = total + self.there[j][p, plane].astype(jnp.float32)
        for other in others:
            total = total + other.astype(jnp.float32)
        return total

    def _store(self, j, p, plane, total):
        self.mine[j][p, plane] = total.astype(self.mine[j].dtype)

    def advance(self, i):
        spot = self.spot
        if i < 4:
            p = self.order[i]
            for j in self.all:
                self._cross(j, p).wait_recv()
                self._store(j, p, spot.plane_both, self._sum(j, p, spot.plane_both))
                self._far(j, p).start()
        if 0 <= i - 1 < 4:
            p = self.order[i - 1]
            for j in self.all:
                self._store(j, p, spot.plane_first, self._sum(j, p, spot.plane_first))
                self._far(j, p).wait_recv()
                self._store(
                    j, p, spot.plane_second, self._sum(j, p, spot.plane_second, self.far[j][p])
                )
                self._near(j, p, 0).start()
                self._near(j, p, 1).start()
        if 0 <= i - 2 < 4:
            p = self.order[i - 2]
            for j in self.all:
                self._near(j, p, 0).wait_recv()
                self._near(j, p, 1).wait_recv()
                total = self._sum(j, p, spot.plane, self.near[j][p, 0], self.near[j][p, 1])
                if p:
                    self._store(j, p, spot.plane, total)
                    self._line(j, p).start()
                else:
                    for k in (1, 2, 3):
                        self._line(j, k).wait_recv()
                        total = total + self.line[j][k - 1].astype(jnp.float32)
                    self.outs[j][:, self._columns(j, spot.c)] = total
                    self._last(j).start()

    def finish(self):
        for j in self.all:
            for p in self.order:
                if j not in self.freed:
                    self._cross(j, p).wait_send()
                self._far(j, p).wait_send()
                self._near(j, p, 0).wait_send()
                self._near(j, p, 1).wait_send()
                if p:
                    self._line(j, p).wait_send()
            self._last(j).wait()


def gather_kernel(groups, *refs):
    counts = [len(group) for group in groups]
    count = sum(counts)
    shards, (x_ref, memory_ref, qm_ref, own_km_one, own_km_two, grad_ref), refs = (
        refs[:count], refs[count : count + 6], refs[count + 6 :],
    )
    wholes, (lines_ref, sums_ref), results, refs = (
        refs[:count], refs[count : count + 2], refs[count + 2 : count + 22], refs[count + 22 :],
    )
    kept, refs = refs[:20], refs[20:]
    (
        mixed_one, qx_one, first, normed_one, inverse_one, mixed_two, qx_two, second, active,
        grad_inner, k_one, v_one, k_two, v_two, km_one, km_two, layer_out, grad_outer, grad_two,
        branch_two,
    ) = kept
    (
        normed_two, inverse_two, slope, outer, query, weight, table, send, recv, local, weight_sem,
        send_row, recv_row, out_sem,
    ) = refs
    spot = Spot()
    length, width = x_ref.shape
    scale = HEAD_DIM ** (-0.5)
    gathers, start = [], 0
    for n in counts:
        chosen = slice(start, start + n)
        gathers.append(Gather(spot, shards[chosen], wholes[chosen], send, recv, local, start))
        start += n
    one, two, three_, four = gathers

    def fetch(i):
        return pltpu.make_async_copy(wholes[i], weight.at[i if i < 3 else i - 1], weight_sem.at[i])

    def matrix(i):
        return weight[i if i < 3 else i - 1].reshape(width, width)

    def line(i):
        return lines_ref[i : i + 1, :]

    def cross(i, ref):
        return pltpu.make_async_remote_copy(
            ref.at[pl.ds(0, length)], ref.at[pl.ds(length, length)], send_row.at[i],
            recv_row.at[i], device_id=spot.other, device_id_type=MESH,
        )

    def leave(i):
        return pltpu.make_async_copy(kept[i], results[i], out_sem.at[i])

    def norm(total, gain, shift, low, normed, inverse):
        center = total - jnp.mean(total, axis=-1, keepdims=True)
        spread = jnp.mean(center * center, axis=-1, keepdims=True)
        factor = lax.rsqrt(spread + eps_norm)
        unit = center * factor
        normed[...] = unit
        inverse[...] = jnp.broadcast_to(factor, inverse.shape)
        low[...] = (unit * gain + shift).astype(jnp.bfloat16)

    def pairs(first_pair, last_pair, causal, k, v, km, mixed, qx):
        def one_pair(i, carry):
            columns = pl.ds(pl.multiple_of(i * PAIR, PAIR), PAIR)
            forward_pair(
                spot.c, causal, query.at[:, columns], k.at[:, columns], v.at[:, columns], qm_ref,
                km, mixed.at[:, columns], qx.at[pl.ds(2 * i, 2)],
            )
            return carry

        lax.fori_loop(first_pair, last_pair, one_pair, 0)

    spot.meet()
    one.start()
    two.start()
    km_one[0:length, :] = own_km_one[...]
    km_two[0:length, :] = own_km_two[...]
    marks = [cross(0, km_one), cross(1, km_two)]
    for copy in marks:
        copy.start()
    one.advance(1)
    one.advance(2)
    one.advance(3)
    one.advance(4)
    one.advance(5)
    one.finish()
    three_.start()
    for i in range(3):
        fetch(i).start()
    vector_copy = pltpu.make_async_copy(wholes[3], table, weight_sem.at[3])
    vector_copy.start()
    vector_copy.wait()
    lines = jnp.zeros(lines_ref.shape, jnp.float32)
    bias = jnp.zeros((8, width), jnp.float32)
    for f in range(16):
        i = lax.broadcasted_iota(jnp.int32, (128, width), 0)
        j = lax.broadcasted_iota(jnp.int32, (128, width), 1)
        at = ((i < 48) & (j == i + 48 * f)).astype(jnp.bfloat16)
        piece = table[f // 4, f % 4, :, 0:128].astype(jnp.bfloat16)
        lines = lines + dense(piece, at)
        piece = [table[q, f // 4, 13 + f % 4 : 14 + f % 4, 0:128] for q in range(4)]
        bias = bias + dense(jnp.concatenate(piece + piece).astype(jnp.bfloat16), at)
    lines_ref[...] = lines

    fetch(0).wait()
    fetch(1).wait()
    fetch(2).wait()
    k_one[0:length, :] = dense(x_ref[...], matrix(1)).astype(jnp.bfloat16)
    row_one = [cross(2, k_one), cross(3, v_one)]
    row_one[0].start()
    v_one[0:length, :] = (dense(x_ref[...], matrix(2)) + line(1)).astype(jnp.bfloat16)
    row_one[1].start()
    query[...] = ((dense(x_ref[...], matrix(0)) + line(0)) * scale).astype(jnp.bfloat16)
    two.advance(1)
    for copy in marks:
        copy.wait()
    for copy in row_one:
        copy.wait()
    leaving = [leave(i) for i in (10, 11, 14, 15)]
    for copy in leaving:
        copy.start()
    pairs(0, 2, True, k_one, v_one, km_one, mixed_one, qx_one)
    two.advance(2)
    pairs(2, 4, True, k_one, v_one, km_one, mixed_one, qx_one)
    two.advance(3)
    pairs(4, 6, True, k_one, v_one, km_one, mixed_one, qx_one)
    for i in (0, 1):
        leaving.append(leave(i))
        leaving[-1].start()
    two.advance(4)
    three_.advance(1)
    four.start()
    two.advance(5)
    two.finish()
    for i in range(4, 9):
        fetch(i).start()
    fetch(4).wait()
    k_two[0:length, :] = dense(memory_ref[...], matrix(4)).astype(jnp.bfloat16)
    row_two = [cross(4, k_two), cross(5, v_two)]
    row_two[0].start()
    fetch(5).wait()
    v_two[0:length, :] = (dense(memory_ref[...], matrix(5)) + line(6)).astype(jnp.bfloat16)
    row_two[1].start()
    three_.advance(2)
    fetch(6).wait()
    total = x_ref[...].astype(jnp.float32) + dense(mixed_one[...], matrix(6)) + line(2)
    norm(total, line(3), line(4), first, normed_one, inverse_one)
    fetch(7).wait()
    query[...] = ((dense(first[...], matrix(7)) + line(5)) * scale).astype(jnp.bfloat16)
    three_.advance(3)
    for copy in row_two:
        copy.wait()
    for i in (2, 3, 4, 12, 13):
        leaving.append(leave(i))
        leaving[-1].start()
    pairs(0, 2, False, k_two, v_two, km_two, mixed_two, qx_two)
    three_.advance(4)
    four.advance(1)
    pairs(2, 4, False, k_two, v_two, km_two, mixed_two, qx_two)
    three_.advance(5)
    four.advance(2)
    pairs(4, 6, False, k_two, v_two, km_two, mixed_two, qx_two)
    three_.finish()
    chunks = [slice(q * width, (q + 1) * width) for q in range(4)]
    inner = [
        pltpu.make_async_copy(wholes[9].at[:, :, :, chunks[q]], weight.at[q], weight_sem.at[q])
        for q in range(4)
    ]
    for copy in inner:
        copy.start()
    four.advance(3)
    fetch(8).wait()
    total = first[...].astype(jnp.float32) + dense(mixed_two[...], matrix(8)) + line(7)
    norm(total, line(8), line(9), second, normed_two, inverse_two)
    for i in (5, 6, 7):
        leaving.append(leave(i))
        leaving[-1].start()
    four.advance(4)
    for q in range(4):
        inner[q].wait()
        value = dense(second[...], weight[q].reshape(width, width)) + bias[q : q + 1, :]
        cumulative = 0.5 * (1.0 + lax.erf(value * math.sqrt(0.5)))
        active[:, chunks[q]] = (value * cumulative).astype(jnp.bfloat16)
        density = jnp.exp(-0.5 * value * value) * (1.0 / math.sqrt(2.0 * math.pi))
        slope[:, chunks[q]] = cumulative + value * density
        if q == 0:
            four.advance(5)
    four.finish()
    last = pltpu.make_async_copy(wholes[10], outer, weight_sem.at[4])
    last.start()
    leaving.append(leave(8))
    leaving[-1].start()

    def add_row(i, values):
        sums_ref[i : i + 1, :] = jnp.sum(values.astype(jnp.float32), axis=0, keepdims=True)

    def back(grad, normed, factor, gain):
        scaled = grad * gain
        plain_mean = jnp.mean(scaled, axis=-1, keepdims=True)
        cross_mean = jnp.mean(scaled * normed, axis=-1, keepdims=True)
        return factor * (scaled - plain_mean - normed * cross_mean)

    last.wait()
    total = second[...].astype(jnp.float32) + line(10)
    for q in range(4):
        total = total + dense(active[:, chunks[q]], outer[q].reshape(width, width))
    center = total - jnp.mean(total, axis=-1, keepdims=True)
    factor = lax.rsqrt(jnp.mean(center * center, axis=-1, keepdims=True) + eps_norm)
    unit = center * factor
    layer_out[...] = (unit * line(11) + line(12)).astype(jnp.bfloat16)
    keep = jnp.where(qm_ref[:, 0:1].astype(jnp.float32) < 0.0, 1.0, 0.0)
    upstream = grad_ref[...].astype(jnp.float32) * keep
    add_row(0, upstream * unit)
    add_row(1, upstream)
    grad_three = back(upstream, unit, factor, line(11))
    grad_outer[...] = grad_three.astype(jnp.bfloat16)
    add_row(2, grad_outer[...])
    for i in (16, 17):
        leaving.append(leave(i))
        leaving[-1].start()
    grad = grad_three
    for q in range(4):
        value = dense_back(grad_outer[...], outer[q].reshape(width, width))
        piece = (value * slope[:, chunks[q]]).astype(jnp.bfloat16)
        grad_inner[:, chunks[q]] = piece
        add_row(8 + q, piece)
        grad = grad + dense_back(piece, weight[q].reshape(width, width))
    leaving.append(leave(9))
    leaving[-1].start()
    unit = normed_two[...]
    add_row(3, grad * unit)
    add_row(4, grad)
    grad_two[...] = back(grad, unit, inverse_two[:, 0:1], line(8))
    branch_two[...] = grad_two[...].astype(jnp.bfloat16)
    for i in (18, 19):
        leaving.append(leave(i))
        leaving[-1].start()
    add_row(5, branch_two[...])
    for copy in leaving:
        copy.wait()


def back_kernel(*refs):
    active, grad_outer, second, grad_inner = refs[:4]
    branch_two, grad_two, normed_one, inverse_one, lines_ref, first, memory = refs[4:11]
    attends = (refs[11:16], refs[16:21])
    wholes = refs[21:24]
    outs, refs = refs[24:30], refs[30:]
    (grad_one, branch_one, dq_two, kg_two, vg_two, dq_one, kg_one, vg_one, sums_ref), refs = (
        refs[:9], refs[9:],
    )
    (
        wide, narrow, qx, k, v, mixed, km, e, dk, dv, dk_there, dv_there, weight, dk_acc, dv_acc,
        dq_acc, sem, send_row, recv_row,
    ) = refs[-19:]
    spot = Spot()
    reduce = Reduce.unpack(spot, outs, refs[:-19], 4)
    length, width = branch_two.shape
    half = width // 2

    def load(source, target, i):
        return pltpu.make_async_copy(source, target, sem.at[i])

    def load_attend(i):
        targets = (qx, k, v, mixed, km)
        return [load(source, target, 4 + n) for n, (source, target) in enumerate(zip(attends[i], targets))]

    early = [
        load(active, wide.at[0], 0), load(grad_outer, narrow.at[0], 1),
        load(second, narrow.at[1], 2), load(grad_inner, wide.at[1], 3),
    ]
    for copy in early:
        copy.start()
    attend = load_attend(0)
    matrices = [load(wholes[i], weight.at[i], 9 + i) for i in range(3)]
    for copy in attend + matrices:
        copy.start()
    spot.meet()
    for copy in early[:2]:
        copy.wait()
    for core_of in (1, 0):
        start = pl.multiple_of((spot.c if core_of == 0 else 1 - spot.c) * half, 128)
        right = narrow[0, :, pl.ds(start, half)]
        for chunk in range(4):
            left = wide[0, :, chunk * width : (chunk + 1) * width]
            reduce.put(0, core_of, dense_grad(left, right), None, chunk)
        if core_of:
            reduce.start(0)
    for copy in early[2:]:
        copy.wait()
    for core_of in (1, 0):
        for chunk in range(4):
            base = (spot.c if core_of == 0 else 1 - spot.c) * 2 * width + chunk * half
            right = wide[1, :, pl.ds(pl.multiple_of(base, 128), half)]
            columns = slice(chunk * half, (chunk + 1) * half)
            reduce.put(1, core_of, dense_grad(narrow[1], right), columns)
        if core_of:
            reduce.start(1)
    ffn, others = reduce.part((0, 1)), reduce.part((2, 3, 4, 5))

    def multiply(j, left, right):
        for core_of in (1, 0):
            start = pl.multiple_of((spot.c if core_of == 0 else 1 - spot.c) * half, 128)
            reduce.put(j, core_of, dense_grad(left[...], right[:, pl.ds(start, half)]))
            if core_of:
                reduce.start(j)

    def matrix(i):
        return weight[i].reshape(width, width)

    def pairs(first_pair, last_pair, causal, dq):
        def one_pair(i, carry):
            columns = pl.ds(pl.multiple_of(i * PAIR, PAIR), PAIR)
            backward_pair(
                spot.c, causal, qx.at[pl.ds(2 * i, 2)], k.at[:, columns], v.at[:, columns],
                e.at[:, columns], mixed.at[:, columns], km, dq.at[:, columns], dk.at[:, columns],
                dv.at[:, columns], dk_acc, dv_acc, dq_acc,
            )
            return carry

        lax.fori_loop(first_pair, last_pair, one_pair, 0)

    def cross(i):
        source, target = ((dk, dk_there), (dv, dv_there))[i % 2]
        return pltpu.make_async_remote_copy(
            source.at[pl.ds(length, length)], target, send_row.at[i], recv_row.at[i],
            device_id=spot.other, device_id_type=MESH,
        )

    def left(own, out, n):
        return load(own.at[pl.ds(0, length)], out, 12 + n)

    def join(i, kg, vg):
        for n, (own, there, out) in enumerate(((dk, dk_there, kg), (dv, dv_there, vg))):
            cross(2 * i + n).wait()
            total = own[0:length, :].astype(jnp.float32) + there[...].astype(jnp.float32)
            own[0:length, :] = total.astype(jnp.bfloat16)
            left(own, out, n).start()

    def add_row(i, values):
        sums_ref[i : i + 1, :] = jnp.sum(values.astype(jnp.float32), axis=0, keepdims=True)

    factors = [load(first, narrow.at[0], 1), load(memory, narrow.at[1], 2)]
    for copy in factors:
        copy.start()
    ffn.advance(0)
    for copy in attend + matrices:
        copy.wait()
    e[...] = dense_back(branch_two[...], matrix(0)).astype(jnp.bfloat16)
    pairs(0, 2, False, dq_two)
    ffn.advance(1)
    for copy in factors:
        copy.wait()
    reduce.free(1)
    multiply(2, mixed, branch_two)
    pairs(2, 4, False, dq_two)
    ffn.advance(2)
    pairs(4, 6, False, dq_two)
    cross(0).start()
    cross(1).start()
    attend = load_attend(1)
    for copy in attend:
        copy.start()
    ffn.advance(3)
    multiply(3, narrow.at[0], dq_two)
    join(0, kg_two, vg_two)
    key_part, value_part = dk.at[pl.ds(0, length)], dv.at[pl.ds(0, length)]
    multiply(4, narrow.at[1], key_part)
    multiply(5, narrow.at[1], value_part)
    add_row(4, value_part[...])
    grad = grad_two[...] + dense_back(dq_two[...], matrix(1))
    normed = normed_one[...]
    add_row(0, grad * normed)
    add_row(1, grad)
    scaled = grad * lines_ref[3:4, :]
    plain_mean = jnp.mean(scaled, axis=-1, keepdims=True)
    cross_mean = jnp.mean(scaled * normed, axis=-1, keepdims=True)
    grad_one[...] = inverse_one[:, 0:1] * (scaled - plain_mean - normed * cross_mean)
    branch_one[...] = grad_one[...].astype(jnp.bfloat16)
    ffn.advance(4)
    others.advance(0)
    e[...] = dense_back(branch_one[...], matrix(2)).astype(jnp.bfloat16)
    for copy in attend:
        copy.wait()
    left(dk, kg_two, 0).wait()
    left(dv, vg_two, 1).wait()
    pairs(0, 2, True, dq_one)
    ffn.advance(5)
    others.advance(1)
    pairs(2, 4, True, dq_one)
    others.advance(2)
    pairs(4, 6, True, dq_one)
    cross(2).start()
    cross(3).start()
    others.advance(3)
    add_row(2, branch_one[...])
    add_row(3, dq_two[...])
    add_row(5, dq_one[...])
    others.advance(4)
    join(1, kg_one, vg_one)
    add_row(6, value_part[...])
    others.advance(5)
    reduce.finish()
    left(dk, kg_one, 0).wait()
    left(dv, vg_one, 1).wait()


def reduce_kernel(count, *refs):
    factors, refs = refs[: 2 * count], refs[2 * count :]
    (table, grad_one, key_two, value_two), wholes, refs = refs[:4], refs[4:9], refs[9:]
    outs, (input_ref, memory_ref), refs = (
        refs[: count + 1], refs[count + 1 : count + 3], refs[count + 3 :],
    )
    weight, refs = refs[-1], refs[:-1]
    sem, refs = refs[-1], refs[:-1]
    spot = Spot()
    reduce = Reduce.unpack(spot, outs, refs)
    width = factors[0].shape[1]
    half = width // 2
    copies = [pltpu.make_async_copy(wholes[i], weight.at[i], sem.at[i]) for i in range(5)]
    for copy in copies:
        copy.start()
    spot.meet()
    for core_of in (1, 0):
        start = pl.multiple_of((spot.c if core_of == 0 else 1 - spot.c) * 128, 128)
        for z in range(4):
            p = (z + 4 - spot.z) % 4
            target = reduce.give[count] if core_of else reduce.mine[count]
            target[p] = table[z, :, :, pl.ds(start, 128)]
    reduce.start(count)
    for core_of in (1, 0):
        start = pl.multiple_of((spot.c if core_of == 0 else 1 - spot.c) * half, 128)
        for i in range(count):
            right = factors[2 * i + 1][:, pl.ds(start, half)]
            reduce.put(i, core_of, dense_grad(factors[2 * i][...], right))
            if core_of:
                reduce.start(i)
    reduce.advance(0)
    for copy in copies:
        copy.wait()

    def product(i, factor):
        return dense_back(factor[...], weight[i].reshape(width, width))

    total = grad_one[...] + product(0, factors[-5])
    reduce.advance(1)
    total = total + product(1, factors[-3]) + product(2, factors[-1])
    input_ref[...] = total.astype(jnp.bfloat16)
    reduce.advance(2)
    memory_ref[...] = (product(3, key_two) + product(4, value_two)).astype(jnp.bfloat16)
    reduce.advance(3)
    reduce.advance(4)
    reduce.advance(5)
    reduce.finish()


def hand_on(*refs):
    count = len(refs) // 2
    for source, target in zip(refs[:count], refs[count:]):
        target[...] = source[...]


class Staged:
    staged = True

    def __init__(self):
        self.c = lax.axis_index("seq")
        self.parts = []

    def swap(self, array):
        pairs = [(f * 2 + c, f * 2 + 1 - c) for f in range(16) for c in range(2)]
        return lax.ppermute(array, ("fsdp", "seq"), pairs)

    def front(self, w, all_, sums, hidden, memory, target_ids, memory_ids, out_grad):
        vectors = split_vectors(w)
        narrow = [v for v in vectors if v.shape[0] == 48]
        (wide,) = [v for v in vectors if v.shape[0] != 48]
        table = jnp.concatenate([jnp.stack(narrow), wide.reshape(-1, 48)]).astype(jnp.float32)
        table = jnp.pad(table, ((0, 24 - table.shape[0]), (0, 256 - 48)))
        groups = (
            (w.self_query, w.self_key, w.self_value, table),
            (w.cross_key, w.cross_value, w.self_output, w.cross_query, w.cross_output),
            (w.inner_weight,),
            (w.outer_weight,),
        )
        shards = [array for group in groups for array in group]
        count, (length, width) = len(shards), hidden.shape
        pairs = width // PAIR
        low, full = jnp.bfloat16, jnp.float32
        some = [
            ((length, width), low), ((2 * pairs, length, PAIR), low), ((length, width), low),
            ((length, width), full), ((length, 128), full),
        ]
        wide_state = ((length, w.inner_weight.shape[1]), low)
        kept = some + some[:3] + [wide_state] * 2 + [((2 * length, width), low)] * 4
        kept += [((2 * length, PAIR), low)] * 2 + [some[0], some[0], some[3], some[0]]
        anywhere, near = pl.BlockSpec(memory_space=pl.ANY), pl.BlockSpec(memory_space=pltpu.VMEM)
        results = pl.pallas_call(
            functools.partial(gather_kernel, groups),
            out_shape=[jax.ShapeDtypeStruct((4, 4) + s.shape, s.dtype) for s in shards]
            + [jax.ShapeDtypeStruct((24, width), full), jax.ShapeDtypeStruct((16, width), full)]
            + [jax.ShapeDtypeStruct(*k) for k in kept],
            in_specs=[anywhere] * count + [near] * 6,
            out_specs=[anywhere] * count + [near] * 2 + [anywhere] * len(kept),
            scratch_shapes=[pltpu.VMEM(*k) for k in kept]
            + [
                pltpu.VMEM(*some[3]),
                pltpu.VMEM(*some[4]),
                pltpu.VMEM(wide_state[0], full),
                pltpu.VMEM((4, 4, *w.outer_weight.shape), low),
                pltpu.VMEM((length, width), low),
                pltpu.VMEM((8, 4, 4, width // 16, width), low),
                pltpu.VMEM((4, 4, 24, 256), full),
                pltpu.SemaphoreType.DMA((count, Gather.sems)),
                pltpu.SemaphoreType.DMA((count, Gather.sems)),
                pltpu.SemaphoreType.DMA((count,)),
                pltpu.SemaphoreType.DMA((9,)),
                pltpu.SemaphoreType.DMA((6,)),
                pltpu.SemaphoreType.DMA((6,)),
                pltpu.SemaphoreType.DMA((20,)),
            ],
            compiler_params=pltpu.CompilerParams(
                collective_id=0, has_side_effects=True, vmem_limit_bytes=60 * 2**20
            ),
        )(
            *shards, hidden, memory, query_marks(target_ids[0]), key_marks_of(target_ids[0]),
            key_marks_of(memory_ids[0]), out_grad,
        )
        wholes, (lines, summed), results = (
            results[:count], results[count : count + 2], results[count + 2 :],
        )
        flats = [array.reshape(-1, array.shape[3]) for array in wholes]
        (
            all_.self_query, all_.self_key, all_.self_value, _, all_.cross_key, all_.cross_value,
            all_.self_output, all_.cross_query, all_.cross_output, all_.inner_weight,
            all_.outer_weight,
        ) = flats
        (
            mixed_one, qx_one, first, normed_one, inverse_one, mixed_two, qx_two, second, active,
            grad_inner, k_one, v_one, k_two, v_two, km_one, km_two, layer_out, grad_outer,
            grad_two, branch_two,
        ) = results
        (
            sums.third_gain, sums.third_shift, sums.outer_bias, sums.second_gain,
            sums.second_shift, sums.cross_output_bias,
        ) = summed[:6]
        sums.inner_bias = summed[8:12].reshape(-1)
        self.kept = (
            (qx_two, k_two, v_two, mixed_two, km_two), (qx_one, k_one, v_one, mixed_one, km_one),
            normed_one, inverse_one, lines, branch_two,
        )
        self.first, self.all, self.inputs = first, all_, (hidden, memory)
        return layer_out, active, grad_outer, second, grad_inner, grad_two

    def back(self, g, sums, active, grad_outer, second, grad_inner, grad_two):
        two, one, normed_one, inverse_one, lines, branch_two = self.kept
        all_ = self.all
        length, width = branch_two.shape
        anywhere, near = pl.BlockSpec(memory_space=pl.ANY), pl.BlockSpec(memory_space=pltpu.VMEM)
        low, full = jnp.bfloat16, jnp.float32
        shapes = [(active.shape[1] // 16, width), (width // 16, active.shape[1])]
        shapes += [(width // 16, width)] * 4
        hidden, memory = self.inputs

        def blocks(array):
            return array.reshape(4, 4, -1, width)

        state = ((length, width), low)
        row = ((2 * length, width), low)
        outs = [((length, width), full)] + [state] * 7 + [((8, width), full)]
        (
            g.outer_weight, g.inner_weight, g.cross_output, g.cross_query, g.cross_key,
            g.cross_value, grad_one, branch_one, query_two, key_two, value_two, query_one, key_one,
            value_one, lines_sum,
        ) = pl.pallas_call(
            back_kernel,
            out_shape=[jax.ShapeDtypeStruct(s, full) for s in shapes]
            + [jax.ShapeDtypeStruct(*o) for o in outs],
            in_specs=[anywhere] * 4 + [near] * 5 + [anywhere] * 15,
            out_specs=[near] * 9 + [anywhere] * 2 + [near] + [anywhere] * 2 + [near],
            scratch_shapes=Reduce.scratch(shapes, [low] * 6, 4)
            + [
                pltpu.VMEM((2, length, 4 * width), low),
                pltpu.VMEM((2, length, width), low),
                pltpu.VMEM((width // HEAD_DIM, length, PAIR), low),
                pltpu.VMEM(*row), pltpu.VMEM(*row), pltpu.VMEM(*state),
                pltpu.VMEM((2 * length, PAIR), low),
                pltpu.VMEM(*state), pltpu.VMEM(*row), pltpu.VMEM(*row),
                pltpu.VMEM(*state), pltpu.VMEM(*state),
                pltpu.VMEM((3, 4, 4, width // 16, width), low),
                pltpu.VMEM((2 * length, PAIR), full), pltpu.VMEM((2 * length, PAIR), full),
                pltpu.VMEM((PAIR, length), full),
                pltpu.SemaphoreType.DMA((14,)),
                pltpu.SemaphoreType.DMA((4,)),
                pltpu.SemaphoreType.DMA((4,)),
            ],
            compiler_params=pltpu.CompilerParams(
                collective_id=2, has_side_effects=True, vmem_limit_bytes=61 * 2**20
            ),
        )(
            active, grad_outer, second, grad_inner, branch_two, grad_two, normed_one, inverse_one,
            lines, self.first, memory, *two, *one,
            blocks(all_.cross_output), blocks(all_.cross_query), blocks(all_.self_output),
        )
        (
            sums.first_gain, sums.first_shift, sums.self_output_bias, sums.cross_query_bias,
            sums.cross_value_bias, sums.self_query_bias, sums.self_value_bias, _,
        ) = lines_sum
        products = [
            (one[3], branch_one), (hidden, query_one), (hidden, key_one), (hidden, value_one),
        ]
        weights = (
            all_.self_query, all_.self_key, all_.self_value, all_.cross_key, all_.cross_value
        )
        vectors = vectors_of(sums)
        narrow = [v for v in vectors if v.shape[0] == 768]
        (wide,) = [v for v in vectors if v.shape[0] != 768]
        rows = len(narrow)
        table = jnp.concatenate(
            [
                jnp.stack(narrow).reshape(rows, 16, 48).transpose(1, 0, 2),
                wide.reshape(16, -1, 48),
            ],
            axis=1,
        )
        table = jnp.pad(table, ((0, 0), (0, 24 - table.shape[1]), (0, 256 - 48)))
        count = len(products)
        shapes = [(width // 16, width)] * count + [(24, 256)]
        *results, table, input_grad, memory_grad = pl.pallas_call(
            functools.partial(reduce_kernel, count),
            out_shape=[jax.ShapeDtypeStruct(s, full) for s in shapes]
            + [jax.ShapeDtypeStruct(*state)] * 2,
            in_specs=[near] * (2 * count + 4) + [anywhere] * 5,
            out_specs=[near] * (count + 3),
            scratch_shapes=Reduce.scratch(shapes, [low] * count + [full])
            + [
                pltpu.SemaphoreType.DMA((5,)),
                pltpu.VMEM((5, 4, 4, width // 16, width), low),
            ],
            compiler_params=pltpu.CompilerParams(
                collective_id=1, has_side_effects=True, vmem_limit_bytes=60 * 2**20
            ),
        )(
            *[factor for pair in products for factor in pair], table.reshape(4, 4, 24, 256),
            grad_one, key_two, value_two, *[blocks(array) for array in weights],
        )
        g.self_output, g.self_query, g.self_key, g.self_value = results
        reduced, row = [], 0
        for v in vectors:
            if v.shape[0] == 768:
                reduced.append(table[row, :48])
                row += 1
            else:
                reduced.append(table[rows : rows + v.shape[0] // 768, :48].reshape(-1))
        done = (
            g.self_query, g.self_key, g.self_value, g.self_output, g.cross_query, g.cross_key,
            g.cross_value, g.cross_output, g.inner_weight, g.outer_weight, input_grad, memory_grad,
        )
        (
            g.self_query, g.self_key, g.self_value, g.self_output, g.cross_query, g.cross_key,
            g.cross_value, g.cross_output, g.inner_weight, g.outer_weight, input_grad, memory_grad,
        ) = pl.pallas_call(
            hand_on,
            out_shape=[jax.ShapeDtypeStruct(array.shape, array.dtype) for array in done],
            in_specs=[near] * len(done),
            out_specs=[near] * len(done),
        )(*done)
        return reduced, input_grad, memory_grad


class Plain:
    staged = False

    def front(self, w, all_, sums, hidden, memory, target_ids, memory_ids, out_grad):
        def whole(array):
            return lax.all_gather(array, "fsdp", axis=0, tiled=True)

        all_.__dict__.update(Weights(*map(whole, w))._asdict())
        vectors = [array.astype(jnp.float32) for array in split_vectors(Weights(**vars(all_)))]
        (
            self_query_bias, self_value_bias, self_output_bias, first_gain, first_shift,
            cross_query_bias, cross_value_bias, cross_output_bias, second_gain, second_shift,
            inner_bias, outer_bias, third_gain, third_shift,
        ) = vectors
        rows, length = target_ids.shape
        width = hidden.shape[1]
        scale = HEAD_DIM ** (-0.5)

        def low(array):
            return array.astype(jnp.bfloat16).reshape(rows, length, width)

        row_ids, source_ids = self.gather_row(target_ids), self.gather_row(memory_ids)
        query_places = lax.axis_index("seq") * length + jnp.arange(length)
        key_places = jnp.arange(row_ids.shape[1])
        allowed_self = (target_ids[:, :, None] == row_ids[:, None, :]) & (
            key_places[None, None, :] <= query_places[None, :, None]
        )
        allowed_cross = target_ids[:, :, None] == source_ids[:, None, :]

        def attention(query, keys, values, allowed):
            mixed, logsum = plain_attend(query, keys, values, allowed)

            def back(grad):
                query_sum, key_sum, value_sum = plain_attend_back(
                    query, keys, values, allowed, logsum, grad.reshape(rows, length, width)
                )
                return query_sum.astype(jnp.bfloat16) * scale, key_sum, value_sum

            return mixed.astype(jnp.bfloat16).reshape(rows * length, width), back

        key_one = self.gather_row(low(dense(hidden, all_.self_key)))
        value_one = self.gather_row(low(dense(hidden, all_.self_value) + self_value_bias))
        query_one = low((dense(hidden, all_.self_query) + self_query_bias) * scale)
        mixed_one, back_one = attention(query_one, key_one, value_one, allowed_self)
        key_two = self.gather_row(low(dense(memory, all_.cross_key)))
        value_two = self.gather_row(low(dense(memory, all_.cross_value) + cross_value_bias))
        resid_one = (
            hidden.astype(jnp.float32) + dense(mixed_one, all_.self_output) + self_output_bias
        )
        first, normed_one, inverse_one = layer_norm(resid_one, first_gain, first_shift)
        first = first.astype(jnp.bfloat16)
        query_two = low((dense(first, all_.cross_query) + cross_query_bias) * scale)
        mixed_two, back_two = attention(query_two, key_two, value_two, allowed_cross)
        resid_two = (
            first.astype(jnp.float32) + dense(mixed_two, all_.cross_output) + cross_output_bias
        )
        second, normed_two, inverse_two = layer_norm(resid_two, second_gain, second_shift)
        self.kept = (
            hidden, memory, all_, mixed_one, first, normed_one, inverse_one, first_gain, back_one,
            mixed_two, back_two,
        )
        second = second.astype(jnp.bfloat16)
        inner = dense(second, all_.inner_weight) + inner_bias
        cumulative = 0.5 * (1.0 + lax.erf(inner * math.sqrt(0.5)))
        active = (inner * cumulative).astype(jnp.bfloat16)
        density = jnp.exp(-0.5 * inner * inner) * (1.0 / math.sqrt(2.0 * math.pi))
        slope = cumulative + inner * density
        resid_three = second.astype(jnp.float32) + dense(active, all_.outer_weight) + outer_bias
        final, normed_three, inverse_three = layer_norm(resid_three, third_gain, third_shift)

        keep = (target_ids > 0).astype(jnp.float32).reshape(-1, 1)
        upstream = out_grad.astype(jnp.float32) * keep
        grad_three, sums.third_gain, sums.third_shift = norm_back(
            upstream, normed_three, inverse_three, third_gain
        )
        grad_outer = grad_three.astype(jnp.bfloat16)
        sums.outer_bias = column_sum(grad_outer)
        grad_active = dense_back(grad_outer, all_.outer_weight)
        grad_inner = (grad_active * slope).astype(jnp.bfloat16)
        sums.inner_bias = column_sum(grad_inner)
        grad_second = grad_three + dense_back(grad_inner, all_.inner_weight)
        grad_two, sums.second_gain, sums.second_shift = norm_back(
            grad_second, normed_two, inverse_two, second_gain
        )
        return final, active, grad_outer, second, grad_inner, grad_two

    def _reduce(self, total):
        part = lax.psum_scatter(
            total.astype(jnp.bfloat16), "fsdp", scatter_dimension=0, tiled=True
        )
        return lax.psum(part, "seq").astype(jnp.float32)

    def back(self, g, sums, active, grad_outer, second, grad_inner, grad_two):
        (
            hidden, memory, all_, mixed_one, first, normed_one, inverse_one, first_gain, back_one,
            mixed_two, back_two,
        ) = self.kept
        shape = grad_two.shape

        def flat(array):
            return array.astype(jnp.bfloat16).reshape(shape)

        branch_two = grad_two.astype(jnp.bfloat16)
        sums.cross_output_bias = column_sum(branch_two)
        query_grad_two, key_sum, value_sum = back_two(
            flat(dense_back(branch_two, all_.cross_output))
        )
        key_grad_two = flat(self.scatter_row(key_sum))
        value_grad_two = flat(self.scatter_row(value_sum))
        query_grad_two = flat(query_grad_two)
        sums.cross_query_bias = column_sum(query_grad_two)
        sums.cross_value_bias = column_sum(value_grad_two)
        grad_first = grad_two + dense_back(query_grad_two, all_.cross_query)
        grad_one, sums.first_gain, sums.first_shift = norm_back(
            grad_first, normed_one, inverse_one, first_gain
        )
        branch_one = grad_one.astype(jnp.bfloat16)
        sums.self_output_bias = column_sum(branch_one)
        query_grad_one, key_sum, value_sum = back_one(
            flat(dense_back(branch_one, all_.self_output))
        )
        key_grad_one = flat(self.scatter_row(key_sum))
        value_grad_one = flat(self.scatter_row(value_sum))
        query_grad_one = flat(query_grad_one)
        sums.self_query_bias = column_sum(query_grad_one)
        sums.self_value_bias = column_sum(value_grad_one)
        g.outer_weight = self._reduce(dense_grad(active, grad_outer))
        g.inner_weight = self._reduce(dense_grad(second, grad_inner))
        g.cross_output = self._reduce(dense_grad(mixed_two, branch_two))
        g.cross_query = self._reduce(dense_grad(first, query_grad_two))
        g.cross_key = self._reduce(dense_grad(memory, key_grad_two))
        g.cross_value = self._reduce(dense_grad(memory, value_grad_two))
        g.self_output = self._reduce(dense_grad(mixed_one, branch_one))
        g.self_query = self._reduce(dense_grad(hidden, query_grad_one))
        g.self_key = self._reduce(dense_grad(hidden, key_grad_one))
        g.self_value = self._reduce(dense_grad(hidden, value_grad_one))
        input_grad = (
            grad_one
            + dense_back(query_grad_one, all_.self_query)
            + dense_back(key_grad_one, all_.self_key)
            + dense_back(value_grad_one, all_.self_value)
        )
        memory_grad = dense_back(key_grad_two, all_.cross_key) + dense_back(
            value_grad_two, all_.cross_value
        )
        return [self._reduce(v) for v in vectors_of(sums)], input_grad, memory_grad

    def gather_row(self, array):
        return lax.all_gather(array, "seq", axis=1, tiled=True)

    def scatter_row(self, array):
        return lax.psum_scatter(
            array.astype(jnp.bfloat16), "seq", scatter_dimension=1, tiled=True
        ).astype(jnp.float32)


def query_marks(ids):
    lanes = jnp.arange(PAIR)[None, :] % HEAD_DIM
    return jnp.where((lanes < SEGMENTS) & (ids[:, None] != lanes), masked_score, 0.0).astype(
        jnp.bfloat16
    )


def key_marks_of(ids):
    lanes = jnp.arange(PAIR)[None, :] % HEAD_DIM
    ones = (lanes >= SEGMENTS) & (lanes < SEGMENTS + 3)
    return (ones | (ids[:, None] == lanes)).astype(jnp.bfloat16)


def against(left, right):
    return lax.dot_general(
        left, right, (((1,), (1,)), ((), ())), preferred_element_type=jnp.float32
    )


def three(value):
    high = value.astype(jnp.bfloat16).astype(jnp.float32)
    rest = value - high
    middle = rest.astype(jnp.bfloat16).astype(jnp.float32)
    return high, middle, rest - middle


def place_three(lanes, base, value, other):
    high, middle, small = three(value)
    first = base + SEGMENTS
    return jnp.where(
        lanes == first,
        high,
        jnp.where(lanes == first + 1, middle, jnp.where(lanes == first + 2, small, other)),
    )


def plan(length, causal, later):
    half = length // 2
    result = []
    for tile in range(2):
        if not causal:
            result.append([(0, 2 * length, False)])
            continue
        ranges = [(0, half, False)] if tile else []
        ranges.append((tile * half, half, True))
        if later:
            ranges.append((length + tile * half, length - tile * half, False))
        result.append(ranges)
    return result


def each_plan(core, length, causal, run):
    if not causal:
        run(plan(length, False, False))
        return
    for later in range(2):
        @pl.when(core == later)
        def _():
            run(plan(length, True, bool(later)))


def forward_pair(core, causal, q_ref, k_ref, v_ref, qm_ref, km_ref, mixed_ref, qx_ref):
    length = q_ref.shape[0]

    def run(tiles):
        for head in range(2):
            base = HEAD_DIM * (1 - head)

            def own(lanes):
                return (lanes < HEAD_DIM) if head == 0 else (lanes >= HEAD_DIM)

            for tile, ranges in enumerate(tiles):
                rows = slice(tile * TILE, tile * TILE + TILE)
                lanes = lax.broadcasted_iota(jnp.int32, (TILE, PAIR), 1)
                q = jnp.where(own(lanes), q_ref[rows, :], qm_ref[rows, :])
                scores = []
                for start, size, diagonal in ranges:
                    keys = slice(start, start + size)
                    key_lanes = lax.broadcasted_iota(jnp.int32, (size, PAIR), 1)
                    k = jnp.where(own(key_lanes), k_ref[keys, :], km_ref[keys, :])
                    s = against(q, k)
                    if diagonal:
                        i = lax.broadcasted_iota(jnp.int32, s.shape, 0)
                        j = lax.broadcasted_iota(jnp.int32, s.shape, 1)
                        s = jnp.where(j <= i, s, masked_score)
                    scores.append(s)
                highest = functools.reduce(
                    jnp.maximum, [jnp.max(s, axis=1, keepdims=True) for s in scores]
                )
                out = jnp.zeros((TILE, PAIR), jnp.float32)
                for s, (start, size, _) in zip(scores, ranges):
                    keys = slice(start, start + size)
                    key_lanes = lax.broadcasted_iota(jnp.int32, (size, PAIR), 1)
                    v = jnp.where(own(key_lanes), v_ref[keys, :], jnp.ones((), jnp.bfloat16))
                    e = jnp.exp(s - highest).astype(jnp.bfloat16)
                    out = out + jnp.dot(e, v, preferred_element_type=jnp.float32)
                total = pltpu.roll(out, HEAD_DIM, 1)
                mixed = (out / total).astype(jnp.bfloat16)
                if head:
                    mixed = jnp.where(own(lanes), mixed, mixed_ref[rows, :])
                mixed_ref[rows, :] = mixed
                logsum = highest + jnp.log(out)
                qx = place_three(lanes, base, -logsum, q.astype(jnp.float32))
                qx_ref[head, rows, :] = qx.astype(jnp.bfloat16)

    each_plan(core, length, causal, run)


def backward_pair(
    core, causal, qx_ref, k_ref, v_ref, e_ref, o_ref, km_ref, dq_ref, dk_ref, dv_ref, dk_acc,
    dv_acc, dq_acc,
):
    length = e_ref.shape[0]
    scale = HEAD_DIM ** (-0.5)

    def run(tiles):
        dk_acc[...] = jnp.zeros_like(dk_acc)
        dv_acc[...] = jnp.zeros_like(dv_acc)
        for head in range(2):
            base = HEAD_DIM * (1 - head)

            def own(lanes):
                return (lanes < HEAD_DIM) if head == 0 else (lanes >= HEAD_DIM)

            for tile, ranges in enumerate(tiles):
                rows = slice(tile * TILE, tile * TILE + TILE)
                lanes = lax.broadcasted_iota(jnp.int32, (TILE, PAIR), 1)
                nothing = jnp.zeros((), jnp.bfloat16)
                qx = qx_ref[head, rows, :]
                q = jnp.where(own(lanes), qx, nothing)
                e = jnp.where(own(lanes), e_ref[rows, :], nothing)
                wide = e.astype(jnp.float32)
                delta = jnp.sum(wide * o_ref[rows, :].astype(jnp.float32), axis=1, keepdims=True)
                ex = place_three(lanes, base, -delta, wide).astype(jnp.bfloat16)
                dq = jnp.zeros((HEAD_DIM, TILE), jnp.float32)
                for start, size, diagonal in ranges:
                    keys = slice(start, start + size)
                    key_lanes = lax.broadcasted_iota(jnp.int32, (size, PAIR), 1)
                    k = jnp.where(own(key_lanes), k_ref[keys, :], km_ref[keys, :])
                    v = jnp.where(own(key_lanes), v_ref[keys, :], km_ref[keys, :])
                    p = jnp.exp(against(k, qx))
                    if diagonal:
                        j = lax.broadcasted_iota(jnp.int32, p.shape, 0)
                        i = lax.broadcasted_iota(jnp.int32, p.shape, 1)
                        p = jnp.where(j <= i, p, 0.0)
                    ds = (p * against(v, ex)).astype(jnp.bfloat16)
                    p = p.astype(jnp.bfloat16)
                    dv_acc[keys, :] += jnp.dot(p, e, preferred_element_type=jnp.float32)
                    dk_acc[keys, :] += jnp.dot(ds, q, preferred_element_type=jnp.float32)
                    kt = k_ref[keys, :].T[head * HEAD_DIM : (head + 1) * HEAD_DIM, :]
                    dq = dq + jnp.dot(kt, ds, preferred_element_type=jnp.float32)
                dq_acc[head * HEAD_DIM : (head + 1) * HEAD_DIM, rows] = dq
        dq_ref[...] = (dq_acc[...].T.astype(jnp.bfloat16) * jnp.bfloat16(scale)).astype(jnp.bfloat16)
        dk_ref[...] = dk_acc[...].astype(jnp.bfloat16)
        dv_ref[...] = dv_acc[...].astype(jnp.bfloat16)

    each_plan(core, length, causal, run)


def head_slice(array, start, span):
    piece = lax.dynamic_slice_in_dim(array, start, span, 2)
    return piece.reshape(array.shape[0], array.shape[1], 2, span // 2)


def plain_attend(query, keys, values, allowed):
    rows, length, width = query.shape
    span = 2 * HEAD_DIM
    pairs = width // span

    def one_pair(index, carry):
        mixed, logsum = carry
        start = index * span
        query_part = head_slice(query, start, span)
        key_part = head_slice(keys, start, span)
        value_part = head_slice(values, start, span)
        scores = jnp.einsum(
            "rqhe,rkhe->rhqk", query_part, key_part, preferred_element_type=jnp.float32
        )
        scores = jnp.where(allowed[:, None], scores, masked_score)
        highest = jnp.max(scores, axis=-1, keepdims=True)
        exponent = jnp.exp(scores - highest)
        total = jnp.sum(exponent, axis=-1, keepdims=True)
        probs = (exponent / total).astype(jnp.bfloat16)
        part = jnp.einsum("rhqk,rkhe->rqhe", probs, value_part, preferred_element_type=jnp.float32)
        mixed = lax.dynamic_update_slice_in_dim(mixed, part.reshape(rows, length, span), start, 2)
        logsum = lax.dynamic_update_slice_in_dim(
            logsum, (highest + jnp.log(total))[None, :, :, :, 0], index, 0
        )
        return (mixed, logsum)

    mixed = jnp.zeros((rows, length, width), jnp.float32)
    logsum = jnp.zeros((pairs, rows, 2, length), jnp.float32)
    return lax.fori_loop(0, pairs, one_pair, (mixed, logsum))


def plain_attend_back(query, keys, values, allowed, logsum, grad_mixed):
    rows, length, width = query.shape
    extent = keys.shape[1]
    span = 2 * HEAD_DIM
    pairs = width // span

    def one_pair(index, carry):
        start = index * span
        query_part = head_slice(query, start, span)
        key_part = head_slice(keys, start, span)
        value_part = head_slice(values, start, span)
        grad_part = head_slice(grad_mixed, start, span)
        scores = jnp.einsum(
            "rqhe,rkhe->rhqk", query_part, key_part, preferred_element_type=jnp.float32
        )
        scores = jnp.where(allowed[:, None], scores, masked_score)
        pair_logsum = lax.dynamic_index_in_dim(logsum, index, 0, keepdims=False)
        probs = jnp.exp(scores - pair_logsum[..., None])
        prob_grad = jnp.einsum(
            "rqhe,rkhe->rhqk", grad_part, value_part, preferred_element_type=jnp.float32
        )
        row_total = jnp.sum(probs * prob_grad, axis=-1, keepdims=True)
        score_grad = (probs * (prob_grad - row_total)).astype(jnp.bfloat16)
        query_grad = jnp.einsum(
            "rhqk,rkhe->rqhe", score_grad, key_part, preferred_element_type=jnp.float32
        )
        grad_query = lax.dynamic_update_slice_in_dim(
            carry[0], query_grad.reshape(rows, length, span), start, 2
        )
        probs_low = probs.astype(jnp.bfloat16)
        value_grad = jnp.einsum(
            "rhqk,rqhe->rkhe", probs_low, grad_part, preferred_element_type=jnp.float32
        )
        key_grad = jnp.einsum(
            "rhqk,rqhe->rkhe", score_grad, query_part, preferred_element_type=jnp.float32
        )
        grad_keys = lax.dynamic_update_slice_in_dim(
            carry[1], key_grad.reshape(rows, extent, span), start, 2
        )
        grad_values = lax.dynamic_update_slice_in_dim(
            carry[2], value_grad.reshape(rows, extent, span), start, 2
        )
        return (grad_query, grad_keys, grad_values)

    start_query = jnp.zeros((rows, length, width), jnp.float32)
    start_keys = jnp.zeros((rows, extent, width), jnp.float32)
    return lax.fori_loop(0, pairs, one_pair, (start_query, start_keys, start_keys))


def body(staged, hidden_in, memory, target_ids, memory_ids, out_grad, *weights):
    w = Weights(*weights)
    rows, length, width = hidden_in.shape
    staged = staged and (rows, length, width) == (1, 2 * TILE, 768)
    net = Staged() if staged else Plain()
    all_ = SimpleNamespace()
    tokens = rows * length
    flat_in = hidden_in.reshape(tokens, width)
    flat_memory = memory.reshape(tokens, width)

    def low(array):
        return array.astype(jnp.bfloat16).reshape(rows, length, width)

    sums = SimpleNamespace()
    layer_out, *states = net.front(
        w, all_, sums, flat_in, flat_memory, target_ids, memory_ids,
        out_grad.reshape(tokens, width),
    )
    g = SimpleNamespace()
    (
        g.self_query_bias, g.self_value_bias, g.self_output_bias, g.first_gain, g.first_shift,
        g.cross_query_bias, g.cross_value_bias, g.cross_output_bias, g.second_gain,
        g.second_shift, g.inner_bias, g.outer_bias, g.third_gain, g.third_shift,
    ), input_grad, memory_grad = net.back(g, sums, *states)
    return (low(layer_out), low(input_grad), low(memory_grad), *Weights(**vars(g)))


def solution(mesh):
    staged = mesh.shape["fsdp"] == 16 and mesh.shape["seq"] == 2
    row, ids = P("fsdp", "seq", None), P("fsdp", "seq")
    matrix, vector = P("fsdp", None), P("fsdp")
    weights = Weights(
        matrix, vector, matrix, matrix, vector, matrix, vector, vector, vector, matrix, vector,
        matrix, matrix, vector, matrix, vector, vector, vector, matrix, vector, matrix, vector,
        vector, vector,
    )
    return jax.shard_map(
        functools.partial(body, staged),
        mesh=mesh,
        in_specs=(row, row, ids, ids, row, *weights),
        out_specs=(row, row, row, *weights),
        check_vma=False,
    )
```

```python
import functools
import math
from types import SimpleNamespace
from typing import NamedTuple

import jax
import jax.numpy as jnp
from jax import lax
from jax.experimental import pallas as pl
from jax.experimental.pallas import tpu as pltpu
from jax.sharding import PartitionSpec as P

HEAD_DIM = 64
PAIR = 2 * HEAD_DIM
SEGMENTS = 5
TILE = 256
eps_norm = 1e-05
masked_score = -1e30


class Weights(NamedTuple):
    self_query: jax.Array
    self_query_bias: jax.Array
    self_key: jax.Array
    self_value: jax.Array
    self_value_bias: jax.Array
    self_output: jax.Array
    self_output_bias: jax.Array
    first_gain: jax.Array
    first_shift: jax.Array
    cross_query: jax.Array
    cross_query_bias: jax.Array
    cross_key: jax.Array
    cross_value: jax.Array
    cross_value_bias: jax.Array
    cross_output: jax.Array
    cross_output_bias: jax.Array
    second_gain: jax.Array
    second_shift: jax.Array
    inner_weight: jax.Array
    inner_bias: jax.Array
    outer_weight: jax.Array
    outer_bias: jax.Array
    third_gain: jax.Array
    third_shift: jax.Array


def split_vectors(w):
    return [array for array in w if array.ndim == 1]


def vectors_of(sums):
    return [
        sums.self_query_bias, sums.self_value_bias, sums.self_output_bias, sums.first_gain,
        sums.first_shift, sums.cross_query_bias, sums.cross_value_bias, sums.cross_output_bias,
        sums.second_gain, sums.second_shift, sums.inner_bias, sums.outer_bias, sums.third_gain,
        sums.third_shift,
    ]


def dense(left, right):
    return jnp.dot(left, right, preferred_element_type=jnp.float32)


def dense_back(left, right):
    return lax.dot_general(
        left, right, (((1,), (1,)), ((), ())), preferred_element_type=jnp.float32
    )


def dense_grad(left, right):
    return lax.dot_general(
        left, right, (((0,), (0,)), ((), ())), preferred_element_type=jnp.float32
    )


def column_sum(values):
    return jnp.sum(values, axis=0, dtype=jnp.float32)


def layer_norm(resid, gain, shift):
    center = resid - jnp.mean(resid, axis=-1, keepdims=True)
    spread = jnp.mean(center * center, axis=-1, keepdims=True)
    inverse = lax.rsqrt(spread + eps_norm)
    normed = center * inverse
    return (normed * gain + shift, normed, inverse)


def norm_back(upstream, normed, inverse, gain):
    scaled = upstream * gain
    plain_mean = jnp.mean(scaled, axis=-1, keepdims=True)
    cross_mean = jnp.mean(scaled * normed, axis=-1, keepdims=True)
    result = inverse * (scaled - plain_mean - normed * cross_mean)
    return (result, jnp.sum(upstream * normed, axis=0), jnp.sum(upstream, axis=0))


MESH = pl.DeviceIdType.MESH


class Spot:
    def __init__(self):
        f, c = lax.axis_index("fsdp"), lax.axis_index("seq")
        self.c, self.z, self.plane = c, f // 4, f % 4
        self.other = (f, 1 - c)
        self.by_x = ((f // 2) * 2 + (1 - f % 2), c)
        self.by_y = (self.z * 4 + (self.plane + 2) % 4, c)
        self.first = (jnp.where(c == 0, self.by_x[0], self.by_y[0]), c)
        self.second = (jnp.where(c == 0, self.by_y[0], self.by_x[0]), c)
        self.plane_x = self.by_x[0] % 4
        self.plane_y = self.by_y[0] % 4
        self.plane_first = jnp.where(c == 0, self.plane_x, self.plane_y)
        self.plane_second = jnp.where(c == 0, self.plane_y, self.plane_x)
        self.plane_both = 3 - self.plane

    def at_z(self, k):
        z = (self.z + k) % 4
        return z, (z * 4 + self.plane, self.c)

    def meet(self):
        barrier = pltpu.get_barrier_semaphore()
        partners = [self.other, self.by_x, self.by_y] + [self.at_z(k)[1] for k in (1, 2, 3)]
        for partner in partners:
            pl.semaphore_signal(barrier, inc=1, device_id=partner, device_id_type=MESH)
        pl.semaphore_wait(barrier, len(partners))


class Gather:
    sems = 31
    order = (0, 1, 3, 2)

    def __init__(self, spot, shards, wholes, send, recv, local, base):
        self.spot, self.shards, self.wholes = spot, shards, wholes
        self.send, self.recv, self.local, self.base = send, recv, local, base
        self.all = range(len(shards))

    def _columns(self, j):
        half = self.wholes[j].shape[3] // 2
        return pl.ds(pl.multiple_of(self.spot.c * half, 128), half)

    def _view(self, j, p, plane):
        return self.wholes[j].at[(self.spot.z + 4 - p) % 4, plane, :, self._columns(j)]

    def _copy(self, j, n, source, target, partner):
        return pltpu.make_async_remote_copy(
            source, target, self.send.at[self.base + j, n], self.recv.at[self.base + j, n],
            device_id=partner, device_id_type=MESH,
        )

    def _z(self, j, k):
        spot = self.spot
        source = self.shards[j].at[:, self._columns(j)]
        return self._copy(j, k - 1, source, self._view(j, 0, spot.plane), spot.at_z(k)[1])

    def _near(self, j, p, way):
        spot = self.spot
        view = self._view(j, p, spot.plane)
        source = view if p else self.shards[j].at[:, self._columns(j)]
        return self._copy(j, 3 + 2 * p + way, source, view, spot.by_y if way else spot.by_x)

    def _far(self, j, p):
        view = self._view(j, p, self.spot.plane_first)
        return self._copy(j, 11 + p, view, view, self.spot.second)

    def _swap(self, j, p, n):
        spot = self.spot
        plane = (spot.plane, spot.plane_x, spot.plane_y, spot.plane_both)[n]
        view = self._view(j, p, plane)
        return self._copy(j, 15 + 4 * p + n, view, view, spot.other)

    def _locals(self):
        return [
            pltpu.make_async_copy(
                self.shards[j], self.wholes[j].at[self.spot.z, self.spot.plane],
                self.local.at[self.base + j],
            )
            for j in self.all
        ]

    def start(self):
        for k in self.order[1:2]:
            for j in self.all:
                self._z(j, k).start()
        for j in self.all:
            for way in range(2):
                self._near(j, 0, way).start()
        for k in self.order[2:]:
            for j in self.all:
                self._z(j, k).start()
        for copy in self._locals():
            copy.start()

    def advance(self, i):
        if i < 4:
            p = self.order[i]
            for j in self.all:
                self._z(j, p).wait_recv()
                self._near(j, p, 0).start()
                self._near(j, p, 1).start()
                self._swap(j, p, 0).start()
        if 1 <= i < 5:
            p = self.order[i - 1]
            for j in self.all:
                self._near(j, p, 0).wait_recv()
                self._near(j, p, 1).wait_recv()
                self._far(j, p).start()
                self._swap(j, p, 1).start()
                self._swap(j, p, 2).start()
        if 2 <= i < 6:
            p = self.order[i - 2]
            for j in self.all:
                self._far(j, p).wait_recv()
                self._swap(j, p, 3).start()

    def finish(self):
        for copy in self._locals():
            copy.wait()
        for j in self.all:
            for p in self.order:
                if p:
                    self._z(j, p).wait_send()
                self._near(j, p, 0).wait_send()
                self._near(j, p, 1).wait_send()
                self._far(j, p).wait_send()
                for n in range(0 if p else 1, 4):
                    self._swap(j, p, n).wait()
class Reduce:
    sems = 21
    order = (2, 3, 1, 0)

    def __init__(self, spot, outs, give, mine, there, far, near, line, send, recv):
        self.spot, self.outs, self.give = spot, outs, give
        self.mine, self.there, self.far, self.near, self.line = mine, there, far, near, line
        self.send, self.recv = send, recv
        self.all = range(len(outs))

    @staticmethod
    def scratch(shapes, dtypes, shared=0):
        def buffers(*lead):
            return [pltpu.VMEM((*lead, r, w // 2), d) for (r, w), d in zip(shapes, dtypes)]

        n = len(shapes)
        return (
            buffers(4, 4)[: n - shared] + buffers(4, 4) + buffers(4, 4) + buffers(4)
            + buffers(4, 2) + buffers(3) + [pltpu.SemaphoreType.DMA((n, Reduce.sems))] * 2
        )

    @staticmethod
    def unpack(spot, outs, refs, shared=0):
        n = len(outs)
        give, refs = list(refs[: n - shared]), refs[n - shared :]
        for i in range(shared):
            half = outs[n - shared + i].shape[1] // 2
            give.append(give[n - shared - 1].at[:, :, :, pl.ds(i * half, half)])
        groups = [refs[i * n : (i + 1) * n] for i in range(5)]
        return Reduce(spot, outs, give, *groups, *refs[5 * n : 5 * n + 2])

    def free(self, j):
        for p in self.order:
            self._cross(j, p).wait_send()
        self.freed = (j,)

    freed = ()

    def part(self, js):
        def some(items):
            return [items[j] for j in js]

        lists = (self.outs, self.give, self.mine, self.there, self.far, self.near, self.line)
        chosen = Reduce(self.spot, *[some(items) for items in lists], self.send, self.recv)
        chosen.base = js[0]
        return chosen

    base = 0

    def put(self, j, core_of, value, columns=None, z_first=0):
        target = self.give[j] if core_of else self.mine[j]
        rows = target.shape[2]
        block = 4 * rows
        columns = slice(None) if columns is None else columns
        for i in range(value.shape[0] // block):
            p = (z_first + i + 4 - self.spot.z) % 4
            piece = value[i * block : (i + 1) * block]
            target[p, :, :, columns] = piece.reshape(4, rows, -1).astype(target.dtype)

    def _columns(self, j, core):
        half = self.outs[j].shape[1] // 2
        return pl.ds(pl.multiple_of(core * half, 128), half)

    def _copy(self, j, n, source, target, partner):
        return pltpu.make_async_remote_copy(
            source, target, self.send.at[self.base + j, n], self.recv.at[self.base + j, n],
            device_id=partner, device_id_type=MESH,
        )

    def _cross(self, j, p):
        return self._copy(j, p, self.give[j].at[p], self.there[j].at[p], self.spot.other)

    def _far(self, j, p):
        spot = self.spot
        return self._copy(
            j, 4 + p, self.mine[j].at[p, spot.plane_both], self.far[j].at[p], spot.first
        )

    def _near(self, j, p, way):
        spot = self.spot
        plane, partner = (spot.plane_y, spot.by_y) if way else (spot.plane_x, spot.by_x)
        return self._copy(
            j, 8 + 2 * p + way, self.mine[j].at[p, plane], self.near[j].at[p, way], partner
        )

    def _line(self, j, p):
        spot = self.spot
        return self._copy(
            j, 16 + p, self.mine[j].at[p, spot.plane], self.line[j].at[p - 1], spot.at_z(p)[1]
        )

    def _last(self, j):
        view = self.outs[j].at[:, self._columns(j, self.spot.c)]
        return self._copy(j, 20, view, view, self.spot.other)

    def start(self, j):
        for p in self.order:
            self._cross(j, p).start()

    def _sum(self, j, p, plane, *others):
        total = self.mine[j][p, plane].astype(jnp.float32)
        total = total + self.there[j][p, plane].astype(jnp.float32)
        for other in others:
            total = total + other.astype(jnp.float32)
        return total

    def _store(self, j, p, plane, total):
        self.mine[j][p, plane] = total.astype(self.mine[j].dtype)

    def advance(self, i):
        spot = self.spot
        if i < 4:
            p = self.order[i]
            for j in self.all:
                self._cross(j, p).wait_recv()
                self._store(j, p, spot.plane_both, self._sum(j, p, spot.plane_both))
                self._far(j, p).start()
        if 0 <= i - 1 < 4:
            p = self.order[i - 1]
            for j in self.all:
                self._store(j, p, spot.plane_first, self._sum(j, p, spot.plane_first))
                self._far(j, p).wait_recv()
                self._store(
                    j, p, spot.plane_second, self._sum(j, p, spot.plane_second, self.far[j][p])
                )
                self._near(j, p, 0).start()
                self._near(j, p, 1).start()
        if 0 <= i - 2 < 4:
            p = self.order[i - 2]
            for j in self.all:
                self._near(j, p, 0).wait_recv()
                self._near(j, p, 1).wait_recv()
                total = self._sum(j, p, spot.plane, self.near[j][p, 0], self.near[j][p, 1])
                if p:
                    self._store(j, p, spot.plane, total)
                    self._line(j, p).start()
                else:
                    for k in (1, 2, 3):
                        self._line(j, k).wait_recv()
                        total = total + self.line[j][k - 1].astype(jnp.float32)
                    self.outs[j][:, self._columns(j, spot.c)] = total
                    self._last(j).start()

    def finish(self):
        for j in self.all:
            for p in self.order:
                if j not in self.freed:
                    self._cross(j, p).wait_send()
                self._far(j, p).wait_send()
                self._near(j, p, 0).wait_send()
                self._near(j, p, 1).wait_send()
                if p:
                    self._line(j, p).wait_send()
            self._last(j).wait()


def gather_kernel(groups, *refs):
    counts = [len(group) for group in groups]
    count = sum(counts)
    shards, (x_ref, memory_ref, marks_ref, grad_ref), refs = (
        refs[:count], refs[count : count + 4], refs[count + 4 :],
    )
    qm_ref, own_km_one, own_km_two = (
        marks_ref.at[pl.ds(i * x_ref.shape[0], x_ref.shape[0])] for i in range(3)
    )
    wholes, (lines_ref, sums_ref), results, refs = (
        refs[:count], refs[count : count + 2], refs[count + 2 : count + 22], refs[count + 22 :],
    )
    kept, refs = refs[:20], refs[20:]
    (
        mixed_one, qx_one, first, normed_one, inverse_one, mixed_two, qx_two, second, active,
        grad_inner, k_one, v_one, k_two, v_two, km_one, km_two, layer_out, grad_outer, grad_two,
        branch_two,
    ) = kept
    (
        normed_two, inverse_two, slope, outer, query, weight, table, send, recv, local, weight_sem,
        send_row, recv_row, out_sem,
    ) = refs
    spot = Spot()
    length, width = x_ref.shape
    scale = HEAD_DIM ** (-0.5)
    gathers, start = [], 0
    for n in counts:
        chosen = slice(start, start + n)
        gathers.append(Gather(spot, shards[chosen], wholes[chosen], send, recv, local, start))
        start += n
    one, two, three_, four = gathers

    def fetch(i):
        return pltpu.make_async_copy(wholes[i], weight.at[i if i < 3 else i - 1], weight_sem.at[i])

    def matrix(i):
        return weight[i if i < 3 else i - 1].reshape(width, width)

    def line(i):
        return lines_ref[i : i + 1, :]

    def cross(i, ref):
        return pltpu.make_async_remote_copy(
            ref.at[pl.ds(0, length)], ref.at[pl.ds(length, length)], send_row.at[i],
            recv_row.at[i], device_id=spot.other, device_id_type=MESH,
        )

    def leave(i):
        return pltpu.make_async_copy(kept[i], results[i], out_sem.at[i])

    def norm(total, gain, shift, low, normed, inverse):
        center = total - jnp.mean(total, axis=-1, keepdims=True)
        spread = jnp.mean(center * center, axis=-1, keepdims=True)
        factor = lax.rsqrt(spread + eps_norm)
        unit = center * factor
        normed[...] = unit
        inverse[...] = jnp.broadcast_to(factor, inverse.shape)
        low[...] = (unit * gain + shift).astype(jnp.bfloat16)

    def pairs(first_pair, last_pair, causal, k, v, km, mixed, qx):
        def one_pair(i, carry):
            columns = pl.ds(pl.multiple_of(i * PAIR, PAIR), PAIR)
            forward_pair(
                spot.c, causal, query.at[:, columns], k.at[:, columns], v.at[:, columns], qm_ref,
                km, mixed.at[:, columns], qx.at[pl.ds(2 * i, 2)],
            )
            return carry

        lax.fori_loop(first_pair, last_pair, one_pair, 0)

    spot.meet()
    one.start()
    two.start()
    km_one[0:length, :] = own_km_one[...]
    km_two[0:length, :] = own_km_two[...]
    marks = [cross(0, km_one), cross(1, km_two)]
    for copy in marks:
        copy.start()
    one.advance(1)
    one.advance(2)
    one.advance(3)
    one.advance(4)
    one.advance(5)
    one.finish()
    three_.start()
    for i in range(3):
        fetch(i).start()
    vector_copy = pltpu.make_async_copy(wholes[3], table, weight_sem.at[3])
    vector_copy.start()
    vector_copy.wait()
    lines = jnp.zeros(lines_ref.shape, jnp.float32)
    bias = jnp.zeros((8, width), jnp.float32)
    for f in range(16):
        i = lax.broadcasted_iota(jnp.int32, (128, width), 0)
        j = lax.broadcasted_iota(jnp.int32, (128, width), 1)
        at = ((i < 48) & (j == i + 48 * f)).astype(jnp.bfloat16)
        piece = table[f // 4, f % 4, :, 0:128].astype(jnp.bfloat16)
        lines = lines + dense(piece, at)
        piece = [table[q, f // 4, 13 + f % 4 : 14 + f % 4, 0:128] for q in range(4)]
        bias = bias + dense(jnp.concatenate(piece + piece).astype(jnp.bfloat16), at)
    lines_ref[...] = lines

    fetch(0).wait()
    fetch(1).wait()
    fetch(2).wait()
    k_one[0:length, :] = dense(x_ref[...], matrix(1)).astype(jnp.bfloat16)
    row_one = [cross(2, k_one), cross(3, v_one)]
    row_one[0].start()
    v_one[0:length, :] = (dense(x_ref[...], matrix(2)) + line(1)).astype(jnp.bfloat16)
    row_one[1].start()
    query[...] = ((dense(x_ref[...], matrix(0)) + line(0)) * scale).astype(jnp.bfloat16)
    two.advance(1)
    for copy in marks:
        copy.wait()
    for copy in row_one:
        copy.wait()
    leaving = [leave(i) for i in (10, 11, 14, 15)]
    for copy in leaving:
        copy.start()
    pairs(0, 2, True, k_one, v_one, km_one, mixed_one, qx_one)
    two.advance(2)
    pairs(2, 4, True, k_one, v_one, km_one, mixed_one, qx_one)
    two.advance(3)
    pairs(4, 6, True, k_one, v_one, km_one, mixed_one, qx_one)
    for i in (0, 1):
        leaving.append(leave(i))
        leaving[-1].start()
    two.advance(4)
    three_.advance(1)
    four.start()
    two.advance(5)
    two.finish()
    for i in range(4, 9):
        fetch(i).start()
    fetch(4).wait()
    k_two[0:length, :] = dense(memory_ref[...], matrix(4)).astype(jnp.bfloat16)
    row_two = [cross(4, k_two), cross(5, v_two)]
    row_two[0].start()
    fetch(5).wait()
    v_two[0:length, :] = (dense(memory_ref[...], matrix(5)) + line(6)).astype(jnp.bfloat16)
    row_two[1].start()
    three_.advance(2)
    fetch(6).wait()
    total = x_ref[...].astype(jnp.float32) + dense(mixed_one[...], matrix(6)) + line(2)
    norm(total, line(3), line(4), first, normed_one, inverse_one)
    fetch(7).wait()
    query[...] = ((dense(first[...], matrix(7)) + line(5)) * scale).astype(jnp.bfloat16)
    three_.advance(3)
    for copy in row_two:
        copy.wait()
    for i in (2, 3, 4, 12, 13):
        leaving.append(leave(i))
        leaving[-1].start()
    pairs(0, 2, False, k_two, v_two, km_two, mixed_two, qx_two)
    three_.advance(4)
    four.advance(1)
    pairs(2, 4, False, k_two, v_two, km_two, mixed_two, qx_two)
    three_.advance(5)
    four.advance(2)
    pairs(4, 6, False, k_two, v_two, km_two, mixed_two, qx_two)
    three_.finish()
    chunks = [slice(q * width, (q + 1) * width) for q in range(4)]
    inner = [
        pltpu.make_async_copy(wholes[9].at[:, :, :, chunks[q]], weight.at[q], weight_sem.at[q])
        for q in range(4)
    ]
    for copy in inner:
        copy.start()
    four.advance(3)
    fetch(8).wait()
    total = first[...].astype(jnp.float32) + dense(mixed_two[...], matrix(8)) + line(7)
    norm(total, line(8), line(9), second, normed_two, inverse_two)
    for i in (5, 6, 7):
        leaving.append(leave(i))
        leaving[-1].start()
    four.advance(4)
    for q in range(4):
        inner[q].wait()
        value = dense(second[...], weight[q].reshape(width, width)) + bias[q : q + 1, :]
        cumulative = 0.5 * (1.0 + lax.erf(value * math.sqrt(0.5)))
        active[:, chunks[q]] = (value * cumulative).astype(jnp.bfloat16)
        density = jnp.exp(-0.5 * value * value) * (1.0 / math.sqrt(2.0 * math.pi))
        slope[:, chunks[q]] = cumulative + value * density
        if q == 0:
            four.advance(5)
    four.finish()
    last = pltpu.make_async_copy(wholes[10], outer, weight_sem.at[4])
    last.start()
    leaving.append(leave(8))
    leaving[-1].start()

    def add_row(i, values):
        sums_ref[i : i + 1, :] = jnp.sum(values.astype(jnp.float32), axis=0, keepdims=True)

    def back(grad, normed, factor, gain):
        scaled = grad * gain
        plain_mean = jnp.mean(scaled, axis=-1, keepdims=True)
        cross_mean = jnp.mean(scaled * normed, axis=-1, keepdims=True)
        return factor * (scaled - plain_mean - normed * cross_mean)

    last.wait()
    total = second[...].astype(jnp.float32) + line(10)
    for q in range(4):
        total = total + dense(active[:, chunks[q]], outer[q].reshape(width, width))
    center = total - jnp.mean(total, axis=-1, keepdims=True)
    factor = lax.rsqrt(jnp.mean(center * center, axis=-1, keepdims=True) + eps_norm)
    unit = center * factor
    layer_out[...] = (unit * line(11) + line(12)).astype(jnp.bfloat16)
    keep = jnp.where(qm_ref[:, 0:1].astype(jnp.float32) < 0.0, 1.0, 0.0)
    upstream = grad_ref[...].astype(jnp.float32) * keep
    add_row(0, upstream * unit)
    add_row(1, upstream)
    grad_three = back(upstream, unit, factor, line(11))
    grad_outer[...] = grad_three.astype(jnp.bfloat16)
    add_row(2, grad_outer[...])
    for i in (16, 17):
        leaving.append(leave(i))
        leaving[-1].start()
    grad = grad_three
    for q in range(4):
        value = dense_back(grad_outer[...], outer[q].reshape(width, width))
        piece = (value * slope[:, chunks[q]]).astype(jnp.bfloat16)
        grad_inner[:, chunks[q]] = piece
        add_row(8 + q, piece)
        grad = grad + dense_back(piece, weight[q].reshape(width, width))
    leaving.append(leave(9))
    leaving[-1].start()
    unit = normed_two[...]
    add_row(3, grad * unit)
    add_row(4, grad)
    grad_two[...] = back(grad, unit, inverse_two[:, 0:1], line(8))
    branch_two[...] = grad_two[...].astype(jnp.bfloat16)
    for i in (18, 19):
        leaving.append(leave(i))
        leaving[-1].start()
    add_row(5, branch_two[...])
    for copy in leaving:
        copy.wait()


def back_kernel(*refs):
    active, grad_outer, second, grad_inner = refs[:4]
    branch_two, grad_two, normed_one, inverse_one, lines_ref, first, memory = refs[4:11]
    attends = (refs[11:16], refs[16:21])
    wholes = refs[21:24]
    outs, refs = refs[24:30], refs[30:]
    (grad_one, branch_one, dq_two, kg_two, vg_two, dq_one, kg_one, vg_one, sums_ref), refs = (
        refs[:9], refs[9:],
    )
    (
        wide, narrow, qx, k, v, mixed, km, e, dk, dv, dk_there, dv_there, weight, dk_acc, dv_acc,
        dq_acc, sem, send_row, recv_row,
    ) = refs[-19:]
    spot = Spot()
    reduce = Reduce.unpack(spot, outs, refs[:-19], 4)
    length, width = branch_two.shape
    half = width // 2

    def load(source, target, i):
        return pltpu.make_async_copy(source, target, sem.at[i])

    def load_attend(i):
        targets = (qx, k, v, mixed, km)
        return [load(source, target, 4 + n) for n, (source, target) in enumerate(zip(attends[i], targets))]

    early = [
        load(active, wide.at[0], 0), load(grad_outer, narrow.at[0], 1),
        load(second, narrow.at[1], 2), load(grad_inner, wide.at[1], 3),
    ]
    for copy in early:
        copy.start()
    attend = load_attend(0)
    matrices = [load(wholes[i], weight.at[i], 9 + i) for i in range(3)]
    for copy in attend + matrices:
        copy.start()
    spot.meet()
    for copy in early[:2]:
        copy.wait()
    for core_of in (1, 0):
        start = pl.multiple_of((spot.c if core_of == 0 else 1 - spot.c) * half, 128)
        right = narrow[0, :, pl.ds(start, half)]
        for chunk in range(4):
            left = wide[0, :, chunk * width : (chunk + 1) * width]
            reduce.put(0, core_of, dense_grad(left, right), None, chunk)
        if core_of:
            reduce.start(0)
    for copy in early[2:]:
        copy.wait()
    for core_of in (1, 0):
        for chunk in range(4):
            base = (spot.c if core_of == 0 else 1 - spot.c) * 2 * width + chunk * half
            right = wide[1, :, pl.ds(pl.multiple_of(base, 128), half)]
            columns = slice(chunk * half, (chunk + 1) * half)
            reduce.put(1, core_of, dense_grad(narrow[1], right), columns)
        if core_of:
            reduce.start(1)
    ffn, others = reduce.part((0, 1)), reduce.part((2, 3, 4, 5))

    def multiply(j, left, right):
        for core_of in (1, 0):
            start = pl.multiple_of((spot.c if core_of == 0 else 1 - spot.c) * half, 128)
            reduce.put(j, core_of, dense_grad(left[...], right[:, pl.ds(start, half)]))
            if core_of:
                reduce.start(j)

    def matrix(i):
        return weight[i].reshape(width, width)

    def pairs(first_pair, last_pair, causal, dq):
        def one_pair(i, carry):
            columns = pl.ds(pl.multiple_of(i * PAIR, PAIR), PAIR)
            backward_pair(
                spot.c, causal, qx.at[pl.ds(2 * i, 2)], k.at[:, columns], v.at[:, columns],
                e.at[:, columns], mixed.at[:, columns], km, dq.at[:, columns], dk.at[:, columns],
                dv.at[:, columns], dk_acc, dv_acc, dq_acc,
            )
            return carry

        lax.fori_loop(first_pair, last_pair, one_pair, 0)

    def cross(i):
        source, target = ((dk, dk_there), (dv, dv_there))[i % 2]
        return pltpu.make_async_remote_copy(
            source.at[pl.ds(length, length)], target, send_row.at[i], recv_row.at[i],
            device_id=spot.other, device_id_type=MESH,
        )

    def left(own, out, n):
        return load(own.at[pl.ds(0, length)], out, 12 + n)

    def join(i, kg, vg):
        for n, (own, there, out) in enumerate(((dk, dk_there, kg), (dv, dv_there, vg))):
            cross(2 * i + n).wait()
            total = own[0:length, :].astype(jnp.float32) + there[...].astype(jnp.float32)
            own[0:length, :] = total.astype(jnp.bfloat16)
            left(own, out, n).start()

    def add_row(i, values):
        sums_ref[i : i + 1, :] = jnp.sum(values.astype(jnp.float32), axis=0, keepdims=True)

    factors = [load(first, narrow.at[0], 1), load(memory, narrow.at[1], 2)]
    for copy in factors:
        copy.start()
    ffn.advance(0)
    for copy in attend + matrices:
        copy.wait()
    e[...] = dense_back(branch_two[...], matrix(0)).astype(jnp.bfloat16)
    pairs(0, 2, False, dq_two)
    ffn.advance(1)
    for copy in factors:
        copy.wait()
    reduce.free(1)
    multiply(2, mixed, branch_two)
    pairs(2, 4, False, dq_two)
    ffn.advance(2)
    pairs(4, 6, False, dq_two)
    cross(0).start()
    cross(1).start()
    attend = load_attend(1)
    for copy in attend:
        copy.start()
    ffn.advance(3)
    multiply(3, narrow.at[0], dq_two)
    join(0, kg_two, vg_two)
    key_part, value_part = dk.at[pl.ds(0, length)], dv.at[pl.ds(0, length)]
    multiply(4, narrow.at[1], key_part)
    multiply(5, narrow.at[1], value_part)
    add_row(4, value_part[...])
    grad = grad_two[...] + dense_back(dq_two[...], matrix(1))
    normed = normed_one[...]
    add_row(0, grad * normed)
    add_row(1, grad)
    scaled = grad * lines_ref[3:4, :]
    plain_mean = jnp.mean(scaled, axis=-1, keepdims=True)
    cross_mean = jnp.mean(scaled * normed, axis=-1, keepdims=True)
    grad_one[...] = inverse_one[:, 0:1] * (scaled - plain_mean - normed * cross_mean)
    branch_one[...] = grad_one[...].astype(jnp.bfloat16)
    ffn.advance(4)
    others.advance(0)
    e[...] = dense_back(branch_one[...], matrix(2)).astype(jnp.bfloat16)
    for copy in attend:
        copy.wait()
    left(dk, kg_two, 0).wait()
    left(dv, vg_two, 1).wait()
    pairs(0, 2, True, dq_one)
    ffn.advance(5)
    others.advance(1)
    pairs(2, 4, True, dq_one)
    others.advance(2)
    pairs(4, 6, True, dq_one)
    cross(2).start()
    cross(3).start()
    others.advance(3)
    add_row(2, branch_one[...])
    add_row(3, dq_two[...])
    add_row(5, dq_one[...])
    others.advance(4)
    join(1, kg_one, vg_one)
    add_row(6, value_part[...])
    others.advance(5)
    reduce.finish()
    left(dk, kg_one, 0).wait()
    left(dv, vg_one, 1).wait()


def reduce_kernel(count, *refs):
    factors, refs = refs[: 2 * count], refs[2 * count :]
    (table, grad_one, key_two, value_two), wholes, refs = refs[:4], refs[4:9], refs[9:]
    outs, (input_ref, memory_ref), refs = (
        refs[: count + 1], refs[count + 1 : count + 3], refs[count + 3 :],
    )
    weight, refs = refs[-1], refs[:-1]
    sem, refs = refs[-1], refs[:-1]
    spot = Spot()
    reduce = Reduce.unpack(spot, outs, refs)
    width = factors[0].shape[1]
    half = width // 2
    copies = [pltpu.make_async_copy(wholes[i], weight.at[i], sem.at[i]) for i in range(5)]
    for copy in copies:
        copy.start()
    spot.meet()
    for core_of in (1, 0):
        start = pl.multiple_of((spot.c if core_of == 0 else 1 - spot.c) * 128, 128)
        for z in range(4):
            p = (z + 4 - spot.z) % 4
            target = reduce.give[count] if core_of else reduce.mine[count]
            target[p] = table[z, :, :, pl.ds(start, 128)]
    reduce.start(count)
    for core_of in (1, 0):
        start = pl.multiple_of((spot.c if core_of == 0 else 1 - spot.c) * half, 128)
        for i in range(count):
            right = factors[2 * i + 1][:, pl.ds(start, half)]
            reduce.put(i, core_of, dense_grad(factors[2 * i][...], right))
            if core_of:
                reduce.start(i)
    reduce.advance(0)
    for copy in copies:
        copy.wait()

    def product(i, factor):
        return dense_back(factor[...], weight[i].reshape(width, width))

    total = grad_one[...] + product(0, factors[-5])
    reduce.advance(1)
    total = total + product(1, factors[-3]) + product(2, factors[-1])
    input_ref[...] = total.astype(jnp.bfloat16)
    reduce.advance(2)
    memory_ref[...] = (product(3, key_two) + product(4, value_two)).astype(jnp.bfloat16)
    reduce.advance(3)
    reduce.advance(4)
    reduce.advance(5)
    reduce.finish()


def hand_on(*refs):
    count = len(refs) // 2
    for source, target in zip(refs[:count], refs[count:]):
        target[...] = source[...]


class Staged:
    staged = True

    def __init__(self):
        self.c = lax.axis_index("seq")
        self.parts = []

    def swap(self, array):
        pairs = [(f * 2 + c, f * 2 + 1 - c) for f in range(16) for c in range(2)]
        return lax.ppermute(array, ("fsdp", "seq"), pairs)

    def front(self, w, all_, sums, hidden, memory, target_ids, memory_ids, out_grad):
        vectors = split_vectors(w)
        narrow = [v for v in vectors if v.shape[0] == 48]
        (wide,) = [v for v in vectors if v.shape[0] != 48]
        table = jnp.concatenate([jnp.stack(narrow), wide.reshape(-1, 48)]).astype(jnp.float32)
        table = jnp.pad(table, ((0, 24 - table.shape[0]), (0, 256 - 48)))
        groups = (
            (w.self_query, w.self_key, w.self_value, table),
            (w.cross_key, w.cross_value, w.self_output, w.cross_query, w.cross_output),
            (w.inner_weight,),
            (w.outer_weight,),
        )
        shards = [array for group in groups for array in group]
        count, (length, width) = len(shards), hidden.shape
        pairs = width // PAIR
        low, full = jnp.bfloat16, jnp.float32
        some = [
            ((length, width), low), ((2 * pairs, length, PAIR), low), ((length, width), low),
            ((length, width), full), ((length, 128), full),
        ]
        wide_state = ((length, w.inner_weight.shape[1]), low)
        kept = some + some[:3] + [wide_state] * 2 + [((2 * length, width), low)] * 4
        kept += [((2 * length, PAIR), low)] * 2 + [some[0], some[0], some[3], some[0]]
        anywhere, near = pl.BlockSpec(memory_space=pl.ANY), pl.BlockSpec(memory_space=pltpu.VMEM)
        results = pl.pallas_call(
            functools.partial(gather_kernel, groups),
            out_shape=[jax.ShapeDtypeStruct((4, 4) + s.shape, s.dtype) for s in shards]
            + [jax.ShapeDtypeStruct((24, width), full), jax.ShapeDtypeStruct((16, width), full)]
            + [jax.ShapeDtypeStruct(*k) for k in kept],
            in_specs=[anywhere] * count + [near] * 4,
            out_specs=[anywhere] * count + [near] * 2 + [anywhere] * len(kept),
            scratch_shapes=[pltpu.VMEM(*k) for k in kept]
            + [
                pltpu.VMEM(*some[3]),
                pltpu.VMEM(*some[4]),
                pltpu.VMEM(wide_state[0], full),
                pltpu.VMEM((4, 4, *w.outer_weight.shape), low),
                pltpu.VMEM((length, width), low),
                pltpu.VMEM((8, 4, 4, width // 16, width), low),
                pltpu.VMEM((4, 4, 24, 256), full),
                pltpu.SemaphoreType.DMA((count, Gather.sems)),
                pltpu.SemaphoreType.DMA((count, Gather.sems)),
                pltpu.SemaphoreType.DMA((count,)),
                pltpu.SemaphoreType.DMA((9,)),
                pltpu.SemaphoreType.DMA((6,)),
                pltpu.SemaphoreType.DMA((6,)),
                pltpu.SemaphoreType.DMA((20,)),
            ],
            compiler_params=pltpu.CompilerParams(
                collective_id=0, has_side_effects=True, vmem_limit_bytes=60 * 2**20
            ),
        )(
            *shards, hidden, memory, marks_of(target_ids[0], memory_ids[0]), out_grad,
        )
        wholes, (lines, summed), results = (
            results[:count], results[count : count + 2], results[count + 2 :],
        )
        flats = [array.reshape(-1, array.shape[3]) for array in wholes]
        (
            all_.self_query, all_.self_key, all_.self_value, _, all_.cross_key, all_.cross_value,
            all_.self_output, all_.cross_query, all_.cross_output, all_.inner_weight,
            all_.outer_weight,
        ) = flats
        (
            mixed_one, qx_one, first, normed_one, inverse_one, mixed_two, qx_two, second, active,
            grad_inner, k_one, v_one, k_two, v_two, km_one, km_two, layer_out, grad_outer,
            grad_two, branch_two,
        ) = results
        (
            sums.third_gain, sums.third_shift, sums.outer_bias, sums.second_gain,
            sums.second_shift, sums.cross_output_bias,
        ) = summed[:6]
        sums.inner_bias = summed[8:12].reshape(-1)
        self.kept = (
            (qx_two, k_two, v_two, mixed_two, km_two), (qx_one, k_one, v_one, mixed_one, km_one),
            normed_one, inverse_one, lines, branch_two,
        )
        self.first, self.all, self.inputs = first, all_, (hidden, memory)
        return layer_out, active, grad_outer, second, grad_inner, grad_two

    def back(self, g, sums, active, grad_outer, second, grad_inner, grad_two):
        two, one, normed_one, inverse_one, lines, branch_two = self.kept
        all_ = self.all
        length, width = branch_two.shape
        anywhere, near = pl.BlockSpec(memory_space=pl.ANY), pl.BlockSpec(memory_space=pltpu.VMEM)
        low, full = jnp.bfloat16, jnp.float32
        shapes = [(active.shape[1] // 16, width), (width // 16, active.shape[1])]
        shapes += [(width // 16, width)] * 4
        hidden, memory = self.inputs

        def blocks(array):
            return array.reshape(4, 4, -1, width)

        state = ((length, width), low)
        row = ((2 * length, width), low)
        outs = [((length, width), full)] + [state] * 7 + [((8, width), full)]
        (
            g.outer_weight, g.inner_weight, g.cross_output, g.cross_query, g.cross_key,
            g.cross_value, grad_one, branch_one, query_two, key_two, value_two, query_one, key_one,
            value_one, lines_sum,
        ) = pl.pallas_call(
            back_kernel,
            out_shape=[jax.ShapeDtypeStruct(s, full) for s in shapes]
            + [jax.ShapeDtypeStruct(*o) for o in outs],
            in_specs=[anywhere] * 4 + [near] * 5 + [anywhere] * 15,
            out_specs=[near] * 9 + [anywhere] * 2 + [near] + [anywhere] * 2 + [near],
            scratch_shapes=Reduce.scratch(shapes, [low] * 6, 4)
            + [
                pltpu.VMEM((2, length, 4 * width), low),
                pltpu.VMEM((2, length, width), low),
                pltpu.VMEM((width // HEAD_DIM, length, PAIR), low),
                pltpu.VMEM(*row), pltpu.VMEM(*row), pltpu.VMEM(*state),
                pltpu.VMEM((2 * length, PAIR), low),
                pltpu.VMEM(*state), pltpu.VMEM(*row), pltpu.VMEM(*row),
                pltpu.VMEM(*state), pltpu.VMEM(*state),
                pltpu.VMEM((3, 4, 4, width // 16, width), low),
                pltpu.VMEM((2 * length, PAIR), full), pltpu.VMEM((2 * length, PAIR), full),
                pltpu.VMEM((PAIR, length), full),
                pltpu.SemaphoreType.DMA((14,)),
                pltpu.SemaphoreType.DMA((4,)),
                pltpu.SemaphoreType.DMA((4,)),
            ],
            compiler_params=pltpu.CompilerParams(
                collective_id=2, has_side_effects=True, vmem_limit_bytes=61 * 2**20
            ),
        )(
            active, grad_outer, second, grad_inner, branch_two, grad_two, normed_one, inverse_one,
            lines, self.first, memory, *two, *one,
            blocks(all_.cross_output), blocks(all_.cross_query), blocks(all_.self_output),
        )
        (
            sums.first_gain, sums.first_shift, sums.self_output_bias, sums.cross_query_bias,
            sums.cross_value_bias, sums.self_query_bias, sums.self_value_bias, _,
        ) = lines_sum
        products = [
            (one[3], branch_one), (hidden, query_one), (hidden, key_one), (hidden, value_one),
        ]
        weights = (
            all_.self_query, all_.self_key, all_.self_value, all_.cross_key, all_.cross_value
        )
        vectors = vectors_of(sums)
        narrow = [v for v in vectors if v.shape[0] == 768]
        (wide,) = [v for v in vectors if v.shape[0] != 768]
        rows = len(narrow)
        table = jnp.concatenate(
            [
                jnp.stack(narrow).reshape(rows, 16, 48).transpose(1, 0, 2),
                wide.reshape(16, -1, 48),
            ],
            axis=1,
        )
        table = jnp.pad(table, ((0, 0), (0, 24 - table.shape[1]), (0, 256 - 48)))
        count = len(products)
        shapes = [(width // 16, width)] * count + [(24, 256)]
        *results, table, input_grad, memory_grad = pl.pallas_call(
            functools.partial(reduce_kernel, count),
            out_shape=[jax.ShapeDtypeStruct(s, full) for s in shapes]
            + [jax.ShapeDtypeStruct(*state)] * 2,
            in_specs=[near] * (2 * count + 4) + [anywhere] * 5,
            out_specs=[near] * (count + 3),
            scratch_shapes=Reduce.scratch(shapes, [low] * count + [full])
            + [
                pltpu.SemaphoreType.DMA((5,)),
                pltpu.VMEM((5, 4, 4, width // 16, width), low),
            ],
            compiler_params=pltpu.CompilerParams(
                collective_id=1, has_side_effects=True, vmem_limit_bytes=60 * 2**20
            ),
        )(
            *[factor for pair in products for factor in pair], table.reshape(4, 4, 24, 256),
            grad_one, key_two, value_two, *[blocks(array) for array in weights],
        )
        g.self_output, g.self_query, g.self_key, g.self_value = results
        reduced, row = [], 0
        for v in vectors:
            if v.shape[0] == 768:
                reduced.append(table[row, :48])
                row += 1
            else:
                reduced.append(table[rows : rows + v.shape[0] // 768, :48].reshape(-1))
        done = (
            g.self_query, g.self_key, g.self_value, g.self_output, g.cross_query, g.cross_key,
            g.cross_value, g.cross_output, g.inner_weight, g.outer_weight, input_grad, memory_grad,
        )
        (
            g.self_query, g.self_key, g.self_value, g.self_output, g.cross_query, g.cross_key,
            g.cross_value, g.cross_output, g.inner_weight, g.outer_weight, input_grad, memory_grad,
        ) = pl.pallas_call(
            hand_on,
            out_shape=[jax.ShapeDtypeStruct(array.shape, array.dtype) for array in done],
            in_specs=[near] * len(done),
            out_specs=[near] * len(done),
        )(*done)
        return reduced, input_grad, memory_grad


class Plain:
    staged = False

    def front(self, w, all_, sums, hidden, memory, target_ids, memory_ids, out_grad):
        def whole(array):
            return lax.all_gather(array, "fsdp", axis=0, tiled=True)

        all_.__dict__.update(Weights(*map(whole, w))._asdict())
        vectors = [array.astype(jnp.float32) for array in split_vectors(Weights(**vars(all_)))]
        (
            self_query_bias, self_value_bias, self_output_bias, first_gain, first_shift,
            cross_query_bias, cross_value_bias, cross_output_bias, second_gain, second_shift,
            inner_bias, outer_bias, third_gain, third_shift,
        ) = vectors
        rows, length = target_ids.shape
        width = hidden.shape[1]
        scale = HEAD_DIM ** (-0.5)

        def low(array):
            return array.astype(jnp.bfloat16).reshape(rows, length, width)

        row_ids, source_ids = self.gather_row(target_ids), self.gather_row(memory_ids)
        query_places = lax.axis_index("seq") * length + jnp.arange(length)
        key_places = jnp.arange(row_ids.shape[1])
        allowed_self = (target_ids[:, :, None] == row_ids[:, None, :]) & (
            key_places[None, None, :] <= query_places[None, :, None]
        )
        allowed_cross = target_ids[:, :, None] == source_ids[:, None, :]

        def attention(query, keys, values, allowed):
            mixed, logsum = plain_attend(query, keys, values, allowed)

            def back(grad):
                query_sum, key_sum, value_sum = plain_attend_back(
                    query, keys, values, allowed, logsum, grad.reshape(rows, length, width)
                )
                return query_sum.astype(jnp.bfloat16) * scale, key_sum, value_sum

            return mixed.astype(jnp.bfloat16).reshape(rows * length, width), back

        key_one = self.gather_row(low(dense(hidden, all_.self_key)))
        value_one = self.gather_row(low(dense(hidden, all_.self_value) + self_value_bias))
        query_one = low((dense(hidden, all_.self_query) + self_query_bias) * scale)
        mixed_one, back_one = attention(query_one, key_one, value_one, allowed_self)
        key_two = self.gather_row(low(dense(memory, all_.cross_key)))
        value_two = self.gather_row(low(dense(memory, all_.cross_value) + cross_value_bias))
        resid_one = (
            hidden.astype(jnp.float32) + dense(mixed_one, all_.self_output) + self_output_bias
        )
        first, normed_one, inverse_one = layer_norm(resid_one, first_gain, first_shift)
        first = first.astype(jnp.bfloat16)
        query_two = low((dense(first, all_.cross_query) + cross_query_bias) * scale)
        mixed_two, back_two = attention(query_two, key_two, value_two, allowed_cross)
        resid_two = (
            first.astype(jnp.float32) + dense(mixed_two, all_.cross_output) + cross_output_bias
        )
        second, normed_two, inverse_two = layer_norm(resid_two, second_gain, second_shift)
        self.kept = (
            hidden, memory, all_, mixed_one, first, normed_one, inverse_one, first_gain, back_one,
            mixed_two, back_two,
        )
        second = second.astype(jnp.bfloat16)
        inner = dense(second, all_.inner_weight) + inner_bias
        cumulative = 0.5 * (1.0 + lax.erf(inner * math.sqrt(0.5)))
        active = (inner * cumulative).astype(jnp.bfloat16)
        density = jnp.exp(-0.5 * inner * inner) * (1.0 / math.sqrt(2.0 * math.pi))
        slope = cumulative + inner * density
        resid_three = second.astype(jnp.float32) + dense(active, all_.outer_weight) + outer_bias
        final, normed_three, inverse_three = layer_norm(resid_three, third_gain, third_shift)

        keep = (target_ids > 0).astype(jnp.float32).reshape(-1, 1)
        upstream = out_grad.astype(jnp.float32) * keep
        grad_three, sums.third_gain, sums.third_shift = norm_back(
            upstream, normed_three, inverse_three, third_gain
        )
        grad_outer = grad_three.astype(jnp.bfloat16)
        sums.outer_bias = column_sum(grad_outer)
        grad_active = dense_back(grad_outer, all_.outer_weight)
        grad_inner = (grad_active * slope).astype(jnp.bfloat16)
        sums.inner_bias = column_sum(grad_inner)
        grad_second = grad_three + dense_back(grad_inner, all_.inner_weight)
        grad_two, sums.second_gain, sums.second_shift = norm_back(
            grad_second, normed_two, inverse_two, second_gain
        )
        return final, active, grad_outer, second, grad_inner, grad_two

    def _reduce(self, total):
        part = lax.psum_scatter(
            total.astype(jnp.bfloat16), "fsdp", scatter_dimension=0, tiled=True
        )
        return lax.psum(part, "seq").astype(jnp.float32)

    def back(self, g, sums, active, grad_outer, second, grad_inner, grad_two):
        (
            hidden, memory, all_, mixed_one, first, normed_one, inverse_one, first_gain, back_one,
            mixed_two, back_two,
        ) = self.kept
        shape = grad_two.shape

        def flat(array):
            return array.astype(jnp.bfloat16).reshape(shape)

        branch_two = grad_two.astype(jnp.bfloat16)
        sums.cross_output_bias = column_sum(branch_two)
        query_grad_two, key_sum, value_sum = back_two(
            flat(dense_back(branch_two, all_.cross_output))
        )
        key_grad_two = flat(self.scatter_row(key_sum))
        value_grad_two = flat(self.scatter_row(value_sum))
        query_grad_two = flat(query_grad_two)
        sums.cross_query_bias = column_sum(query_grad_two)
        sums.cross_value_bias = column_sum(value_grad_two)
        grad_first = grad_two + dense_back(query_grad_two, all_.cross_query)
        grad_one, sums.first_gain, sums.first_shift = norm_back(
            grad_first, normed_one, inverse_one, first_gain
        )
        branch_one = grad_one.astype(jnp.bfloat16)
        sums.self_output_bias = column_sum(branch_one)
        query_grad_one, key_sum, value_sum = back_one(
            flat(dense_back(branch_one, all_.self_output))
        )
        key_grad_one = flat(self.scatter_row(key_sum))
        value_grad_one = flat(self.scatter_row(value_sum))
        query_grad_one = flat(query_grad_one)
        sums.self_query_bias = column_sum(query_grad_one)
        sums.self_value_bias = column_sum(value_grad_one)
        g.outer_weight = self._reduce(dense_grad(active, grad_outer))
        g.inner_weight = self._reduce(dense_grad(second, grad_inner))
        g.cross_output = self._reduce(dense_grad(mixed_two, branch_two))
        g.cross_query = self._reduce(dense_grad(first, query_grad_two))
        g.cross_key = self._reduce(dense_grad(memory, key_grad_two))
        g.cross_value = self._reduce(dense_grad(memory, value_grad_two))
        g.self_output = self._reduce(dense_grad(mixed_one, branch_one))
        g.self_query = self._reduce(dense_grad(hidden, query_grad_one))
        g.self_key = self._reduce(dense_grad(hidden, key_grad_one))
        g.self_value = self._reduce(dense_grad(hidden, value_grad_one))
        input_grad = (
            grad_one
            + dense_back(query_grad_one, all_.self_query)
            + dense_back(key_grad_one, all_.self_key)
            + dense_back(value_grad_one, all_.self_value)
        )
        memory_grad = dense_back(key_grad_two, all_.cross_key) + dense_back(
            value_grad_two, all_.cross_value
        )
        return [self._reduce(v) for v in vectors_of(sums)], input_grad, memory_grad

    def gather_row(self, array):
        return lax.all_gather(array, "seq", axis=1, tiled=True)

    def scatter_row(self, array):
        return lax.psum_scatter(
            array.astype(jnp.bfloat16), "seq", scatter_dimension=1, tiled=True
        ).astype(jnp.float32)


def marks_of(target_ids, memory_ids):
    length = target_ids.shape[0]
    ids = jnp.concatenate([target_ids, target_ids, memory_ids])
    lanes = lax.broadcasted_iota(jnp.int32, (3 * length, PAIR), 1) % HEAD_DIM
    queries = lax.broadcasted_iota(jnp.int32, (3 * length, PAIR), 0) < length
    same = ids[:, None] == lanes
    ones = (lanes >= SEGMENTS) & (lanes < SEGMENTS + 3)
    for_queries = jnp.where((lanes < SEGMENTS) & ~same, masked_score, 0.0)
    for_keys = jnp.where(ones | same, 1.0, 0.0)
    return jnp.where(queries, for_queries, for_keys).astype(jnp.bfloat16)


def against(left, right):
    return lax.dot_general(
        left, right, (((1,), (1,)), ((), ())), preferred_element_type=jnp.float32
    )


def three(value):
    high = value.astype(jnp.bfloat16).astype(jnp.float32)
    rest = value - high
    middle = rest.astype(jnp.bfloat16).astype(jnp.float32)
    return high, middle, rest - middle


def place_three(lanes, base, value, other):
    high, middle, small = three(value)
    first = base + SEGMENTS
    return jnp.where(
        lanes == first,
        high,
        jnp.where(lanes == first + 1, middle, jnp.where(lanes == first + 2, small, other)),
    )


def plan(length, causal, later):
    half = length // 2
    result = []
    for tile in range(2):
        if not causal:
            result.append([(0, 2 * length, False)])
            continue
        ranges = [(0, half, False)] if tile else []
        ranges.append((tile * half, half, True))
        if later:
            ranges.append((length + tile * half, length - tile * half, False))
        result.append(ranges)
    return result


def each_plan(core, length, causal, run):
    if not causal:
        run(plan(length, False, False))
        return
    for later in range(2):
        @pl.when(core == later)
        def _():
            run(plan(length, True, bool(later)))


def forward_pair(core, causal, q_ref, k_ref, v_ref, qm_ref, km_ref, mixed_ref, qx_ref):
    length = q_ref.shape[0]

    def run(tiles):
        for head in range(2):
            base = HEAD_DIM * (1 - head)

            def own(lanes):
                return (lanes < HEAD_DIM) if head == 0 else (lanes >= HEAD_DIM)

            for tile, ranges in enumerate(tiles):
                rows = slice(tile * TILE, tile * TILE + TILE)
                lanes = lax.broadcasted_iota(jnp.int32, (TILE, PAIR), 1)
                q = jnp.where(own(lanes), q_ref[rows, :], qm_ref[rows, :])
                scores = []
                for start, size, diagonal in ranges:
                    keys = slice(start, start + size)
                    key_lanes = lax.broadcasted_iota(jnp.int32, (size, PAIR), 1)
                    k = jnp.where(own(key_lanes), k_ref[keys, :], km_ref[keys, :])
                    s = against(q, k)
                    if diagonal:
                        i = lax.broadcasted_iota(jnp.int32, s.shape, 0)
                        j = lax.broadcasted_iota(jnp.int32, s.shape, 1)
                        s = jnp.where(j <= i, s, masked_score)
                    scores.append(s)
                highest = functools.reduce(
                    jnp.maximum, [jnp.max(s, axis=1, keepdims=True) for s in scores]
                )
                out = jnp.zeros((TILE, PAIR), jnp.float32)
                for s, (start, size, _) in zip(scores, ranges):
                    keys = slice(start, start + size)
                    key_lanes = lax.broadcasted_iota(jnp.int32, (size, PAIR), 1)
                    v = jnp.where(own(key_lanes), v_ref[keys, :], jnp.ones((), jnp.bfloat16))
                    e = jnp.exp(s - highest).astype(jnp.bfloat16)
                    out = out + jnp.dot(e, v, preferred_element_type=jnp.float32)
                total = pltpu.roll(out, HEAD_DIM, 1)
                mixed = (out / total).astype(jnp.bfloat16)
                if head:
                    mixed = jnp.where(own(lanes), mixed, mixed_ref[rows, :])
                mixed_ref[rows, :] = mixed
                logsum = highest + jnp.log(out)
                qx = place_three(lanes, base, -logsum, q.astype(jnp.float32))
                qx_ref[head, rows, :] = qx.astype(jnp.bfloat16)

    each_plan(core, length, causal, run)


def backward_pair(
    core, causal, qx_ref, k_ref, v_ref, e_ref, o_ref, km_ref, dq_ref, dk_ref, dv_ref, dk_acc,
    dv_acc, dq_acc,
):
    length = e_ref.shape[0]
    scale = HEAD_DIM ** (-0.5)

    def run(tiles):
        dk_acc[...] = jnp.zeros_like(dk_acc)
        dv_acc[...] = jnp.zeros_like(dv_acc)
        for head in range(2):
            base = HEAD_DIM * (1 - head)

            def own(lanes):
                return (lanes < HEAD_DIM) if head == 0 else (lanes >= HEAD_DIM)

            for tile, ranges in enumerate(tiles):
                rows = slice(tile * TILE, tile * TILE + TILE)
                lanes = lax.broadcasted_iota(jnp.int32, (TILE, PAIR), 1)
                nothing = jnp.zeros((), jnp.bfloat16)
                qx = qx_ref[head, rows, :]
                q = jnp.where(own(lanes), qx, nothing)
                e = jnp.where(own(lanes), e_ref[rows, :], nothing)
                wide = e.astype(jnp.float32)
                delta = jnp.sum(wide * o_ref[rows, :].astype(jnp.float32), axis=1, keepdims=True)
                ex = place_three(lanes, base, -delta, wide).astype(jnp.bfloat16)
                dq = jnp.zeros((HEAD_DIM, TILE), jnp.float32)
                for start, size, diagonal in ranges:
                    keys = slice(start, start + size)
                    key_lanes = lax.broadcasted_iota(jnp.int32, (size, PAIR), 1)
                    k = jnp.where(own(key_lanes), k_ref[keys, :], km_ref[keys, :])
                    v = jnp.where(own(key_lanes), v_ref[keys, :], km_ref[keys, :])
                    p = jnp.exp(against(k, qx))
                    if diagonal:
                        j = lax.broadcasted_iota(jnp.int32, p.shape, 0)
                        i = lax.broadcasted_iota(jnp.int32, p.shape, 1)
                        p = jnp.where(j <= i, p, 0.0)
                    ds = (p * against(v, ex)).astype(jnp.bfloat16)
                    p = p.astype(jnp.bfloat16)
                    dv_acc[keys, :] += jnp.dot(p, e, preferred_element_type=jnp.float32)
                    dk_acc[keys, :] += jnp.dot(ds, q, preferred_element_type=jnp.float32)
                    kt = k_ref[keys, :].T[head * HEAD_DIM : (head + 1) * HEAD_DIM, :]
                    dq = dq + jnp.dot(kt, ds, preferred_element_type=jnp.float32)
                dq_acc[head * HEAD_DIM : (head + 1) * HEAD_DIM, rows] = dq
        dq_ref[...] = (dq_acc[...].T.astype(jnp.bfloat16) * jnp.bfloat16(scale)).astype(jnp.bfloat16)
        dk_ref[...] = dk_acc[...].astype(jnp.bfloat16)
        dv_ref[...] = dv_acc[...].astype(jnp.bfloat16)

    each_plan(core, length, causal, run)


def head_slice(array, start, span):
    piece = lax.dynamic_slice_in_dim(array, start, span, 2)
    return piece.reshape(array.shape[0], array.shape[1], 2, span // 2)


def plain_attend(query, keys, values, allowed):
    rows, length, width = query.shape
    span = 2 * HEAD_DIM
    pairs = width // span

    def one_pair(index, carry):
        mixed, logsum = carry
        start = index * span
        query_part = head_slice(query, start, span)
        key_part = head_slice(keys, start, span)
        value_part = head_slice(values, start, span)
        scores = jnp.einsum(
            "rqhe,rkhe->rhqk", query_part, key_part, preferred_element_type=jnp.float32
        )
        scores = jnp.where(allowed[:, None], scores, masked_score)
        highest = jnp.max(scores, axis=-1, keepdims=True)
        exponent = jnp.exp(scores - highest)
        total = jnp.sum(exponent, axis=-1, keepdims=True)
        probs = (exponent / total).astype(jnp.bfloat16)
        part = jnp.einsum("rhqk,rkhe->rqhe", probs, value_part, preferred_element_type=jnp.float32)
        mixed = lax.dynamic_update_slice_in_dim(mixed, part.reshape(rows, length, span), start, 2)
        logsum = lax.dynamic_update_slice_in_dim(
            logsum, (highest + jnp.log(total))[None, :, :, :, 0], index, 0
        )
        return (mixed, logsum)

    mixed = jnp.zeros((rows, length, width), jnp.float32)
    logsum = jnp.zeros((pairs, rows, 2, length), jnp.float32)
    return lax.fori_loop(0, pairs, one_pair, (mixed, logsum))


def plain_attend_back(query, keys, values, allowed, logsum, grad_mixed):
    rows, length, width = query.shape
    extent = keys.shape[1]
    span = 2 * HEAD_DIM
    pairs = width // span

    def one_pair(index, carry):
        start = index * span
        query_part = head_slice(query, start, span)
        key_part = head_slice(keys, start, span)
        value_part = head_slice(values, start, span)
        grad_part = head_slice(grad_mixed, start, span)
        scores = jnp.einsum(
            "rqhe,rkhe->rhqk", query_part, key_part, preferred_element_type=jnp.float32
        )
        scores = jnp.where(allowed[:, None], scores, masked_score)
        pair_logsum = lax.dynamic_index_in_dim(logsum, index, 0, keepdims=False)
        probs = jnp.exp(scores - pair_logsum[..., None])
        prob_grad = jnp.einsum(
            "rqhe,rkhe->rhqk", grad_part, value_part, preferred_element_type=jnp.float32
        )
        row_total = jnp.sum(probs * prob_grad, axis=-1, keepdims=True)
        score_grad = (probs * (prob_grad - row_total)).astype(jnp.bfloat16)
        query_grad = jnp.einsum(
            "rhqk,rkhe->rqhe", score_grad, key_part, preferred_element_type=jnp.float32
        )
        grad_query = lax.dynamic_update_slice_in_dim(
            carry[0], query_grad.reshape(rows, length, span), start, 2
        )
        probs_low = probs.astype(jnp.bfloat16)
        value_grad = jnp.einsum(
            "rhqk,rqhe->rkhe", probs_low, grad_part, preferred_element_type=jnp.float32
        )
        key_grad = jnp.einsum(
            "rhqk,rqhe->rkhe", score_grad, query_part, preferred_element_type=jnp.float32
        )
        grad_keys = lax.dynamic_update_slice_in_dim(
            carry[1], key_grad.reshape(rows, extent, span), start, 2
        )
        grad_values = lax.dynamic_update_slice_in_dim(
            carry[2], value_grad.reshape(rows, extent, span), start, 2
        )
        return (grad_query, grad_keys, grad_values)

    start_query = jnp.zeros((rows, length, width), jnp.float32)
    start_keys = jnp.zeros((rows, extent, width), jnp.float32)
    return lax.fori_loop(0, pairs, one_pair, (start_query, start_keys, start_keys))


def body(staged, hidden_in, memory, target_ids, memory_ids, out_grad, *weights):
    w = Weights(*weights)
    rows, length, width = hidden_in.shape
    staged = staged and (rows, length, width) == (1, 2 * TILE, 768)
    net = Staged() if staged else Plain()
    all_ = SimpleNamespace()
    tokens = rows * length
    flat_in = hidden_in.reshape(tokens, width)
    flat_memory = memory.reshape(tokens, width)

    def low(array):
        return array.astype(jnp.bfloat16).reshape(rows, length, width)

    sums = SimpleNamespace()
    layer_out, *states = net.front(
        w, all_, sums, flat_in, flat_memory, target_ids, memory_ids,
        out_grad.reshape(tokens, width),
    )
    g = SimpleNamespace()
    (
        g.self_query_bias, g.self_value_bias, g.self_output_bias, g.first_gain, g.first_shift,
        g.cross_query_bias, g.cross_value_bias, g.cross_output_bias, g.second_gain,
        g.second_shift, g.inner_bias, g.outer_bias, g.third_gain, g.third_shift,
    ), input_grad, memory_grad = net.back(g, sums, *states)
    return (low(layer_out), low(input_grad), low(memory_grad), *Weights(**vars(g)))


def solution(mesh):
    staged = mesh.shape["fsdp"] == 16 and mesh.shape["seq"] == 2
    row, ids = P("fsdp", "seq", None), P("fsdp", "seq")
    matrix, vector = P("fsdp", None), P("fsdp")
    weights = Weights(
        matrix, vector, matrix, matrix, vector, matrix, vector, vector, vector, matrix, vector,
        matrix, matrix, vector, matrix, vector, vector, vector, matrix, vector, matrix, vector,
        vector, vector,
    )
    return jax.shard_map(
        functools.partial(body, staged),
        mesh=mesh,
        in_specs=(row, row, ids, ids, row, *weights),
        out_specs=(row, row, row, *weights),
        check_vma=False,
    )
```
